32 devices in a mesh: inst: 4 (over z), tp: 8 (over y, x, core).
Axes of the slice: x: 2, y: 2, z: 4, core: 2. Of those that a mesh axis runs over, the one named last changes fastest.
Arguments:
- x_steps: bfloat16 [2, 256, 8192], P(None, 'inst', 'tp'), may hold values from -6 to 6
- norm_gain: float32 [8192], replicated, may hold values from 0.1 to 1.9
- w_query: bfloat16 [8192, 8192], P(None, 'tp'), may hold values from -0.0625 to 0.0625
- w_keyval: bfloat16 [8192, 2048], P(None, 'tp'), may hold values from -0.0625 to 0.0625
- w_out: bfloat16 [8192, 8192], P('tp'), may hold values from -0.375 to 0.375
- key_cache: bfloat16 [256, 8, 128, 256], P('inst', 'tp')
- lengths: int32 [256], replicated, may hold values from 1 to 128, as said below
- moved_slots: int32 [4, 8], replicated, may hold values from 0 to 63, as said below
- partner_mask: int32 [8], replicated, may hold values from 1 to 3
Outputs:
- attention_out: bfloat16 [2, 256, 8192], P(None, 'inst', 'tp')
- arrived: bfloat16 [32, 8, 128, 256], P('inst', 'tp')
The draws below stay inside these ranges and needn't reach their ends.
Inputs may be any that keep to these rules, and one draw needn't show every extreme that they name: `lengths`: some request has 128 cached tokens and some has 1. `moved_slots`: the 8 slots of one instance are distinct.
All inputs are finite; a program needn't handle non-finite values.
Results may differ from the reference program's by a relative error of at most 0.012.
The reference program's roundings to bfloat16 on the way count: a program that leaves them out, or rounds other values in their place, can miss the bound.
Values may be sent and summed in bfloat16 or wider, within the bound.
A program may use at most 128 MiB of HBM per device.

```python
import math
from functools import reduce
import jax
import jax.numpy as jnp
from jax import lax

D = 8192
HEADS = 64
KVH = 8
HD = 128
REQ = 64
MOVE = 8
BLK = 128
GROUP = 1
INSTANCES = 4
N_TP = 8


def draw_key_cache(key, part):
    key = jax.random.fold_in(key, 11)
    key_one = jax.random.fold_in(key, 0)
    shape = (INSTANCES * REQ, N_TP, BLK, 2 * HD)
    values = jax.random.normal(key_one, shape, jnp.float32)
    return values.astype(jnp.bfloat16)


def draw_lengths(key, part):
    key = jax.random.fold_in(key, 5)
    key_one, key_two, key_three = jax.random.split(key, 3)
    total_rows = INSTANCES * REQ
    values = jax.random.randint(key_one, (total_rows,), 1, GROUP * BLK + 1)
    top_index = jax.random.randint(key_two, (), 0, total_rows)
    low_index = (top_index + 1 + jax.random.randint(key_three, (), 0, total_rows - 1)) % total_rows
    values = values.at[low_index].set(1).at[top_index].set(GROUP * BLK)
    return values.astype(jnp.int32)


def draw_moved_slots(key, part):
    key = jax.random.fold_in(key, 7)
    key_rows, key_extra = jax.random.split(key)
    row_keys = jax.random.split(key_rows, INSTANCES)
    slot_rows = jax.vmap(lambda row_key: jax.random.permutation(row_key, REQ)[:MOVE])(row_keys)
    inner = 1 + jax.random.permutation(key_extra, REQ - 2)[:MOVE - 2]
    first_row = jnp.concatenate([jnp.array([REQ - 1, 0], jnp.int32), inner.astype(jnp.int32)])
    slot_rows = slot_rows.astype(jnp.int32).at[0].set(first_row)
    return slot_rows


def place_ends(result, key, smallest, top_value):
    spot = [jax.random.randint(jax.random.fold_in(key, axis), (), 0, length) for axis, length in enumerate(result.shape)]
    widest = result.shape.index(max(result.shape))
    neighbour = spot[:widest] + [(spot[widest] + 1) % result.shape[widest]] + spot[widest + 1:]
    return result.at[tuple(spot)].set(smallest).at[tuple(neighbour)].set(top_value)


def block_levels(own_key, shape, cuts, smallest, largest):
    level, own = 1.0, jax.random.fold_in(own_key, 6)
    for dim, blocks in cuts:
        draws = jnp.exp(jax.random.uniform(jax.random.fold_in(own, dim), (blocks,), jnp.float32, smallest / len(cuts), largest / len(cuts)))
        level = level * jnp.repeat(draws, shape[dim] // blocks).reshape([-1 if axis == dim else 1 for axis in range(len(shape))])
    return level


def centred(stream_key, extent, scale, bound, shards=(), kind=jnp.bfloat16):
    drawn = scale * jax.random.normal(stream_key, extent, jnp.float32)
    if shards:
        drawn = drawn * block_levels(stream_key, extent, shards, -0.22, 0.18)
    return jnp.clip(drawn, -bound, bound).astype(kind)


def setup_inputs(seed: int = 0) -> dict:
    streams_of = jax.random.split(jax.random.key(seed), 10)
    x_steps = centred(streams_of[0], (2, INSTANCES * REQ, D), 1.0, 6.0, ((1, 4), (2, 8)))
    norm_gain = jnp.clip(1.0 + 0.18 * jax.random.normal(streams_of[1], (D,), jnp.float32), 0.1, 1.9)
    w_query = centred(streams_of[2], (D, HEADS * HD), D ** -0.5, 0.0625, ((1, 8),))
    w_keyval = centred(streams_of[3], (D, 2 * KVH * HD), D ** -0.5, 0.0625, ((1, 8),))
    w_out = centred(streams_of[4], (HEADS * HD, D), (D // 32) ** -0.5, 0.375, ((0, 8),))
    key_cache = draw_key_cache(jax.random.fold_in(streams_of[9], 71), 0)
    lengths = draw_lengths(jax.random.fold_in(streams_of[9], 71), 0)
    moved_slots = draw_moved_slots(jax.random.fold_in(streams_of[9], 71), 0)
    partner_mask = place_ends(jax.random.randint(streams_of[8], (MOVE,), 1, INSTANCES), jax.random.fold_in(streams_of[8], 1), 1, INSTANCES - 1).astype(jnp.int32)
    return dict(x_steps=x_steps, norm_gain=norm_gain, w_query=w_query, w_keyval=w_keyval, w_out=w_out, key_cache=key_cache, lengths=lengths, moved_slots=moved_slots, partner_mask=partner_mask)


eps_norm = 1e-05
rope_base = 500000.0
floor_score = -1e+30

def rotary(vectors, positions):
    half_dim = vectors.shape[-1] // 2
    frequency = rope_base ** (-(jnp.arange(half_dim, dtype=jnp.float32) * 2.0) / vectors.shape[-1])
    angles = positions.astype(jnp.float32)[..., None] * frequency
    cosine = jnp.cos(angles)[..., None, :]
    sine_part = jnp.sin(angles)[..., None, :]
    first_half = vectors[..., :half_dim]
    second_half = vectors[..., half_dim:]
    return jnp.concatenate([first_half * cosine - second_half * sine_part, second_half * cosine + first_half * sine_part], -1)

def block_terms(grouped, block, start, length_rows):
    queries = grouped.astype(jnp.float32)
    keys = block[..., :HD].astype(jnp.float32)
    values = block[..., HD:].astype(jnp.float32)
    scores = jnp.einsum('irkgd,irktd->irkgt', queries, keys) / math.sqrt(HD)
    places = start + jnp.arange(BLK, dtype=jnp.int32)
    visible = (places[None, None, :] < length_rows[:, :, None])[:, :, None, None, :]
    scores = jnp.where(visible, scores, floor_score)
    block_max = lax.optimization_barrier(jnp.max(scores, -1))
    weights = jnp.where(visible, jnp.exp(scores - block_max[..., None]), 0.0).astype(jnp.bfloat16)
    block_sum = lax.optimization_barrier(jnp.sum(weights.astype(jnp.float32), -1))
    block_mix = jnp.einsum('irkgt,irktd->irkgd', weights.astype(jnp.float32), values)
    return (block_max, block_sum, block_mix)

def fresh_terms(grouped, fresh_kv):
    queries = grouped.astype(jnp.float32)
    score = jnp.einsum('irkgd,irkd->irkg', queries, fresh_kv[..., :HD].astype(jnp.float32)) / math.sqrt(HD)
    block_mix = jnp.broadcast_to(fresh_kv[:, :, :, None, HD:].astype(jnp.float32), queries.shape)
    return (score, jnp.ones_like(score), block_mix)

def combine(pieces):
    overall_max = reduce(jnp.maximum, [piece[0] for piece in pieces])
    numerator = reduce(jnp.add, [jnp.exp(piece[0] - overall_max)[..., None] * piece[2] for piece in pieces])
    denominator = reduce(jnp.add, [jnp.exp(piece[0] - overall_max) * piece[1] for piece in pieces])
    return numerator / denominator[..., None]

def reference(x_steps, norm_gain, w_query, w_keyval, w_out, key_cache, lengths, moved_slots, partner_mask):
    inst_count = INSTANCES
    x_all = x_steps.reshape(2, inst_count, REQ, D)
    cache_all = key_cache.reshape(inst_count, REQ, N_TP, BLK, 2 * HD)
    length_all = lengths.reshape(inst_count, REQ)

    def project(step_x, positions):
        widened = step_x.astype(jnp.float32)
        normed = (widened * jax.lax.rsqrt(lax.optimization_barrier(jnp.mean(widened * widened, -1, keepdims=True)) + eps_norm) * norm_gain).astype(jnp.bfloat16)
        flat = normed.reshape(inst_count * REQ, D)
        query_raw = jnp.dot(flat, w_query, preferred_element_type=jnp.float32).reshape(inst_count, REQ, HEADS, HD)
        keyval_raw = jnp.dot(flat, w_keyval, preferred_element_type=jnp.float32).reshape(inst_count, REQ, KVH, 2, HD)
        queries = rotary(query_raw, positions).astype(jnp.bfloat16)
        keys = rotary(keyval_raw[..., 0, :], positions)
        fresh_kv = jnp.concatenate([keys, keyval_raw[..., 1, :]], -1).astype(jnp.bfloat16)
        return (queries, fresh_kv)

    def attend(queries, cache_rows, length_rows, fresh_list):
        grouped = queries.reshape(inst_count, REQ, KVH, HEADS // KVH, HD)
        blocks = cache_rows.reshape(inst_count, REQ, KVH, GROUP, BLK, 2 * HD)
        pieces = []
        for block_index in range(GROUP):
            pieces.append(block_terms(grouped, blocks[:, :, :, block_index], block_index * BLK, length_rows))
        for fresh_item in fresh_list:
            pieces.append(fresh_terms(grouped, fresh_item))
        attended = combine(pieces).reshape(inst_count * REQ, HEADS * HD).astype(jnp.bfloat16)
        return jnp.dot(attended, w_out, preferred_element_type=jnp.float32).astype(jnp.bfloat16)
    first_queries, first_fresh = project(x_all[0], length_all)
    first_out = attend(first_queries, cache_all, length_all, [first_fresh])
    row_ids = jnp.arange(inst_count, dtype=jnp.int32)[:, None]
    move_ids = jnp.arange(MOVE, dtype=jnp.int32)[None, :]
    partner = jnp.bitwise_xor(row_ids, partner_mask[None, :])
    slots_partner = moved_slots[partner, move_ids]
    arrived_rows = cache_all[partner, slots_partner]
    cache_next = cache_all.at[row_ids, moved_slots].set(arrived_rows)
    fresh_next = first_fresh.at[row_ids, moved_slots].set(first_fresh[partner, slots_partner])
    length_next = length_all.at[row_ids, moved_slots].set(length_all[partner, slots_partner])
    second_queries, second_fresh = project(x_all[1], length_next + 1)
    second_out = attend(second_queries, cache_next, length_next, [fresh_next, second_fresh])
    return (jnp.stack([first_out, second_out]), arrived_rows.reshape(inst_count * MOVE, N_TP, BLK, 2 * HD))
```

```python
from functools import reduce
import math

import jax
import jax.numpy as jnp
from jax import lax
from jax.experimental import pallas as pl
from jax.experimental.pallas import tpu as pltpu
from jax.sharding import PartitionSpec as P

KVH = 8


eps_norm = 1e-05
rope_base = 500000.0
floor_score = -1e30


def from_partner(block, axis, bit):
    count = lax.axis_size(axis)
    route = []
    for low in range(count):
        high = low | 1 << bit
        if high != low and high < count:
            route += [(low, high), (high, low)]
    return lax.ppermute(block, axis, route)


def as_sent(value):

    def short(part):
        return part.astype(jnp.bfloat16) if part.dtype == jnp.float32 else part

    return jax.tree.map(short, value)


def rotary(vectors, positions):
    half_dim = vectors.shape[-1] // 2
    frequency = rope_base ** (-(jnp.arange(half_dim, dtype=jnp.float32) * 2.0) / vectors.shape[-1])
    angles = positions.astype(jnp.float32)[..., None] * frequency
    cosine = jnp.cos(angles)[..., None, :]
    sine_part = jnp.sin(angles)[..., None, :]
    first_half = vectors[..., :half_dim]
    second_half = vectors[..., half_dim:]
    return jnp.concatenate(
        [
            first_half * cosine - second_half * sine_part,
            second_half * cosine + first_half * sine_part,
        ],
        -1,
    )


def block_terms(queries, block, start, length_rows):
    head_dim = queries.shape[-1]
    block_len = block.shape[1]
    scores = jnp.einsum(
        "rhd,rtd->rht", queries, block[..., :head_dim], preferred_element_type=jnp.float32
    ) / math.sqrt(head_dim)
    places = start + jnp.arange(block_len, dtype=jnp.int32)
    visible = (places[None, :] < length_rows[:, None])[:, None, :]
    scores = jnp.where(visible, scores, floor_score)
    block_max = jnp.max(scores, -1)
    weights = jnp.where(visible, jnp.exp(scores - block_max[..., None]), 0.0).astype(jnp.bfloat16)
    block_sum = jnp.sum(weights.astype(jnp.float32), -1)
    block_mix = jnp.einsum(
        "rht,rtd->rhd", weights, block[..., head_dim:], preferred_element_type=jnp.float32
    )
    return (block_max, block_sum, block_mix)


def fresh_terms(queries, fresh_kv):
    head_dim = queries.shape[-1]
    score = jnp.einsum(
        "rhd,rd->rh", queries, fresh_kv[:, :head_dim], preferred_element_type=jnp.float32
    ) / math.sqrt(head_dim)
    block_mix = jnp.broadcast_to(fresh_kv[:, None, head_dim:].astype(jnp.float32), queries.shape)
    return (score, jnp.ones_like(score), block_mix)


def combine(pieces):
    overall_max = reduce(jnp.maximum, [piece[0] for piece in pieces])
    numerator = reduce(
        jnp.add, [jnp.exp(piece[0] - overall_max)[..., None] * piece[2] for piece in pieces]
    )
    denominator = reduce(jnp.add, [jnp.exp(piece[0] - overall_max) * piece[1] for piece in pieces])
    return numerator / denominator[..., None]


def shards(
    x_steps, norm_gain, w_query, w_keyval, w_out, key_cache, lengths, moved_slots, partner_mask
):
    row_count = x_steps.shape[1]
    head_dim = key_cache.shape[-1] // 2
    block_len = key_cache.shape[2]
    group_size = lax.axis_size("tp") // KVH
    group_bits = group_size.bit_length() - 1
    member = lax.axis_index("tp") % group_size
    instance = lax.axis_index("inst")
    own_heads = w_query.shape[1] // head_dim
    own_lengths = lax.dynamic_slice_in_dim(lengths, instance * row_count, row_count)

    def collect(value, swapper):
        stacked = jax.tree.map(lambda leaf: leaf[None], value)
        for bit_index in range(group_bits):
            received = swapper(stacked, bit_index)
            low_side = member >> bit_index & 1 == 0
            stacked = jax.tree.map(
                lambda mine_part, their_part: jnp.where(
                    low_side,
                    jnp.concatenate([mine_part, their_part], 0),
                    jnp.concatenate([their_part, mine_part], 0),
                ),
                stacked,
                received,
            )
        return stacked

    def decode(step_index, positions, cache_rows, length_rows, earlier):
        gathered = lax.all_gather(x_steps[step_index], "tp", axis=1, tiled=True)
        widened = gathered.astype(jnp.float32)
        normed = (
            widened
            * lax.rsqrt(jnp.mean(widened * widened, -1, keepdims=True) + eps_norm)
            * norm_gain
        ).astype(jnp.bfloat16)
        query_raw = jnp.dot(normed, w_query, preferred_element_type=jnp.float32)
        keyval_raw = jnp.dot(normed, w_keyval, preferred_element_type=jnp.float32)
        joined = collect(
            jnp.concatenate([query_raw, keyval_raw], 1),
            lambda value, bit_index: from_partner(value, "tp", bit_index),
        )
        query_width = own_heads * head_dim
        query_all = jnp.moveaxis(joined[:, :, :query_width], 0, 1).reshape(
            row_count, group_size * own_heads, head_dim
        )
        keyval = jnp.moveaxis(joined[:, :, query_width:], 0, 1).reshape(row_count, 2 * head_dim)
        queries = rotary(query_all, positions).astype(jnp.bfloat16)
        partial_value = block_terms(queries, cache_rows[:, 0], member * block_len, length_rows)
        shared = collect(
            partial_value, lambda value, bit_index: from_partner(value, "tp", bit_index)
        )
        own_queries = lax.dynamic_slice_in_dim(queries, member * own_heads, own_heads, 1)
        pieces = [
            tuple(
                (
                    lax.dynamic_slice_in_dim(
                        member_part[block_index], member * own_heads, own_heads, 1
                    )
                    for member_part in shared
                )
            )
            for block_index in range(group_size)
        ]
        fresh_kv = jnp.concatenate(
            [rotary(keyval[:, None, :head_dim], positions)[:, 0], keyval[:, head_dim:]], -1
        ).astype(jnp.bfloat16)
        for fresh_item in earlier + [fresh_kv]:
            pieces.append(fresh_terms(own_queries, fresh_item))
        attended = combine(pieces).reshape(row_count, own_heads * head_dim).astype(jnp.bfloat16)
        head_terms = jnp.dot(attended, w_out, preferred_element_type=jnp.float32)
        return (
            lax.psum_scatter(head_terms, "tp", scatter_dimension=1, tiled=True).astype(
                jnp.bfloat16
            ),
            fresh_kv,
        )

    first_out, first_fresh = decode(0, own_lengths, key_cache, own_lengths, [])
    move_count = moved_slots.shape[1]
    move_ids = jnp.arange(move_count, dtype=jnp.int32)
    partner = jnp.bitwise_xor(instance, partner_mask)
    slots_self = moved_slots[instance]
    slots_partner = moved_slots[partner, move_ids]
    payload = (key_cache[slots_self], first_fresh[slots_self])
    moving = payload
    for bit_index in range(lax.axis_size("inst").bit_length() - 1):
        received = jax.tree.map(
            lambda part, own: part.astype(own.dtype),
            from_partner(as_sent(moving), "inst", bit_index),
            moving,
        )
        use_swap = partner_mask >> bit_index & 1 == 1
        moving = jax.tree.map(
            lambda their_part, mine_part: jnp.where(
                use_swap.reshape((move_count,) + (1,) * (mine_part.ndim - 1)), their_part, mine_part
            ),
            received,
            moving,
        )
    arrived_rows, arrived_fresh = moving
    cache_next = key_cache.at[slots_self].set(arrived_rows)
    fresh_next = first_fresh.at[slots_self].set(arrived_fresh)
    length_next = own_lengths.at[slots_self].set(lengths[partner * row_count + slots_partner])
    second_out, unused = decode(1, length_next + 1, cache_next, length_next, [fresh_next])
    return (jnp.stack([first_out, second_out]), arrived_rows)


def fused_kernel(
    len_ref,
    slot_ref,
    mask_ref,
    x_ref,
    gain_ref,
    wq_hbm,
    wkv_hbm,
    wo_hbm,
    cache_hbm,
    out_ref,
    arrived_ref,
    wq,
    wkv,
    wo,
    cache,
    xg,
    acc,
    square,
    place,
    qs,
    fresh,
    mixed,
    attended,
    leave,
    mid_in,
    mid,
    last_in,
    fsend,
    frecv,
    sib_send,
    sib_recv,
    own,
    first_send,
    first_recv,
    second_send,
    second_recv,
    late_mixed,
    late_send,
    late_recv,
    load_sem,
    gather_send,
    gather_recv,
    move_send,
    move_recv,
    fresh_send,
    fresh_recv,
    sum_send,
    sum_recv,
    late_send_sem,
    late_recv_sem,
):
    tp = lax.axis_index("tp")
    inst = lax.axis_index("inst")
    rows = x_ref.shape[1]
    width = x_ref.shape[2]
    moves = slot_ref.shape[1]
    hd = cache.shape[-1] // 2
    heads = qs.shape[1] // 2
    scale = 1.0 / math.sqrt(hd)

    def remote(src, dst, send, recv, **where):
        return pltpu.make_async_remote_copy(
            src_ref=src,
            dst_ref=dst,
            send_sem=send,
            recv_sem=recv,
            device_id=where,
            device_id_type=pl.DeviceIdType.MESH,
        )

    cache_load = pltpu.make_async_copy(cache_hbm, cache, load_sem.at[24])
    cache_load.start()
    weight_loads = []
    for i in range(8):
        start = pl.multiple_of((tp ^ i) * width, width)
        pair = (
            pltpu.make_async_copy(wq_hbm.at[pl.ds(start, width), :], wq.at[i], load_sem.at[i]),
            pltpu.make_async_copy(
                wkv_hbm.at[pl.ds(start, width), :], wkv.at[i], load_sem.at[8 + i]
            ),
        )
        for load in pair:
            load.start()
        weight_loads.append(pair)
    out_order = (1, 3, 5, 7, 2, 6, 4, 0)
    out_loads = {}
    for i in out_order:
        start = pl.multiple_of((tp ^ i) * width, width)
        out_loads[i] = pltpu.make_async_copy(
            wo_hbm.at[:, pl.ds(start, width)], wo.at[i], load_sem.at[16 + i]
        )
        out_loads[i].start()

    barrier = pltpu.get_barrier_semaphore()
    for i in range(1, 8):
        pl.semaphore_signal(
            barrier, inc=1, device_id={"tp": tp ^ i}, device_id_type=pl.DeviceIdType.MESH
        )
    for i in range(1, 4):
        pl.semaphore_signal(
            barrier, inc=1, device_id={"inst": inst ^ i}, device_id_type=pl.DeviceIdType.MESH
        )
    xg[0] = x_ref[...]
    pl.semaphore_wait(barrier, 10)

    def feature_copy(k, src, dst, to, part=None):
        src_ref = xg.at[src] if part is None else xg.at[src, part]
        dst_ref = xg.at[dst] if part is None else xg.at[dst, part]
        return remote(src_ref, dst_ref, gather_send.at[k], gather_recv.at[k], tp=tp ^ to)

    along_x = [feature_copy(0, 0, 2, 2, 0), feature_copy(1, 0, 2, 2, 1)]
    along_y = [feature_copy(2, 0, 4, 4, 1), feature_copy(3, 0, 4, 4, 0)]
    to_sibling = [feature_copy(6, 0, 1, 1)]
    along_x[0].start()
    along_y[0].start()
    along_x[1].start()
    along_y[1].start()
    to_sibling[0].start()

    cache_load.wait()
    move_bits = [(1, 2) if j < moves // 2 else (2, 1) for j in range(moves)]
    first_moves = []
    for j in range(moves):
        leave[j] = cache[slot_ref[inst, j]]
        move = remote(
            leave.at[j], mid_in.at[j], move_send.at[j], move_recv.at[j], inst=inst ^ move_bits[j][0]
        )
        move.start()
        first_moves.append(move)

    @pl.loop(0, rows)
    def _(r):
        level = jnp.full((1, 2 * hd), len_ref[inst * rows + r], jnp.int32)
        place[pl.ds(r, 1), :] = level[:, :hd]

    row_ids = lax.broadcasted_iota(jnp.int32, (rows, hd), 0)
    own_place = place[...]
    next_place = own_place
    moved_len = []
    for j in range(moves):
        partner = inst ^ mask_ref[j]
        length = len_ref[partner * rows + slot_ref[partner, j]]
        moved_len.append(length)
        next_place = jnp.where(row_ids == slot_ref[inst, j], length, next_place)
    positions = jnp.concatenate([own_place, next_place + 1], 0).astype(jnp.float32)
    lane = lax.broadcasted_iota(jnp.int32, (1, hd), 1)
    pair_id = jnp.where(lane < hd // 2, lane, lane - hd // 2).astype(jnp.float32)
    frequency = jnp.exp(pair_id * (-2.0 * math.log(rope_base) / hd))
    angles = positions * frequency
    cosine = jnp.cos(angles)
    sine = jnp.sin(angles)
    sine = jnp.where(lane < hd // 2, -sine, sine)

    acc[...] = jnp.zeros_like(acc)
    square[...] = jnp.zeros_like(square)
    q_width = wq.shape[2]

    def project(i):
        for load in weight_loads[i]:
            load.wait()
        wide = xg[i].reshape(2 * rows, width).astype(jnp.float32)
        square[...] += jnp.sum(wide * wide, -1, keepdims=True)
        scaled = (wide * gain_ref[pl.ds(tp ^ i, 1), :]).astype(jnp.bfloat16)

        @pl.loop(0, q_width // 256)
        def _(c):
            cols = pl.ds(pl.multiple_of(c * 256, 256), 256)
            acc[:, cols] += jnp.dot(scaled, wq[i, :, cols], preferred_element_type=jnp.float32)

        acc[:, q_width:] += jnp.dot(scaled, wkv[i], preferred_element_type=jnp.float32)

    project(0)
    along_x[0].wait_recv()
    along_y[0].wait_recv()
    across = [feature_copy(4, 2, 6, 4, 0), feature_copy(5, 4, 6, 2, 1)]
    across[0].start()
    across[1].start()
    to_sibling[0].wait_recv()
    project(1)
    along_x[1].wait_recv()
    to_sibling.append(feature_copy(7, 2, 3, 1))
    to_sibling[1].start()
    along_y[1].wait_recv()
    to_sibling.append(feature_copy(8, 4, 5, 1))
    to_sibling[2].start()
    project(2)
    project(4)
    to_sibling[1].wait_recv()
    project(3)
    to_sibling[2].wait_recv()
    project(5)
    across[0].wait_recv()
    across[1].wait_recv()
    to_sibling.append(feature_copy(9, 6, 7, 1))
    to_sibling[3].start()
    project(6)
    to_sibling[3].wait_recv()
    project(7)

    factor = lax.rsqrt(square[...] * (1.0 / (8 * width)) + eps_norm)

    def turned(part):
        part = part * factor
        return (part * cosine + pltpu.roll(part, hd // 2, 1) * sine).astype(jnp.bfloat16)

    for h in range(heads):
        rotated = turned(acc[:, h * hd : (h + 1) * hd]).astype(jnp.float32)
        qs[:, h, :] = rotated[:rows]
        qs[:, heads + h, :] = rotated[rows:]
    fresh[:, :hd] = turned(acc[:, q_width : q_width + hd]).astype(jnp.float32)
    fresh[:, hd:] = (acc[:, q_width + hd :] * factor).astype(jnp.bfloat16).astype(jnp.float32)

    for j in range(moves):
        fsend[pl.ds(j, 1), :] = fresh[pl.ds(slot_ref[inst, j], 1), :]
    fresh_moves = []
    for i in range(1, 4):
        move = remote(
            fsend, frecv.at[i - 1], fresh_send.at[i - 1], fresh_recv.at[i - 1], inst=inst ^ i
        )
        move.start()
        fresh_moves.append(move)

    second_moves = []
    for j in range(moves):
        first_moves[j].wait_recv()
        taken = (mask_ref[j] & move_bits[j][0]) != 0
        mid[j] = jnp.where(taken, mid_in[j], leave[j])
        move = remote(
            mid.at[j],
            last_in.at[j],
            move_send.at[moves + j],
            move_recv.at[moves + j],
            inst=inst ^ move_bits[j][1],
        )
        move.start()
        second_moves.append(move)

    def attend(queries, keys, values, length, news):
        score = scale * lax.dot_general(
            queries.astype(jnp.bfloat16),
            keys,
            (((1,), (1,)), ((), ())),
            preferred_element_type=jnp.float32,
        )
        visible = lax.broadcasted_iota(jnp.int32, score.shape, 1) < length
        score = jnp.where(visible, score, floor_score)
        top = jnp.max(score, -1, keepdims=True)
        weights = jnp.where(visible, jnp.exp(score - top), 0.0).astype(jnp.bfloat16)
        total = jnp.sum(weights.astype(jnp.float32), -1, keepdims=True)
        mix = jnp.dot(weights, values, preferred_element_type=jnp.float32)
        marks = []
        overall = top
        for row, allowed in news:
            mark = scale * jnp.sum(queries * row[:, :hd], -1, keepdims=True)
            if allowed is not None:
                mark = jnp.where(allowed, mark, floor_score)
            marks.append(mark)
            overall = jnp.maximum(overall, mark)
        share = jnp.exp(top - overall)
        numerator = share * mix
        denominator = share * total
        for (row, allowed), mark in zip(news, marks):
            share = jnp.exp(mark - overall)
            if allowed is not None:
                share = jnp.where(allowed, share, 0.0)
            numerator = numerator + share * row[:, hd:]
            denominator = denominator + share
        return numerator / denominator

    later = lax.broadcasted_iota(jnp.int32, (2 * heads, 1), 0) >= heads

    @pl.loop(0, rows // 8)
    def _(group):
        for u in range(8):
            r = group * 8 + u
            mixed[r] = attend(
                qs[r],
                cache[r, :, :hd],
                cache[r, :, hd:],
                len_ref[inst * rows + r],
                [(fresh[pl.ds(r, 1), :], None), (fresh[pl.ds(rows + r, 1), :], later)],
            )

    for h in range(heads):
        cols = slice(h * hd, (h + 1) * hd)
        attended[:rows, cols] = mixed[:, h, :].astype(jnp.bfloat16)
        attended[rows:, cols] = mixed[:, heads + h, :].astype(jnp.bfloat16)

    tile = 256

    def column_loop(body):
        @pl.loop(0, width // tile)
        def _(c):
            body(pl.ds(pl.multiple_of(c * tile, tile), tile))

    def term(i, cols):
        return jnp.dot(attended[...], wo[i, :, cols], preferred_element_type=jnp.float32)

    sibling_sums = []
    for i in (1, 3, 5, 7):
        k = i // 2
        out_loads[i].wait()

        def body(cols):
            sib_send[k, :, cols] = term(i, cols).astype(jnp.bfloat16)

        column_loop(body)
        copy = remote(
            sib_send.at[k], sib_recv.at[k], sum_send.at[k], sum_recv.at[k], tp=tp ^ 1
        )
        copy.start()
        sibling_sums.append(copy)

    first_sums = [[None, None], [None, None]]

    def send_first(s, n):
        k = 4 + 2 * s + n
        copy = remote(
            first_send.at[s, n],
            first_recv.at[s, n],
            sum_send.at[k],
            sum_recv.at[k],
            tp=tp ^ (2, 4)[s],
        )
        copy.start()
        first_sums[s][n] = copy

    for i in (6, 2, 4, 0):
        k = i // 2
        out_loads[i].wait()
        sibling_sums[k].wait_recv()

        def body(cols):
            chip = term(i, cols) + sib_recv[k, :, cols].astype(jnp.float32)
            if i == 6:
                first_send[0, 1, :, cols] = chip[:rows].astype(jnp.bfloat16)
                first_send[1, 1, :, cols] = chip[rows:].astype(jnp.bfloat16)
            elif i == 2:
                first_send[0, 0, :, cols] = chip[:rows].astype(jnp.bfloat16)
                own[1, :rows, cols] = chip[rows:]
            elif i == 4:
                own[1, rows:, cols] = chip[:rows]
                first_send[1, 0, :, cols] = chip[rows:].astype(jnp.bfloat16)
            else:
                own[0, :, cols] = chip

        column_loop(body)
        if i == 6:
            send_first(0, 1)
            send_first(1, 1)
        elif i == 2:
            send_first(0, 0)
        elif i == 4:
            send_first(1, 0)

    second_sums = []
    for s in range(2):
        first_sums[s][1].wait_recv()
        base = own[1, rows:, :] if s == 0 else own[1, :rows, :]
        second_send[s] = (base + first_recv[s, 1].astype(jnp.float32)).astype(jnp.bfloat16)
        copy = remote(
            second_send.at[s],
            second_recv.at[s],
            sum_send.at[8 + s],
            sum_recv.at[8 + s],
            tp=tp ^ (4, 2)[s],
        )
        copy.start()
        second_sums.append(copy)

    for move in fresh_moves:
        move.wait_recv()
    for j in range(moves):
        second_moves[j].wait_recv()
        taken = (mask_ref[j] & move_bits[j][1]) != 0
        arrived_ref[j, 0] = jnp.where(taken, last_in[j], mid[j])
    for j in range(moves):
        mask = mask_ref[j]
        carried = jnp.where(
            mask == 1,
            frecv[0, pl.ds(j, 1), :],
            jnp.where(mask == 2, frecv[1, pl.ds(j, 1), :], frecv[2, pl.ds(j, 1), :]),
        )
        slot = slot_ref[inst, j]
        late_mixed[j] = attend(
            qs[slot],
            arrived_ref[j, 0, :, :hd],
            arrived_ref[j, 0, :, hd:],
            moved_len[j],
            [(carried, None), (fresh[pl.ds(rows + slot, 1), :], None)],
        )
    late = jnp.concatenate([late_mixed[:, heads + h, :] for h in range(heads)], -1)
    late = late.astype(jnp.bfloat16)
    late_copies = []
    for i in (6, 7, 2, 3, 4, 5, 1, 0):

        def body(cols):
            late_send[i, :, cols] = jnp.dot(
                late, wo[i, :, cols], preferred_element_type=jnp.float32
            )

        column_loop(body)
        if i:
            copy = remote(
                late_send.at[i],
                late_recv.at[i],
                late_send_sem.at[i],
                late_recv_sem.at[i],
                tp=tp ^ i,
            )
            copy.start()
            late_copies.append(copy)

    results = []
    for s in range(2):
        first_sums[s][0].wait_recv()
        second_sums[s].wait_recv()
        part = own[0, s * rows : (s + 1) * rows, :]
        part = part + first_recv[s, 0].astype(jnp.float32)
        results.append(part + second_recv[s].astype(jnp.float32))
    out_ref[0] = results[0].astype(jnp.bfloat16)
    late_total = late_send[0]
    for copy in late_copies:
        copy.wait_recv()
    for i in range(1, 8):
        late_total = late_total + late_recv[i]
    second = results[1]
    wide_ids = lax.broadcasted_iota(jnp.int32, second.shape, 0)
    for j in range(moves):
        second = jnp.where(wide_ids == slot_ref[inst, j], late_total[j : j + 1, :], second)
    out_ref[1] = second.astype(jnp.bfloat16)

    for copy in (
        along_x
        + along_y
        + across
        + to_sibling
        + first_moves
        + second_moves
        + fresh_moves
        + sibling_sums
        + first_sums[0]
        + first_sums[1]
        + second_sums
        + late_copies
    ):
        copy.wait_send()


def fused(
    x_steps, norm_gain, w_query, w_keyval, w_out, key_cache, lengths, moved_slots, partner_mask
):
    steps, rows, width = x_steps.shape
    moves = moved_slots.shape[1]
    block_len, pair_dim = key_cache.shape[2:]
    hd = pair_dim // 2
    q_width = w_query.shape[1]
    heads = q_width // hd
    both = steps * rows
    shards_tp = norm_gain.shape[0] // width
    bf16, f32 = jnp.bfloat16, jnp.float32
    smem = pl.BlockSpec(memory_space=pltpu.SMEM)
    vmem = pl.BlockSpec(memory_space=pltpu.VMEM)
    anywhere = pl.BlockSpec(memory_space=pl.ANY)
    dma = pltpu.SemaphoreType.DMA
    return pl.pallas_call(
        fused_kernel,
        out_shape=(
            jax.ShapeDtypeStruct((steps, rows, width), bf16),
            jax.ShapeDtypeStruct((moves,) + key_cache.shape[1:], bf16),
        ),
        in_specs=[smem, smem, smem, vmem, vmem, anywhere, anywhere, anywhere, anywhere],
        out_specs=(vmem, vmem),
        scratch_shapes=[
            pltpu.VMEM((8, width, q_width), bf16),
            pltpu.VMEM((8, width, pair_dim), bf16),
            pltpu.VMEM((8, q_width, width), bf16),
            pltpu.VMEM((rows, block_len, pair_dim), bf16),
            pltpu.VMEM((8, steps, rows, width), bf16),
            pltpu.VMEM((both, q_width + pair_dim), f32),
            pltpu.VMEM((both, 1), f32),
            pltpu.VMEM((rows, hd), jnp.int32),
            pltpu.VMEM((rows, 2 * heads, hd), f32),
            pltpu.VMEM((both, pair_dim), f32),
            pltpu.VMEM((rows, 2 * heads, hd), f32),
            pltpu.VMEM((both, q_width), bf16),
            pltpu.VMEM((moves, block_len, pair_dim), bf16),
            pltpu.VMEM((moves, block_len, pair_dim), bf16),
            pltpu.VMEM((moves, block_len, pair_dim), bf16),
            pltpu.VMEM((moves, block_len, pair_dim), bf16),
            pltpu.VMEM((moves, pair_dim), f32),
            pltpu.VMEM((3, moves, pair_dim), f32),
            pltpu.VMEM((4, both, width), bf16),
            pltpu.VMEM((4, both, width), bf16),
            pltpu.VMEM((2, both, width), f32),
            pltpu.VMEM((2, 2, rows, width), bf16),
            pltpu.VMEM((2, 2, rows, width), bf16),
            pltpu.VMEM((2, rows, width), bf16),
            pltpu.VMEM((2, rows, width), bf16),
            pltpu.VMEM((moves, 2 * heads, hd), f32),
            pltpu.VMEM((8, moves, width), f32),
            pltpu.VMEM((8, moves, width), f32),
            dma((25,)),
            dma((10,)),
            dma((10,)),
            dma((2 * moves,)),
            dma((2 * moves,)),
            dma((3,)),
            dma((3,)),
            dma((10,)),
            dma((10,)),
            dma((8,)),
            dma((8,)),
        ],
        compiler_params=pltpu.CompilerParams(
            collective_id=0, has_side_effects=True, vmem_limit_bytes=60 * 2**20
        ),
        cost_estimate=pl.CostEstimate(
            flops=2 * both * w_query.shape[0] * (2 * q_width + pair_dim),
            bytes_accessed=2 * (w_query.size + w_keyval.size + w_out.size + key_cache.size),
            transcendentals=0,
        ),
    )(
        lengths,
        moved_slots,
        partner_mask,
        x_steps,
        norm_gain.reshape(shards_tp, width),
        w_query,
        w_keyval,
        w_out,
        key_cache.reshape(rows, block_len, pair_dim),
    )


def solution(mesh):
    placed = (
        P(None, "inst", "tp"),
        P(),
        P(None, "tp"),
        P(None, "tp"),
        P("tp", None),
        P("inst", "tp", None, None),
        P(),
        P(),
        P(),
    )
    body = fused if mesh.shape["tp"] == KVH and mesh.shape["inst"] == 4 else shards
    return jax.shard_map(
        body,
        mesh=mesh,
        in_specs=placed,
        out_specs=(P(None, "inst", "tp"), P("inst", "tp", None, None)),
        check_vma=False,
    )
```

```python
from functools import reduce
import math

import jax
import jax.numpy as jnp
from jax import lax
from jax.experimental import pallas as pl
from jax.experimental.pallas import tpu as pltpu
from jax.sharding import PartitionSpec as P

KVH = 8


eps_norm = 1e-05
rope_base = 500000.0
floor_score = -1e30


def from_partner(block, axis, bit):
    count = lax.axis_size(axis)
    route = []
    for low in range(count):
        high = low | 1 << bit
        if high != low and high < count:
            route += [(low, high), (high, low)]
    return lax.ppermute(block, axis, route)


def as_sent(value):

    def short(part):
        return part.astype(jnp.bfloat16) if part.dtype == jnp.float32 else part

    return jax.tree.map(short, value)


def rotary(vectors, positions):
    half_dim = vectors.shape[-1] // 2
    frequency = rope_base ** (-(jnp.arange(half_dim, dtype=jnp.float32) * 2.0) / vectors.shape[-1])
    angles = positions.astype(jnp.float32)[..., None] * frequency
    cosine = jnp.cos(angles)[..., None, :]
    sine_part = jnp.sin(angles)[..., None, :]
    first_half = vectors[..., :half_dim]
    second_half = vectors[..., half_dim:]
    return jnp.concatenate(
        [
            first_half * cosine - second_half * sine_part,
            second_half * cosine + first_half * sine_part,
        ],
        -1,
    )


def block_terms(queries, block, start, length_rows):
    head_dim = queries.shape[-1]
    block_len = block.shape[1]
    scores = jnp.einsum(
        "rhd,rtd->rht", queries, block[..., :head_dim], preferred_element_type=jnp.float32
    ) / math.sqrt(head_dim)
    places = start + jnp.arange(block_len, dtype=jnp.int32)
    visible = (places[None, :] < length_rows[:, None])[:, None, :]
    scores = jnp.where(visible, scores, floor_score)
    block_max = jnp.max(scores, -1)
    weights = jnp.where(visible, jnp.exp(scores - block_max[..., None]), 0.0).astype(jnp.bfloat16)
    block_sum = jnp.sum(weights.astype(jnp.float32), -1)
    block_mix = jnp.einsum(
        "rht,rtd->rhd", weights, block[..., head_dim:], preferred_element_type=jnp.float32
    )
    return (block_max, block_sum, block_mix)


def fresh_terms(queries, fresh_kv):
    head_dim = queries.shape[-1]
    score = jnp.einsum(
        "rhd,rd->rh", queries, fresh_kv[:, :head_dim], preferred_element_type=jnp.float32
    ) / math.sqrt(head_dim)
    block_mix = jnp.broadcast_to(fresh_kv[:, None, head_dim:].astype(jnp.float32), queries.shape)
    return (score, jnp.ones_like(score), block_mix)


def combine(pieces):
    overall_max = reduce(jnp.maximum, [piece[0] for piece in pieces])
    numerator = reduce(
        jnp.add, [jnp.exp(piece[0] - overall_max)[..., None] * piece[2] for piece in pieces]
    )
    denominator = reduce(jnp.add, [jnp.exp(piece[0] - overall_max) * piece[1] for piece in pieces])
    return numerator / denominator[..., None]


def shards(
    x_steps, norm_gain, w_query, w_keyval, w_out, key_cache, lengths, moved_slots, partner_mask
):
    row_count = x_steps.shape[1]
    head_dim = key_cache.shape[-1] // 2
    block_len = key_cache.shape[2]
    group_size = lax.axis_size("tp") // KVH
    group_bits = group_size.bit_length() - 1
    member = lax.axis_index("tp") % group_size
    instance = lax.axis_index("inst")
    own_heads = w_query.shape[1] // head_dim
    own_lengths = lax.dynamic_slice_in_dim(lengths, instance * row_count, row_count)

    def collect(value, swapper):
        stacked = jax.tree.map(lambda leaf: leaf[None], value)
        for bit_index in range(group_bits):
            received = swapper(stacked, bit_index)
            low_side = member >> bit_index & 1 == 0
            stacked = jax.tree.map(
                lambda mine_part, their_part: jnp.where(
                    low_side,
                    jnp.concatenate([mine_part, their_part], 0),
                    jnp.concatenate([their_part, mine_part], 0),
                ),
                stacked,
                received,
            )
        return stacked

    def decode(step_index, positions, cache_rows, length_rows, earlier):
        gathered = lax.all_gather(x_steps[step_index], "tp", axis=1, tiled=True)
        widened = gathered.astype(jnp.float32)
        normed = (
            widened
            * lax.rsqrt(jnp.mean(widened * widened, -1, keepdims=True) + eps_norm)
            * norm_gain
        ).astype(jnp.bfloat16)
        query_raw = jnp.dot(normed, w_query, preferred_element_type=jnp.float32)
        keyval_raw = jnp.dot(normed, w_keyval, preferred_element_type=jnp.float32)
        joined = collect(
            jnp.concatenate([query_raw, keyval_raw], 1),
            lambda value, bit_index: from_partner(value, "tp", bit_index),
        )
        query_width = own_heads * head_dim
        query_all = jnp.moveaxis(joined[:, :, :query_width], 0, 1).reshape(
            row_count, group_size * own_heads, head_dim
        )
        keyval = jnp.moveaxis(joined[:, :, query_width:], 0, 1).reshape(row_count, 2 * head_dim)
        queries = rotary(query_all, positions).astype(jnp.bfloat16)
        partial_value = block_terms(queries, cache_rows[:, 0], member * block_len, length_rows)
        shared = collect(
            partial_value, lambda value, bit_index: from_partner(value, "tp", bit_index)
        )
        own_queries = lax.dynamic_slice_in_dim(queries, member * own_heads, own_heads, 1)
        pieces = [
            tuple(
                (
                    lax.dynamic_slice_in_dim(
                        member_part[block_index], member * own_heads, own_heads, 1
                    )
                    for member_part in shared
                )
            )
            for block_index in range(group_size)
        ]
        fresh_kv = jnp.concatenate(
            [rotary(keyval[:, None, :head_dim], positions)[:, 0], keyval[:, head_dim:]], -1
        ).astype(jnp.bfloat16)
        for fresh_item in earlier + [fresh_kv]:
            pieces.append(fresh_terms(own_queries, fresh_item))
        attended = combine(pieces).reshape(row_count, own_heads * head_dim).astype(jnp.bfloat16)
        head_terms = jnp.dot(attended, w_out, preferred_element_type=jnp.float32)
        return (
            lax.psum_scatter(head_terms, "tp", scatter_dimension=1, tiled=True).astype(
                jnp.bfloat16
            ),
            fresh_kv,
        )

    first_out, first_fresh = decode(0, own_lengths, key_cache, own_lengths, [])
    move_count = moved_slots.shape[1]
    move_ids = jnp.arange(move_count, dtype=jnp.int32)
    partner = jnp.bitwise_xor(instance, partner_mask)
    slots_self = moved_slots[instance]
    slots_partner = moved_slots[partner, move_ids]
    payload = (key_cache[slots_self], first_fresh[slots_self])
    moving = payload
    for bit_index in range(lax.axis_size("inst").bit_length() - 1):
        received = jax.tree.map(
            lambda part, own: part.astype(own.dtype),
            from_partner(as_sent(moving), "inst", bit_index),
            moving,
        )
        use_swap = partner_mask >> bit_index & 1 == 1
        moving = jax.tree.map(
            lambda their_part, mine_part: jnp.where(
                use_swap.reshape((move_count,) + (1,) * (mine_part.ndim - 1)), their_part, mine_part
            ),
            received,
            moving,
        )
    arrived_rows, arrived_fresh = moving
    cache_next = key_cache.at[slots_self].set(arrived_rows)
    fresh_next = first_fresh.at[slots_self].set(arrived_fresh)
    length_next = own_lengths.at[slots_self].set(lengths[partner * row_count + slots_partner])
    second_out, unused = decode(1, length_next + 1, cache_next, length_next, [fresh_next])
    return (jnp.stack([first_out, second_out]), arrived_rows)


def hand_on(out_ref, arrived_ref, out_final, arrived_final, sem):
    copies = [
        pltpu.make_async_copy(source.at[i], target.at[i], sem.at[first + i])
        for source, target, first in ((out_ref, out_final, 0), (arrived_ref, arrived_final, 2))
        for i in range(source.shape[0])
    ]
    for copy in copies:
        copy.start()
    for copy in copies:
        copy.wait()


def fused_kernel(
    len_ref,
    slot_ref,
    mask_ref,
    x_ref,
    gain_ref,
    wq_hbm,
    wkv_hbm,
    wo_hbm,
    cache_hbm,
    out_ref,
    arrived_ref,
    wq,
    wkv,
    wo,
    cache,
    xg,
    acc,
    square,
    place,
    qs,
    fresh,
    mixed,
    attended,
    leave,
    mid_in,
    mid,
    last_in,
    ask_query,
    ask_fresh,
    asked_query,
    asked_fresh,
    reply,
    replied,
    sib_send,
    sib_recv,
    own,
    first_send,
    first_recv,
    second_send,
    second_recv,
    load_sem,
    gather_send,
    gather_recv,
    move_send,
    move_recv,
    ask_send,
    ask_recv,
    reply_send,
    reply_recv,
    sum_send,
    sum_recv,
):
    tp = lax.axis_index("tp")
    inst = lax.axis_index("inst")
    rows = x_ref.shape[1]
    width = x_ref.shape[2]
    moves = slot_ref.shape[1]
    hd = cache.shape[-1] // 2
    heads = qs.shape[1] // 2
    scale = 1.0 / math.sqrt(hd)

    def remote(src, dst, send, recv, **where):
        return pltpu.make_async_remote_copy(
            src_ref=src,
            dst_ref=dst,
            send_sem=send,
            recv_sem=recv,
            device_id=where,
            device_id_type=pl.DeviceIdType.MESH,
        )

    quarter = rows // 4
    cache_loads = [
        pltpu.make_async_copy(
            cache_hbm.at[pl.ds(n * quarter, quarter)],
            cache.at[pl.ds(n * quarter, quarter)],
            load_sem.at[24 + n],
        )
        for n in range(4)
    ]
    for load in cache_loads:
        load.start()
    weight_loads = []
    out_loads = []
    for i in range(8):
        start = pl.multiple_of((tp ^ i) * width, width)
        weight_loads.append(
            (
                pltpu.make_async_copy(wq_hbm.at[pl.ds(start, width), :], wq.at[i], load_sem.at[i]),
                pltpu.make_async_copy(
                    wkv_hbm.at[pl.ds(start, width), :], wkv.at[i], load_sem.at[8 + i]
                ),
            )
        )
        out_loads.append(
            pltpu.make_async_copy(
                wo_hbm.at[:, pl.ds(start, width)], wo.at[i], load_sem.at[16 + i]
            )
        )

    def load_weights(*order):
        for i in order:
            for load in weight_loads[i]:
                load.start()

    load_weights(0)

    barrier = pltpu.get_barrier_semaphore()
    for i in range(1, 8):
        pl.semaphore_signal(
            barrier, inc=1, device_id={"tp": tp ^ i}, device_id_type=pl.DeviceIdType.MESH
        )
    for i in range(1, 4):
        pl.semaphore_signal(
            barrier, inc=1, device_id={"inst": inst ^ i}, device_id_type=pl.DeviceIdType.MESH
        )
    xg[0] = x_ref[...]
    pl.semaphore_wait(barrier, 10)

    def feature_copy(k, src, dst, to, part=None):
        src_ref = xg.at[src] if part is None else xg.at[src, part]
        dst_ref = xg.at[dst] if part is None else xg.at[dst, part]
        return remote(src_ref, dst_ref, gather_send.at[k], gather_recv.at[k], tp=tp ^ to)

    along_x = [feature_copy(0, 0, 2, 2, 0), feature_copy(1, 0, 2, 2, 1)]
    along_y = [feature_copy(2, 0, 4, 4, 1), feature_copy(3, 0, 4, 4, 0)]
    to_sibling = [feature_copy(6, 0, 1, 1)]
    along_x[0].start()
    along_y[0].start()
    along_x[1].start()
    along_y[1].start()
    to_sibling[0].start()

    for load in cache_loads:
        load.wait()
    load_weights(1, 2, 4)
    move_bits = [(1, 2) if j < moves // 2 else (2, 1) for j in range(moves)]
    first_moves = []
    for j in range(moves):
        leave[j] = cache[slot_ref[inst, j]]
        move = remote(
            leave.at[j], mid_in.at[j], move_send.at[j], move_recv.at[j], inst=inst ^ move_bits[j][0]
        )
        move.start()
        first_moves.append(move)

    @pl.loop(0, rows)
    def _(r):
        level = jnp.full((1, 2 * hd), len_ref[inst * rows + r], jnp.int32)
        place[pl.ds(r, 1), :] = level[:, :hd]

    row_ids = lax.broadcasted_iota(jnp.int32, (rows, hd), 0)
    own_place = place[...]
    next_place = own_place
    for j in range(moves):
        partner = inst ^ mask_ref[j]
        length = len_ref[partner * rows + slot_ref[partner, j]]
        next_place = jnp.where(row_ids == slot_ref[inst, j], length, next_place)
    positions = jnp.concatenate([own_place, next_place + 1], 0).astype(jnp.float32)
    lane = lax.broadcasted_iota(jnp.int32, (1, hd), 1)
    pair_id = jnp.where(lane < hd // 2, lane, lane - hd // 2).astype(jnp.float32)
    frequency = jnp.exp(pair_id * (-2.0 * math.log(rope_base) / hd))
    angles = positions * frequency
    cosine = jnp.cos(angles)
    sine = jnp.sin(angles)
    sine = jnp.where(lane < hd // 2, -sine, sine)

    acc[...] = jnp.zeros_like(acc)
    square[...] = jnp.zeros_like(square)
    q_width = wq.shape[2]

    def project(i):
        for load in weight_loads[i]:
            load.wait()
        wide = xg[i].reshape(2 * rows, width).astype(jnp.float32)
        square[...] += jnp.sum(wide * wide, -1, keepdims=True)
        start = pl.multiple_of((tp ^ i) * width, width)
        gain = gain_ref[pl.ds(start, width)]
        scaled = (wide * gain[None, :]).astype(jnp.bfloat16)

        for c in range(0, q_width, 512):
            cols = slice(c, c + 512)
            acc[:, cols] += jnp.dot(scaled, wq[i, :, cols], preferred_element_type=jnp.float32)

        acc[:, q_width:] += jnp.dot(scaled, wkv[i], preferred_element_type=jnp.float32)

    project(0)
    load_weights(3, 5)
    along_x[0].wait_recv()
    along_y[0].wait_recv()
    across = [feature_copy(4, 2, 6, 4, 0), feature_copy(5, 4, 6, 2, 1)]
    across[0].start()
    across[1].start()
    to_sibling[0].wait_recv()
    project(1)
    load_weights(6, 7)
    along_x[1].wait_recv()
    to_sibling.append(feature_copy(7, 2, 3, 1))
    to_sibling[1].start()
    along_y[1].wait_recv()
    to_sibling.append(feature_copy(8, 4, 5, 1))
    to_sibling[2].start()
    project(2)
    project(4)
    for i in (1, 3, 5, 7):
        out_loads[i].start()
    to_sibling[1].wait_recv()
    project(3)
    to_sibling[2].wait_recv()
    project(5)
    for i in (6, 2, 4, 0):
        out_loads[i].start()
    across[0].wait_recv()
    across[1].wait_recv()
    to_sibling.append(feature_copy(9, 6, 7, 1))
    to_sibling[3].start()
    project(6)
    to_sibling[3].wait_recv()
    project(7)

    factor = lax.rsqrt(square[...] * (1.0 / (8 * width)) + eps_norm)

    def turned(part):
        part = part * factor
        return (part * cosine + pltpu.roll(part, hd // 2, 1) * sine).astype(jnp.bfloat16)

    for h in range(heads):
        rotated = turned(acc[:, h * hd : (h + 1) * hd]).astype(jnp.float32)
        qs[:, h, :] = rotated[:rows]
        qs[:, heads + h, :] = rotated[rows:]
    fresh[:, :hd] = turned(acc[:, q_width : q_width + hd]).astype(jnp.float32)
    fresh[:, hd:] = (acc[:, q_width + hd :] * factor).astype(jnp.bfloat16).astype(jnp.float32)

    slots = [slot_ref[inst, j] for j in range(moves)]
    ask_query[...] = jnp.concatenate([qs[slot, heads:, :] for slot in slots], 0).astype(
        jnp.bfloat16
    )
    for j in range(moves):
        ask_fresh[pl.ds(j, 1), :] = fresh[pl.ds(rows + slots[j], 1), :]
    asks = []
    for i in range(3):
        pair = (
            remote(
                ask_query, asked_query.at[i], ask_send.at[i], ask_recv.at[i], inst=inst ^ (i + 1)
            ),
            remote(
                ask_fresh,
                asked_fresh.at[i],
                ask_send.at[3 + i],
                ask_recv.at[3 + i],
                inst=inst ^ (i + 1),
            ),
        )
        for copy in pair:
            copy.start()
            asks.append(copy)

    def matched(mask, parts):
        return jnp.where(mask == 1, parts[0], jnp.where(mask == 2, parts[1], parts[2]))

    def attend(requests):
        scores = [
            scale
            * lax.dot_general(
                queries.astype(jnp.bfloat16),
                keys,
                (((1,), (1,)), ((), ())),
                preferred_element_type=jnp.float32,
            )
            for queries, keys, values, length, news in requests
        ]
        spots = lax.broadcasted_iota(jnp.int32, scores[0].shape, 1)
        scores = [
            jnp.where(spots < request[3], score, floor_score)
            for score, request in zip(scores, requests)
        ]
        tops = [jnp.max(score, -1, keepdims=True) for score in scores]
        marks = []
        for queries, keys, values, length, news in requests:
            row_marks = []
            for row, allowed in news:
                mark = scale * jnp.sum(queries * row[:, :hd], -1, keepdims=True)
                if allowed is not None:
                    mark = jnp.where(allowed, mark, floor_score)
                row_marks.append(mark)
            marks.append(row_marks)
        weights = [
            jnp.where(spots < request[3], jnp.exp(score - top), 0.0).astype(jnp.bfloat16)
            for score, top, request in zip(scores, tops, requests)
        ]
        mixes = [
            jnp.dot(weight, request[2], preferred_element_type=jnp.float32)
            for weight, request in zip(weights, requests)
        ]
        totals = [jnp.sum(weight.astype(jnp.float32), -1, keepdims=True) for weight in weights]
        answers = []
        for request, top, row_marks, mix, total in zip(requests, tops, marks, mixes, totals):
            overall = reduce(jnp.maximum, row_marks, top)
            share = jnp.exp(top - overall)
            numerator = share * mix
            denominator = share * total
            for (row, allowed), mark in zip(request[4], row_marks):
                share = jnp.exp(mark - overall)
                if allowed is not None:
                    share = jnp.where(allowed, share, 0.0)
                numerator = numerator + share * row[:, hd:]
                denominator = denominator + share
            answers.append(numerator / denominator)
        return answers

    later = lax.broadcasted_iota(jnp.int32, (2 * heads, 1), 0) >= heads
    batch = 16

    def attend_slots(first, last):
        @pl.loop(first, last)
        def _(group):
            ids = [group * batch + u for u in range(batch)]
            answers = attend(
                [
                    (
                        qs[r],
                        cache[r, :, :hd],
                        cache[r, :, hd:],
                        len_ref[inst * rows + r],
                        [(fresh[pl.ds(r, 1), :], None), (fresh[pl.ds(rows + r, 1), :], later)],
                    )
                    for r in ids
                ]
            )
            for r, answer in zip(ids, answers):
                mixed[r] = answer

    groups = rows // batch
    attend_slots(0, groups // 2)

    for copy in asks:
        copy.wait_recv()
    requests = []
    for j in range(moves):
        slot = slots[j]
        mask = mask_ref[j]
        part = slice(j * heads, (j + 1) * heads)
        queries = matched(mask, [asked_query[i].astype(jnp.float32)[part] for i in range(3)])
        news = matched(mask, [asked_fresh[i, pl.ds(j, 1), :] for i in range(3)])
        requests.append(
            (
                queries,
                cache[slot, :, :hd],
                cache[slot, :, hd:],
                len_ref[inst * rows + slot],
                [(fresh[pl.ds(slot, 1), :], None), (news, None)],
            )
        )
    reply[...] = jnp.concatenate(attend(requests), 0).astype(jnp.bfloat16)
    replies = []
    for i in range(3):
        copy = remote(
            reply, replied.at[i], reply_send.at[i], reply_recv.at[i], inst=inst ^ (i + 1)
        )
        copy.start()
        replies.append(copy)

    second_moves = []
    for j in range(moves):
        first_moves[j].wait_recv()
        taken = (mask_ref[j] & move_bits[j][0]) != 0
        mid[j] = jnp.where(taken, mid_in[j], leave[j])
        move = remote(
            mid.at[j],
            last_in.at[j],
            move_send.at[moves + j],
            move_recv.at[moves + j],
            inst=inst ^ move_bits[j][1],
        )
        move.start()
        second_moves.append(move)

    attend_slots(groups // 2, groups)

    for copy in replies:
        copy.wait_recv()
    came = [
        matched(
            mask_ref[j],
            [replied[i].astype(jnp.float32)[j * heads : (j + 1) * heads] for i in range(3)],
        )
        for j in range(moves)
    ]
    for h in range(heads):
        cols = slice(h * hd, (h + 1) * hd)
        attended[:rows, cols] = mixed[:, h, :].astype(jnp.bfloat16)
        second = mixed[:, heads + h, :]
        for j in range(moves):
            second = jnp.where(row_ids == slots[j], came[j][h : h + 1], second)
        attended[rows:, cols] = second.astype(jnp.bfloat16)

    tile = 512

    def column_loop(body):
        @pl.loop(0, width // tile)
        def _(c):
            body(pl.ds(pl.multiple_of(c * tile, tile), tile))

    def term(i, cols):
        return jnp.dot(attended[...], wo[i, :, cols], preferred_element_type=jnp.float32)

    sibling_sums = []
    for i in (1, 3, 5, 7):
        k = i // 2
        out_loads[i].wait()

        def body(cols):
            sib_send[k, :, cols] = term(i, cols).astype(jnp.bfloat16)

        column_loop(body)
        copy = remote(
            sib_send.at[k], sib_recv.at[k], sum_send.at[k], sum_recv.at[k], tp=tp ^ 1
        )
        copy.start()
        sibling_sums.append(copy)

    first_sums = [[None, None], [None, None]]

    def send_first(s, n):
        k = 4 + 2 * s + n
        copy = remote(
            first_send.at[s, n],
            first_recv.at[s, n],
            sum_send.at[k],
            sum_recv.at[k],
            tp=tp ^ (2, 4)[s],
        )
        copy.start()
        first_sums[s][n] = copy

    for i in (6, 2, 4, 0):
        k = i // 2
        out_loads[i].wait()
        sibling_sums[k].wait_recv()

        def body(cols):
            chip = term(i, cols) + sib_recv[k, :, cols].astype(jnp.float32)
            if i == 6:
                first_send[0, 1, :, cols] = chip[:rows].astype(jnp.bfloat16)
                first_send[1, 1, :, cols] = chip[rows:].astype(jnp.bfloat16)
            elif i == 2:
                first_send[0, 0, :, cols] = chip[:rows].astype(jnp.bfloat16)
                own[1, :rows, cols] = chip[rows:]
            elif i == 4:
                own[1, rows:, cols] = chip[:rows]
                first_send[1, 0, :, cols] = chip[rows:].astype(jnp.bfloat16)
            else:
                own[0, :, cols] = chip

        column_loop(body)
        if i == 6:
            send_first(0, 1)
            send_first(1, 1)
        elif i == 2:
            send_first(0, 0)
        elif i == 4:
            send_first(1, 0)

    second_sums = []
    for s in range(2):
        first_sums[s][1].wait_recv()
        base = own[1, rows:, :] if s == 0 else own[1, :rows, :]
        second_send[s] = (base + first_recv[s, 1].astype(jnp.float32)).astype(jnp.bfloat16)
        copy = remote(
            second_send.at[s],
            second_recv.at[s],
            sum_send.at[8 + s],
            sum_recv.at[8 + s],
            tp=tp ^ (4, 2)[s],
        )
        copy.start()
        second_sums.append(copy)

    for j in range(moves):
        second_moves[j].wait_recv()
        taken = (mask_ref[j] & move_bits[j][1]) != 0
        arrived_ref[j, 0] = jnp.where(taken, last_in[j], mid[j])

    for s in range(2):
        first_sums[s][0].wait_recv()
        second_sums[s].wait_recv()
        part = own[0, s * rows : (s + 1) * rows, :]
        part = part + first_recv[s, 0].astype(jnp.float32)
        out_ref[s] = (part + second_recv[s].astype(jnp.float32)).astype(jnp.bfloat16)

    for copy in (
        along_x
        + along_y
        + across
        + to_sibling
        + first_moves
        + second_moves
        + asks
        + replies
        + sibling_sums
        + first_sums[0]
        + first_sums[1]
        + second_sums
    ):
        copy.wait_send()


def fused(
    x_steps, norm_gain, w_query, w_keyval, w_out, key_cache, lengths, moved_slots, partner_mask
):
    steps, rows, width = x_steps.shape
    moves = moved_slots.shape[1]
    block_len, pair_dim = key_cache.shape[2:]
    hd = pair_dim // 2
    q_width = w_query.shape[1]
    heads = q_width // hd
    both = steps * rows
    bf16, f32 = jnp.bfloat16, jnp.float32
    smem = pl.BlockSpec(memory_space=pltpu.SMEM)
    vmem = pl.BlockSpec(memory_space=pltpu.VMEM)
    anywhere = pl.BlockSpec(memory_space=pl.ANY)
    dma = pltpu.SemaphoreType.DMA
    results = pl.pallas_call(
        fused_kernel,
        out_shape=(
            jax.ShapeDtypeStruct((steps, rows, width), bf16),
            jax.ShapeDtypeStruct((moves,) + key_cache.shape[1:], bf16),
        ),
        in_specs=[smem, smem, smem, vmem, vmem, anywhere, anywhere, anywhere, anywhere],
        out_specs=(vmem, vmem),
        scratch_shapes=[
            pltpu.VMEM((8, width, q_width), bf16),
            pltpu.VMEM((8, width, pair_dim), bf16),
            pltpu.VMEM((8, q_width, width), bf16),
            pltpu.VMEM((rows, block_len, pair_dim), bf16),
            pltpu.VMEM((8, steps, rows, width), bf16),
            pltpu.VMEM((both, q_width + pair_dim), f32),
            pltpu.VMEM((both, 1), f32),
            pltpu.VMEM((rows, hd), jnp.int32),
            pltpu.VMEM((rows, 2 * heads, hd), f32),
            pltpu.VMEM((both, pair_dim), f32),
            pltpu.VMEM((rows, 2 * heads, hd), f32),
            pltpu.VMEM((both, q_width), bf16),
            pltpu.VMEM((moves, block_len, pair_dim), bf16),
            pltpu.VMEM((moves, block_len, pair_dim), bf16),
            pltpu.VMEM((moves, block_len, pair_dim), bf16),
            pltpu.VMEM((moves, block_len, pair_dim), bf16),
            pltpu.VMEM((moves * heads, hd), bf16),
            pltpu.VMEM((moves, pair_dim), f32),
            pltpu.VMEM((3, moves * heads, hd), bf16),
            pltpu.VMEM((3, moves, pair_dim), f32),
            pltpu.VMEM((moves * heads, hd), bf16),
            pltpu.VMEM((3, moves * heads, hd), bf16),
            pltpu.VMEM((4, both, width), bf16),
            pltpu.VMEM((4, both, width), bf16),
            pltpu.VMEM((2, both, width), f32),
            pltpu.VMEM((2, 2, rows, width), bf16),
            pltpu.VMEM((2, 2, rows, width), bf16),
            pltpu.VMEM((2, rows, width), bf16),
            pltpu.VMEM((2, rows, width), bf16),
            dma((28,)),
            dma((10,)),
            dma((10,)),
            dma((2 * moves,)),
            dma((2 * moves,)),
            dma((6,)),
            dma((6,)),
            dma((3,)),
            dma((3,)),
            dma((10,)),
            dma((10,)),
        ],
        compiler_params=pltpu.CompilerParams(
            collective_id=0, has_side_effects=True, vmem_limit_bytes=60 * 2**20
        ),
        cost_estimate=pl.CostEstimate(
            flops=2 * both * w_query.shape[0] * (2 * q_width + pair_dim),
            bytes_accessed=2 * (w_query.size + w_keyval.size + w_out.size + key_cache.size),
            transcendentals=0,
        ),
    )(
        lengths,
        moved_slots,
        partner_mask,
        x_steps,
        norm_gain,
        w_query,
        w_keyval,
        w_out,
        key_cache.reshape(rows, block_len, pair_dim),
    )
    return pl.pallas_call(
        hand_on,
        out_shape=tuple(jax.ShapeDtypeStruct(part.shape, part.dtype) for part in results),
        in_specs=[anywhere, anywhere],
        out_specs=(anywhere, anywhere),
        scratch_shapes=[dma((10,))],
        compiler_params=pltpu.CompilerParams(vmem_limit_bytes=60 * 2**20),
    )(*results)


def solution(mesh):
    placed = (
        P(None, "inst", "tp"),
        P(),
        P(None, "tp"),
        P(None, "tp"),
        P("tp", None),
        P("inst", "tp", None, None),
        P(),
        P(),
        P(),
    )
    body = fused if mesh.shape["tp"] == KVH and mesh.shape["inst"] == 4 else shards
    return jax.shard_map(
        body,
        mesh=mesh,
        in_specs=placed,
        out_specs=(P(None, "inst", "tp"), P("inst", "tp", None, None)),
        check_vma=False,
    )
```

```python
from functools import reduce
import math

import jax
import jax.numpy as jnp
from jax import lax
from jax.experimental import pallas as pl
from jax.experimental.pallas import tpu as pltpu
from jax.sharding import PartitionSpec as P

KVH = 8


eps_norm = 1e-05
rope_base = 500000.0
floor_score = -1e30


def from_partner(block, axis, bit):
    count = lax.axis_size(axis)
    route = []
    for low in range(count):
        high = low | 1 << bit
        if high != low and high < count:
            route += [(low, high), (high, low)]
    return lax.ppermute(block, axis, route)


def as_sent(value):

    def short(part):
        return part.astype(jnp.bfloat16) if part.dtype == jnp.float32 else part

    return jax.tree.map(short, value)


def rotary(vectors, positions):
    half_dim = vectors.shape[-1] // 2
    frequency = rope_base ** (-(jnp.arange(half_dim, dtype=jnp.float32) * 2.0) / vectors.shape[-1])
    angles = positions.astype(jnp.float32)[..., None] * frequency
    cosine = jnp.cos(angles)[..., None, :]
    sine_part = jnp.sin(angles)[..., None, :]
    first_half = vectors[..., :half_dim]
    second_half = vectors[..., half_dim:]
    return jnp.concatenate(
        [
            first_half * cosine - second_half * sine_part,
            second_half * cosine + first_half * sine_part,
        ],
        -1,
    )


def block_terms(queries, block, start, length_rows):
    head_dim = queries.shape[-1]
    block_len = block.shape[1]
    scores = jnp.einsum(
        "rhd,rtd->rht", queries, block[..., :head_dim], preferred_element_type=jnp.float32
    ) / math.sqrt(head_dim)
    places = start + jnp.arange(block_len, dtype=jnp.int32)
    visible = (places[None, :] < length_rows[:, None])[:, None, :]
    scores = jnp.where(visible, scores, floor_score)
    block_max = jnp.max(scores, -1)
    weights = jnp.where(visible, jnp.exp(scores - block_max[..., None]), 0.0).astype(jnp.bfloat16)
    block_sum = jnp.sum(weights.astype(jnp.float32), -1)
    block_mix = jnp.einsum(
        "rht,rtd->rhd", weights, block[..., head_dim:], preferred_element_type=jnp.float32
    )
    return (block_max, block_sum, block_mix)


def fresh_terms(queries, fresh_kv):
    head_dim = queries.shape[-1]
    score = jnp.einsum(
        "rhd,rd->rh", queries, fresh_kv[:, :head_dim], preferred_element_type=jnp.float32
    ) / math.sqrt(head_dim)
    block_mix = jnp.broadcast_to(fresh_kv[:, None, head_dim:].astype(jnp.float32), queries.shape)
    return (score, jnp.ones_like(score), block_mix)


def combine(pieces):
    overall_max = reduce(jnp.maximum, [piece[0] for piece in pieces])
    numerator = reduce(
        jnp.add, [jnp.exp(piece[0] - overall_max)[..., None] * piece[2] for piece in pieces]
    )
    denominator = reduce(jnp.add, [jnp.exp(piece[0] - overall_max) * piece[1] for piece in pieces])
    return numerator / denominator[..., None]


def shards(
    x_steps, norm_gain, w_query, w_keyval, w_out, key_cache, lengths, moved_slots, partner_mask
):
    row_count = x_steps.shape[1]
    head_dim = key_cache.shape[-1] // 2
    block_len = key_cache.shape[2]
    group_size = lax.axis_size("tp") // KVH
    group_bits = group_size.bit_length() - 1
    member = lax.axis_index("tp") % group_size
    instance = lax.axis_index("inst")
    own_heads = w_query.shape[1] // head_dim
    own_lengths = lax.dynamic_slice_in_dim(lengths, instance * row_count, row_count)

    def collect(value, swapper):
        stacked = jax.tree.map(lambda leaf: leaf[None], value)
        for bit_index in range(group_bits):
            received = swapper(stacked, bit_index)
            low_side = member >> bit_index & 1 == 0
            stacked = jax.tree.map(
                lambda mine_part, their_part: jnp.where(
                    low_side,
                    jnp.concatenate([mine_part, their_part], 0),
                    jnp.concatenate([their_part, mine_part], 0),
                ),
                stacked,
                received,
            )
        return stacked

    def decode(step_index, positions, cache_rows, length_rows, earlier):
        gathered = lax.all_gather(x_steps[step_index], "tp", axis=1, tiled=True)
        widened = gathered.astype(jnp.float32)
        normed = (
            widened
            * lax.rsqrt(jnp.mean(widened * widened, -1, keepdims=True) + eps_norm)
            * norm_gain
        ).astype(jnp.bfloat16)
        query_raw = jnp.dot(normed, w_query, preferred_element_type=jnp.float32)
        keyval_raw = jnp.dot(normed, w_keyval, preferred_element_type=jnp.float32)
        joined = collect(
            jnp.concatenate([query_raw, keyval_raw], 1),
            lambda value, bit_index: from_partner(value, "tp", bit_index),
        )
        query_width = own_heads * head_dim
        query_all = jnp.moveaxis(joined[:, :, :query_width], 0, 1).reshape(
            row_count, group_size * own_heads, head_dim
        )
        keyval = jnp.moveaxis(joined[:, :, query_width:], 0, 1).reshape(row_count, 2 * head_dim)
        queries = rotary(query_all, positions).astype(jnp.bfloat16)
        partial_value = block_terms(queries, cache_rows[:, 0], member * block_len, length_rows)
        shared = collect(
            partial_value, lambda value, bit_index: from_partner(value, "tp", bit_index)
        )
        own_queries = lax.dynamic_slice_in_dim(queries, member * own_heads, own_heads, 1)
        pieces = [
            tuple(
                (
                    lax.dynamic_slice_in_dim(
                        member_part[block_index], member * own_heads, own_heads, 1
                    )
                    for member_part in shared
                )
            )
            for block_index in range(group_size)
        ]
        fresh_kv = jnp.concatenate(
            [rotary(keyval[:, None, :head_dim], positions)[:, 0], keyval[:, head_dim:]], -1
        ).astype(jnp.bfloat16)
        for fresh_item in earlier + [fresh_kv]:
            pieces.append(fresh_terms(own_queries, fresh_item))
        attended = combine(pieces).reshape(row_count, own_heads * head_dim).astype(jnp.bfloat16)
        head_terms = jnp.dot(attended, w_out, preferred_element_type=jnp.float32)
        return (
            lax.psum_scatter(head_terms, "tp", scatter_dimension=1, tiled=True).astype(
                jnp.bfloat16
            ),
            fresh_kv,
        )

    first_out, first_fresh = decode(0, own_lengths, key_cache, own_lengths, [])
    move_count = moved_slots.shape[1]
    move_ids = jnp.arange(move_count, dtype=jnp.int32)
    partner = jnp.bitwise_xor(instance, partner_mask)
    slots_self = moved_slots[instance]
    slots_partner = moved_slots[partner, move_ids]
    payload = (key_cache[slots_self], first_fresh[slots_self])
    moving = payload
    for bit_index in range(lax.axis_size("inst").bit_length() - 1):
        received = jax.tree.map(
            lambda part, own: part.astype(own.dtype),
            from_partner(as_sent(moving), "inst", bit_index),
            moving,
        )
        use_swap = partner_mask >> bit_index & 1 == 1
        moving = jax.tree.map(
            lambda their_part, mine_part: jnp.where(
                use_swap.reshape((move_count,) + (1,) * (mine_part.ndim - 1)), their_part, mine_part
            ),
            received,
            moving,
        )
    arrived_rows, arrived_fresh = moving
    cache_next = key_cache.at[slots_self].set(arrived_rows)
    fresh_next = first_fresh.at[slots_self].set(arrived_fresh)
    length_next = own_lengths.at[slots_self].set(lengths[partner * row_count + slots_partner])
    second_out, unused = decode(1, length_next + 1, cache_next, length_next, [fresh_next])
    return (jnp.stack([first_out, second_out]), arrived_rows)


def hand_on(out_ref, arrived_ref, out_final, arrived_final):
    out_final[...] = out_ref[...]
    arrived_final[...] = arrived_ref[...]


def fused_kernel(
    len_ref,
    slot_ref,
    mask_ref,
    x_ref,
    gain_ref,
    wq_hbm,
    wkv_hbm,
    wo_hbm,
    cache_hbm,
    out_ref,
    arrived_ref,
    wq,
    wkv,
    wo,
    cache,
    xg,
    acc,
    square,
    place,
    qs,
    fresh,
    mixed,
    attended,
    leave,
    mid_in,
    mid,
    last_in,
    ask_query,
    ask_fresh,
    asked_query,
    asked_fresh,
    reply,
    replied,
    sib_send,
    sib_recv,
    own,
    first_send,
    first_recv,
    second_send,
    second_recv,
    load_sem,
    gather_send,
    gather_recv,
    move_send,
    move_recv,
    ask_send,
    ask_recv,
    reply_send,
    reply_recv,
    sum_send,
    sum_recv,
):
    tp = lax.axis_index("tp")
    inst = lax.axis_index("inst")
    rows = x_ref.shape[1]
    width = x_ref.shape[2]
    moves = slot_ref.shape[1]
    hd = cache.shape[-1] // 2
    heads = qs.shape[1] // 2
    scale = 1.0 / math.sqrt(hd)

    def remote(src, dst, send, recv, **where):
        return pltpu.make_async_remote_copy(
            src_ref=src,
            dst_ref=dst,
            send_sem=send,
            recv_sem=recv,
            device_id=where,
            device_id_type=pl.DeviceIdType.MESH,
        )

    quarter = rows // 4
    cache_loads = [
        pltpu.make_async_copy(
            cache_hbm.at[pl.ds(n * quarter, quarter)],
            cache.at[pl.ds(n * quarter, quarter)],
            load_sem.at[24 + n],
        )
        for n in range(4)
    ]
    for load in cache_loads:
        load.start()
    weight_loads = []
    out_loads = []
    for i in range(8):
        start = pl.multiple_of((tp ^ i) * width, width)
        weight_loads.append(
            (
                pltpu.make_async_copy(wq_hbm.at[pl.ds(start, width), :], wq.at[i], load_sem.at[i]),
                pltpu.make_async_copy(
                    wkv_hbm.at[pl.ds(start, width), :], wkv.at[i], load_sem.at[8 + i]
                ),
            )
        )
        out_loads.append(
            pltpu.make_async_copy(
                wo_hbm.at[:, pl.ds(start, width)], wo.at[i], load_sem.at[16 + i]
            )
        )

    def load_weights(*order):
        for i in order:
            for load in weight_loads[i]:
                load.start()

    load_weights(0)

    barrier = pltpu.get_barrier_semaphore()
    for i in range(1, 8):
        pl.semaphore_signal(
            barrier, inc=1, device_id={"tp": tp ^ i}, device_id_type=pl.DeviceIdType.MESH
        )
    for i in range(1, 4):
        pl.semaphore_signal(
            barrier, inc=1, device_id={"inst": inst ^ i}, device_id_type=pl.DeviceIdType.MESH
        )
    xg[0] = x_ref[...]
    pl.semaphore_wait(barrier, 10)

    def feature_copy(k, src, dst, to, part=None):
        src_ref = xg.at[src] if part is None else xg.at[src, part]
        dst_ref = xg.at[dst] if part is None else xg.at[dst, part]
        return remote(src_ref, dst_ref, gather_send.at[k], gather_recv.at[k], tp=tp ^ to)

    along_x = [feature_copy(0, 0, 2, 2, 0), feature_copy(1, 0, 2, 2, 1)]
    along_y = [feature_copy(2, 0, 4, 4, 1), feature_copy(3, 0, 4, 4, 0)]
    to_sibling = [feature_copy(6, 0, 1, 1)]
    along_x[0].start()
    along_y[0].start()
    along_x[1].start()
    along_y[1].start()
    to_sibling[0].start()

    for load in cache_loads:
        load.wait()
    load_weights(1, 2, 4)
    move_bits = [(1, 2) if j < moves // 2 else (2, 1) for j in range(moves)]
    first_moves = []
    for j in range(moves):
        leave[j] = cache[slot_ref[inst, j]]
        move = remote(
            leave.at[j], mid_in.at[j], move_send.at[j], move_recv.at[j], inst=inst ^ move_bits[j][0]
        )
        move.start()
        first_moves.append(move)

    @pl.loop(0, rows)
    def _(r):
        level = jnp.full((1, 2 * hd), len_ref[inst * rows + r], jnp.int32)
        place[pl.ds(r, 1), :] = level[:, :hd]

    row_ids = lax.broadcasted_iota(jnp.int32, (rows, hd), 0)
    own_place = place[...]
    next_place = own_place
    for j in range(moves):
        partner = inst ^ mask_ref[j]
        length = len_ref[partner * rows + slot_ref[partner, j]]
        next_place = jnp.where(row_ids == slot_ref[inst, j], length, next_place)
    positions = jnp.concatenate([own_place, next_place + 1], 0).astype(jnp.float32)
    lane = lax.broadcasted_iota(jnp.int32, (1, hd), 1)
    pair_id = jnp.where(lane < hd // 2, lane, lane - hd // 2).astype(jnp.float32)
    frequency = jnp.exp(pair_id * (-2.0 * math.log(rope_base) / hd))
    angles = positions * frequency
    cosine = jnp.cos(angles)
    sine = jnp.sin(angles)
    sine = jnp.where(lane < hd // 2, -sine, sine)

    acc[...] = jnp.zeros_like(acc)
    square[...] = jnp.zeros_like(square)
    q_width = wq.shape[2]

    def project(i):
        for load in weight_loads[i]:
            load.wait()
        wide = xg[i].reshape(2 * rows, width).astype(jnp.float32)
        square[...] += jnp.sum(wide * wide, -1, keepdims=True)
        start = pl.multiple_of((tp ^ i) * width, width)
        gain = gain_ref[pl.ds(start, width)]
        scaled = (wide * gain[None, :]).astype(jnp.bfloat16)

        for c in range(0, q_width, 512):
            cols = slice(c, c + 512)
            acc[:, cols] += jnp.dot(scaled, wq[i, :, cols], preferred_element_type=jnp.float32)

        acc[:, q_width:] += jnp.dot(scaled, wkv[i], preferred_element_type=jnp.float32)

    along_x[0].wait_recv()
    along_y[0].wait_recv()
    across = [feature_copy(4, 2, 6, 4, 0), feature_copy(5, 4, 6, 2, 1)]
    across[0].start()
    across[1].start()
    project(0)
    load_weights(3, 5)
    to_sibling[0].wait_recv()
    project(1)
    load_weights(6, 7)
    along_x[1].wait_recv()
    to_sibling.append(feature_copy(7, 2, 3, 1))
    to_sibling[1].start()
    along_y[1].wait_recv()
    to_sibling.append(feature_copy(8, 4, 5, 1))
    to_sibling[2].start()
    project(2)
    project(4)
    for i in (7, 3, 6, 5):
        out_loads[i].start()
    to_sibling[1].wait_recv()
    project(3)
    to_sibling[2].wait_recv()
    project(5)
    for i in (2, 1, 4, 0):
        out_loads[i].start()
    across[0].wait_recv()
    across[1].wait_recv()
    to_sibling.append(feature_copy(9, 6, 7, 1))
    to_sibling[3].start()
    project(6)
    to_sibling[3].wait_recv()
    project(7)

    factor = lax.rsqrt(square[...] * (1.0 / (8 * width)) + eps_norm)

    def turned(part):
        part = part * factor
        return (part * cosine + pltpu.roll(part, hd // 2, 1) * sine).astype(jnp.bfloat16)

    for h in range(heads):
        rotated = turned(acc[:, h * hd : (h + 1) * hd]).astype(jnp.float32)
        qs[:, h, :] = rotated[:rows]
        qs[:, heads + h, :] = rotated[rows:]
    fresh[:, :hd] = turned(acc[:, q_width : q_width + hd]).astype(jnp.float32)
    fresh[:, hd:] = (acc[:, q_width + hd :] * factor).astype(jnp.bfloat16).astype(jnp.float32)

    slots = [slot_ref[inst, j] for j in range(moves)]
    ask_query[...] = jnp.concatenate([qs[slot, heads:, :] for slot in slots], 0).astype(
        jnp.bfloat16
    )
    for j in range(moves):
        ask_fresh[pl.ds(j, 1), :] = fresh[pl.ds(rows + slots[j], 1), :]
    asks = []
    for i in range(3):
        pair = (
            remote(
                ask_query, asked_query.at[i], ask_send.at[i], ask_recv.at[i], inst=inst ^ (i + 1)
            ),
            remote(
                ask_fresh,
                asked_fresh.at[i],
                ask_send.at[3 + i],
                ask_recv.at[3 + i],
                inst=inst ^ (i + 1),
            ),
        )
        for copy in pair:
            copy.start()
            asks.append(copy)

    def matched(mask, parts):
        return jnp.where(mask == 1, parts[0], jnp.where(mask == 2, parts[1], parts[2]))

    def attend(requests):
        scores = [
            scale
            * lax.dot_general(
                queries.astype(jnp.bfloat16),
                keys,
                (((1,), (1,)), ((), ())),
                preferred_element_type=jnp.float32,
            )
            for queries, keys, values, length, news in requests
        ]
        spots = lax.broadcasted_iota(jnp.int32, scores[0].shape, 1)
        scores = [
            jnp.where(spots < request[3], score, floor_score)
            for score, request in zip(scores, requests)
        ]
        tops = [jnp.max(score, -1, keepdims=True) for score in scores]
        marks = []
        for queries, keys, values, length, news in requests:
            row_marks = []
            for row, allowed in news:
                mark = scale * jnp.sum(queries * row[:, :hd], -1, keepdims=True)
                if allowed is not None:
                    mark = jnp.where(allowed, mark, floor_score)
                row_marks.append(mark)
            marks.append(row_marks)
        weights = [
            jnp.where(spots < request[3], jnp.exp(score - top), 0.0).astype(jnp.bfloat16)
            for score, top, request in zip(scores, tops, requests)
        ]
        mixes = [
            jnp.dot(weight, request[2], preferred_element_type=jnp.float32)
            for weight, request in zip(weights, requests)
        ]
        totals = [jnp.sum(weight.astype(jnp.float32), -1, keepdims=True) for weight in weights]
        answers = []
        for request, top, row_marks, mix, total in zip(requests, tops, marks, mixes, totals):
            overall = reduce(jnp.maximum, row_marks, top)
            share = jnp.exp(top - overall)
            numerator = share * mix
            denominator = share * total
            for (row, allowed), mark in zip(request[4], row_marks):
                share = jnp.exp(mark - overall)
                if allowed is not None:
                    share = jnp.where(allowed, share, 0.0)
                numerator = numerator + share * row[:, hd:]
                denominator = denominator + share
            answers.append(numerator / denominator)
        return answers

    later = lax.broadcasted_iota(jnp.int32, (2 * heads, 1), 0) >= heads
    batch = 16

    def attend_slots(first, last):
        @pl.loop(first, last)
        def _(group):
            ids = [group * batch + u for u in range(batch)]
            answers = attend(
                [
                    (
                        qs[r],
                        cache[r, :, :hd],
                        cache[r, :, hd:],
                        len_ref[inst * rows + r],
                        [(fresh[pl.ds(r, 1), :], None), (fresh[pl.ds(rows + r, 1), :], later)],
                    )
                    for r in ids
                ]
            )
            for r, answer in zip(ids, answers):
                mixed[r] = answer

    groups = rows // batch
    attend_slots(0, groups // 4)

    second_moves = []
    for j in range(moves):
        first_moves[j].wait_recv()
        taken = (mask_ref[j] & move_bits[j][0]) != 0
        mid[j] = jnp.where(taken, mid_in[j], leave[j])
        move = remote(
            mid.at[j],
            last_in.at[j],
            move_send.at[moves + j],
            move_recv.at[moves + j],
            inst=inst ^ move_bits[j][1],
        )
        move.start()
        second_moves.append(move)

    attend_slots(groups // 4, groups // 2)

    for copy in asks:
        copy.wait_recv()
    requests = []
    for j in range(moves):
        slot = slots[j]
        mask = mask_ref[j]
        part = slice(j * heads, (j + 1) * heads)
        queries = matched(mask, [asked_query[i].astype(jnp.float32)[part] for i in range(3)])
        news = matched(mask, [asked_fresh[i, pl.ds(j, 1), :] for i in range(3)])
        requests.append(
            (
                queries,
                cache[slot, :, :hd],
                cache[slot, :, hd:],
                len_ref[inst * rows + slot],
                [(fresh[pl.ds(slot, 1), :], None), (news, None)],
            )
        )
    reply[...] = jnp.concatenate(attend(requests), 0).astype(jnp.bfloat16)
    replies = []
    for i in range(3):
        copy = remote(
            reply, replied.at[i], reply_send.at[i], reply_recv.at[i], inst=inst ^ (i + 1)
        )
        copy.start()
        replies.append(copy)

    attend_slots(groups // 2, groups)

    for copy in replies:
        copy.wait_recv()
    came = [
        matched(
            mask_ref[j],
            [replied[i].astype(jnp.float32)[j * heads : (j + 1) * heads] for i in range(3)],
        )
        for j in range(moves)
    ]
    for h in range(heads):
        cols = slice(h * hd, (h + 1) * hd)
        attended[:rows, cols] = mixed[:, h, :].astype(jnp.bfloat16)
        second = mixed[:, heads + h, :]
        for j in range(moves):
            second = jnp.where(row_ids == slots[j], came[j][h : h + 1], second)
        attended[rows:, cols] = second.astype(jnp.bfloat16)

    tile = 512

    def column_loop(body):
        for c in range(0, width, tile):
            body(slice(c, c + tile))

    def term(i, cols):
        return jnp.dot(attended[...], wo[i, :, cols], preferred_element_type=jnp.float32)

    first_sums = [[None, None], [None, None]]

    def send_first(s, n):
        k = 4 + 2 * s + n
        copy = remote(
            first_send.at[s, n],
            first_recv.at[s, n],
            sum_send.at[k],
            sum_recv.at[k],
            tp=tp ^ (2, 4)[s],
        )
        copy.start()
        first_sums[s][n] = copy

    sibling_sums = {}
    for i in (7, 3, 6, 5, 2, 1, 4, 0):
        k = i // 2
        out_loads[i].wait()
        if i % 2 == 0:
            sibling_sums[k].wait_recv()

        def body(cols):
            chip = term(i, cols)
            if i % 2:
                sib_send[k, :, cols] = chip.astype(jnp.bfloat16)
                return
            chip = chip + sib_recv[k, :, cols].astype(jnp.float32)
            if i == 6:
                first_send[0, 1, :, cols] = chip[:rows].astype(jnp.bfloat16)
                first_send[1, 1, :, cols] = chip[rows:].astype(jnp.bfloat16)
            elif i == 2:
                first_send[0, 0, :, cols] = chip[:rows].astype(jnp.bfloat16)
                own[1, :rows, cols] = chip[rows:]
            elif i == 4:
                own[1, rows:, cols] = chip[:rows]
                first_send[1, 0, :, cols] = chip[rows:].astype(jnp.bfloat16)
            else:
                own[0, :, cols] = chip

        column_loop(body)
        if i % 2:
            copy = remote(
                sib_send.at[k], sib_recv.at[k], sum_send.at[k], sum_recv.at[k], tp=tp ^ 1
            )
            copy.start()
            sibling_sums[k] = copy
        elif i == 6:
            send_first(0, 1)
            send_first(1, 1)
        elif i == 2:
            send_first(0, 0)
        elif i == 4:
            send_first(1, 0)

    second_sums = []
    for s in range(2):
        first_sums[s][1].wait_recv()
        base = own[1, rows:, :] if s == 0 else own[1, :rows, :]
        second_send[s] = (base + first_recv[s, 1].astype(jnp.float32)).astype(jnp.bfloat16)
        copy = remote(
            second_send.at[s],
            second_recv.at[s],
            sum_send.at[8 + s],
            sum_recv.at[8 + s],
            tp=tp ^ (4, 2)[s],
        )
        copy.start()
        second_sums.append(copy)

    for j in range(moves):
        second_moves[j].wait_recv()
        taken = (mask_ref[j] & move_bits[j][1]) != 0
        arrived_ref[j, 0] = jnp.where(taken, last_in[j], mid[j])

    for s in range(2):
        first_sums[s][0].wait_recv()
        second_sums[s].wait_recv()
        part = own[0, s * rows : (s + 1) * rows, :]
        part = part + first_recv[s, 0].astype(jnp.float32)
        out_ref[s] = (part + second_recv[s].astype(jnp.float32)).astype(jnp.bfloat16)

    for copy in (
        along_x
        + along_y
        + across
        + to_sibling
        + first_moves
        + second_moves
        + asks
        + replies
        + list(sibling_sums.values())
        + first_sums[0]
        + first_sums[1]
        + second_sums
    ):
        copy.wait_send()


def fused(
    x_steps, norm_gain, w_query, w_keyval, w_out, key_cache, lengths, moved_slots, partner_mask
):
    steps, rows, width = x_steps.shape
    moves = moved_slots.shape[1]
    block_len, pair_dim = key_cache.shape[2:]
    hd = pair_dim // 2
    q_width = w_query.shape[1]
    heads = q_width // hd
    both = steps * rows
    bf16, f32 = jnp.bfloat16, jnp.float32
    smem = pl.BlockSpec(memory_space=pltpu.SMEM)
    vmem = pl.BlockSpec(memory_space=pltpu.VMEM)
    anywhere = pl.BlockSpec(memory_space=pl.ANY)
    dma = pltpu.SemaphoreType.DMA
    results = pl.pallas_call(
        fused_kernel,
        out_shape=(
            jax.ShapeDtypeStruct((steps, rows, width), bf16),
            jax.ShapeDtypeStruct((moves,) + key_cache.shape[1:], bf16),
        ),
        in_specs=[smem, smem, smem, vmem, vmem, anywhere, anywhere, anywhere, anywhere],
        out_specs=(vmem, vmem),
        scratch_shapes=[
            pltpu.VMEM((8, width, q_width), bf16),
            pltpu.VMEM((8, width, pair_dim), bf16),
            pltpu.VMEM((8, q_width, width), bf16),
            pltpu.VMEM((rows, block_len, pair_dim), bf16),
            pltpu.VMEM((8, steps, rows, width), bf16),
            pltpu.VMEM((both, q_width + pair_dim), f32),
            pltpu.VMEM((both, 1), f32),
            pltpu.VMEM((rows, hd), jnp.int32),
            pltpu.VMEM((rows, 2 * heads, hd), f32),
            pltpu.VMEM((both, pair_dim), f32),
            pltpu.VMEM((rows, 2 * heads, hd), f32),
            pltpu.VMEM((both, q_width), bf16),
            pltpu.VMEM((moves, block_len, pair_dim), bf16),
            pltpu.VMEM((moves, block_len, pair_dim), bf16),
            pltpu.VMEM((moves, block_len, pair_dim), bf16),
            pltpu.VMEM((moves, block_len, pair_dim), bf16),
            pltpu.VMEM((moves * heads, hd), bf16),
            pltpu.VMEM((moves, pair_dim), f32),
            pltpu.VMEM((3, moves * heads, hd), bf16),
            pltpu.VMEM((3, moves, pair_dim), f32),
            pltpu.VMEM((moves * heads, hd), bf16),
            pltpu.VMEM((3, moves * heads, hd), bf16),
            pltpu.VMEM((4, both, width), bf16),
            pltpu.VMEM((4, both, width), bf16),
            pltpu.VMEM((2, both, width), f32),
            pltpu.VMEM((2, 2, rows, width), bf16),
            pltpu.VMEM((2, 2, rows, width), bf16),
            pltpu.VMEM((2, rows, width), bf16),
            pltpu.VMEM((2, rows, width), bf16),
            dma((28,)),
            dma((10,)),
            dma((10,)),
            dma((2 * moves,)),
            dma((2 * moves,)),
            dma((6,)),
            dma((6,)),
            dma((3,)),
            dma((3,)),
            dma((10,)),
            dma((10,)),
        ],
        compiler_params=pltpu.CompilerParams(
            collective_id=0, has_side_effects=True, vmem_limit_bytes=60 * 2**20
        ),
        cost_estimate=pl.CostEstimate(
            flops=2 * both * w_query.shape[0] * (2 * q_width + pair_dim),
            bytes_accessed=2 * (w_query.size + w_keyval.size + w_out.size + key_cache.size),
            transcendentals=0,
        ),
    )(
        lengths,
        moved_slots,
        partner_mask,
        x_steps,
        norm_gain,
        w_query,
        w_keyval,
        w_out,
        key_cache.reshape(rows, block_len, pair_dim),
    )
    return pl.pallas_call(
        hand_on,
        out_shape=tuple(jax.ShapeDtypeStruct(part.shape, part.dtype) for part in results),
        in_specs=[vmem, vmem],
        out_specs=(vmem, vmem),
    )(*results)


def solution(mesh):
    placed = (
        P(None, "inst", "tp"),
        P(),
        P(None, "tp"),
        P(None, "tp"),
        P("tp", None),
        P("inst", "tp", None, None),
        P(),
        P(),
        P(),
    )
    body = fused if mesh.shape["tp"] == KVH and mesh.shape["inst"] == 4 else shards
    return jax.shard_map(
        body,
        mesh=mesh,
        in_specs=placed,
        out_specs=(P(None, "inst", "tp"), P("inst", "tp", None, None)),
        check_vma=False,
    )
```

```python
from functools import reduce
import math

import jax
import jax.numpy as jnp
from jax import lax
from jax.experimental import pallas as pl
from jax.experimental.pallas import tpu as pltpu
from jax.sharding import PartitionSpec as P

KVH = 8


eps_norm = 1e-05
rope_base = 500000.0
floor_score = -1e30


def from_partner(block, axis, bit):
    count = lax.axis_size(axis)
    route = []
    for low in range(count):
        high = low | 1 << bit
        if high != low and high < count:
            route += [(low, high), (high, low)]
    return lax.ppermute(block, axis, route)


def as_sent(value):

    def short(part):
        return part.astype(jnp.bfloat16) if part.dtype == jnp.float32 else part

    return jax.tree.map(short, value)


def rotary(vectors, positions):
    half_dim = vectors.shape[-1] // 2
    frequency = rope_base ** (-(jnp.arange(half_dim, dtype=jnp.float32) * 2.0) / vectors.shape[-1])
    angles = positions.astype(jnp.float32)[..., None] * frequency
    cosine = jnp.cos(angles)[..., None, :]
    sine_part = jnp.sin(angles)[..., None, :]
    first_half = vectors[..., :half_dim]
    second_half = vectors[..., half_dim:]
    return jnp.concatenate(
        [
            first_half * cosine - second_half * sine_part,
            second_half * cosine + first_half * sine_part,
        ],
        -1,
    )


def block_terms(queries, block, start, length_rows):
    head_dim = queries.shape[-1]
    block_len = block.shape[1]
    scores = jnp.einsum(
        "rhd,rtd->rht", queries, block[..., :head_dim], preferred_element_type=jnp.float32
    ) / math.sqrt(head_dim)
    places = start + jnp.arange(block_len, dtype=jnp.int32)
    visible = (places[None, :] < length_rows[:, None])[:, None, :]
    scores = jnp.where(visible, scores, floor_score)
    block_max = jnp.max(scores, -1)
    weights = jnp.where(visible, jnp.exp(scores - block_max[..., None]), 0.0).astype(jnp.bfloat16)
    block_sum = jnp.sum(weights.astype(jnp.float32), -1)
    block_mix = jnp.einsum(
        "rht,rtd->rhd", weights, block[..., head_dim:], preferred_element_type=jnp.float32
    )
    return (block_max, block_sum, block_mix)


def fresh_terms(queries, fresh_kv):
    head_dim = queries.shape[-1]
    score = jnp.einsum(
        "rhd,rd->rh", queries, fresh_kv[:, :head_dim], preferred_element_type=jnp.float32
    ) / math.sqrt(head_dim)
    block_mix = jnp.broadcast_to(fresh_kv[:, None, head_dim:].astype(jnp.float32), queries.shape)
    return (score, jnp.ones_like(score), block_mix)


def combine(pieces):
    overall_max = reduce(jnp.maximum, [piece[0] for piece in pieces])
    numerator = reduce(
        jnp.add, [jnp.exp(piece[0] - overall_max)[..., None] * piece[2] for piece in pieces]
    )
    denominator = reduce(jnp.add, [jnp.exp(piece[0] - overall_max) * piece[1] for piece in pieces])
    return numerator / denominator[..., None]


def shards(
    x_steps, norm_gain, w_query, w_keyval, w_out, key_cache, lengths, moved_slots, partner_mask
):
    row_count = x_steps.shape[1]
    head_dim = key_cache.shape[-1] // 2
    block_len = key_cache.shape[2]
    group_size = lax.axis_size("tp") // KVH
    group_bits = group_size.bit_length() - 1
    member = lax.axis_index("tp") % group_size
    instance = lax.axis_index("inst")
    own_heads = w_query.shape[1] // head_dim
    own_lengths = lax.dynamic_slice_in_dim(lengths, instance * row_count, row_count)

    def collect(value, swapper):
        stacked = jax.tree.map(lambda leaf: leaf[None], value)
        for bit_index in range(group_bits):
            received = swapper(stacked, bit_index)
            low_side = member >> bit_index & 1 == 0
            stacked = jax.tree.map(
                lambda mine_part, their_part: jnp.where(
                    low_side,
                    jnp.concatenate([mine_part, their_part], 0),
                    jnp.concatenate([their_part, mine_part], 0),
                ),
                stacked,
                received,
            )
        return stacked

    def decode(step_index, positions, cache_rows, length_rows, earlier):
        gathered = lax.all_gather(x_steps[step_index], "tp", axis=1, tiled=True)
        widened = gathered.astype(jnp.float32)
        normed = (
            widened
            * lax.rsqrt(jnp.mean(widened * widened, -1, keepdims=True) + eps_norm)
            * norm_gain
        ).astype(jnp.bfloat16)
        query_raw = jnp.dot(normed, w_query, preferred_element_type=jnp.float32)
        keyval_raw = jnp.dot(normed, w_keyval, preferred_element_type=jnp.float32)
        joined = collect(
            jnp.concatenate([query_raw, keyval_raw], 1),
            lambda value, bit_index: from_partner(value, "tp", bit_index),
        )
        query_width = own_heads * head_dim
        query_all = jnp.moveaxis(joined[:, :, :query_width], 0, 1).reshape(
            row_count, group_size * own_heads, head_dim
        )
        keyval = jnp.moveaxis(joined[:, :, query_width:], 0, 1).reshape(row_count, 2 * head_dim)
        queries = rotary(query_all, positions).astype(jnp.bfloat16)
        partial_value = block_terms(queries, cache_rows[:, 0], member * block_len, length_rows)
        shared = collect(
            partial_value, lambda value, bit_index: from_partner(value, "tp", bit_index)
        )
        own_queries = lax.dynamic_slice_in_dim(queries, member * own_heads, own_heads, 1)
        pieces = [
            tuple(
                (
                    lax.dynamic_slice_in_dim(
                        member_part[block_index], member * own_heads, own_heads, 1
                    )
                    for member_part in shared
                )
            )
            for block_index in range(group_size)
        ]
        fresh_kv = jnp.concatenate(
            [rotary(keyval[:, None, :head_dim], positions)[:, 0], keyval[:, head_dim:]], -1
        ).astype(jnp.bfloat16)
        for fresh_item in earlier + [fresh_kv]:
            pieces.append(fresh_terms(own_queries, fresh_item))
        attended = combine(pieces).reshape(row_count, own_heads * head_dim).astype(jnp.bfloat16)
        head_terms = jnp.dot(attended, w_out, preferred_element_type=jnp.float32)
        return (
            lax.psum_scatter(head_terms, "tp", scatter_dimension=1, tiled=True).astype(
                jnp.bfloat16
            ),
            fresh_kv,
        )

    first_out, first_fresh = decode(0, own_lengths, key_cache, own_lengths, [])
    move_count = moved_slots.shape[1]
    move_ids = jnp.arange(move_count, dtype=jnp.int32)
    partner = jnp.bitwise_xor(instance, partner_mask)
    slots_self = moved_slots[instance]
    slots_partner = moved_slots[partner, move_ids]
    payload = (key_cache[slots_self], first_fresh[slots_self])
    moving = payload
    for bit_index in range(lax.axis_size("inst").bit_length() - 1):
        received = jax.tree.map(
            lambda part, own: part.astype(own.dtype),
            from_partner(as_sent(moving), "inst", bit_index),
            moving,
        )
        use_swap = partner_mask >> bit_index & 1 == 1
        moving = jax.tree.map(
            lambda their_part, mine_part: jnp.where(
                use_swap.reshape((move_count,) + (1,) * (mine_part.ndim - 1)), their_part, mine_part
            ),
            received,
            moving,
        )
    arrived_rows, arrived_fresh = moving
    cache_next = key_cache.at[slots_self].set(arrived_rows)
    fresh_next = first_fresh.at[slots_self].set(arrived_fresh)
    length_next = own_lengths.at[slots_self].set(lengths[partner * row_count + slots_partner])
    second_out, unused = decode(1, length_next + 1, cache_next, length_next, [fresh_next])
    return (jnp.stack([first_out, second_out]), arrived_rows)


def hand_on(out_ref, arrived_ref, out_final, arrived_final):
    out_final[...] = out_ref[...]
    arrived_final[...] = arrived_ref[...]


def fused_kernel(
    len_ref,
    slot_ref,
    mask_ref,
    x_ref,
    gain_ref,
    wq_hbm,
    wkv_hbm,
    wo_hbm,
    cache_hbm,
    out_ref,
    arrived_ref,
    wq,
    wkv,
    wo,
    cache,
    xg,
    acc,
    square,
    place,
    qs,
    fresh,
    mixed,
    attended,
    leave,
    mid_in,
    mid,
    last_in,
    ask_query,
    ask_fresh,
    asked_query,
    asked_fresh,
    reply,
    replied,
    sib_send,
    sib_recv,
    own,
    first_send,
    first_recv,
    second_send,
    second_recv,
    load_sem,
    gather_send,
    gather_recv,
    move_send,
    move_recv,
    ask_send,
    ask_recv,
    reply_send,
    reply_recv,
    sum_send,
    sum_recv,
):
    tp = lax.axis_index("tp")
    inst = lax.axis_index("inst")
    rows = x_ref.shape[1]
    width = x_ref.shape[2]
    moves = slot_ref.shape[1]
    hd = cache.shape[-1] // 2
    heads = qs.shape[1] // 2
    scale = 1.0 / math.sqrt(hd)

    def remote(src, dst, send, recv, **where):
        return pltpu.make_async_remote_copy(
            src_ref=src,
            dst_ref=dst,
            send_sem=send,
            recv_sem=recv,
            device_id=where,
            device_id_type=pl.DeviceIdType.MESH,
        )

    quarter = rows // 4
    cache_loads = [
        pltpu.make_async_copy(
            cache_hbm.at[pl.ds(n * quarter, quarter)],
            cache.at[pl.ds(n * quarter, quarter)],
            load_sem.at[24 + n],
        )
        for n in range(4)
    ]
    for load in cache_loads:
        load.start()
    weight_loads = []
    out_loads = []
    for i in range(8):
        start = pl.multiple_of((tp ^ i) * width, width)
        weight_loads.append(
            (
                pltpu.make_async_copy(wq_hbm.at[pl.ds(start, width), :], wq.at[i], load_sem.at[i]),
                pltpu.make_async_copy(
                    wkv_hbm.at[pl.ds(start, width), :], wkv.at[i], load_sem.at[8 + i]
                ),
            )
        )
        out_loads.append(
            pltpu.make_async_copy(
                wo_hbm.at[:, pl.ds(start, width)], wo.at[i], load_sem.at[16 + i]
            )
        )

    def load_weights(*order):
        for i in order:
            for load in weight_loads[i]:
                load.start()

    load_weights(0)

    barrier = pltpu.get_barrier_semaphore()
    for i in range(1, 8):
        pl.semaphore_signal(
            barrier, inc=1, device_id={"tp": tp ^ i}, device_id_type=pl.DeviceIdType.MESH
        )
    for i in range(1, 4):
        pl.semaphore_signal(
            barrier, inc=1, device_id={"inst": inst ^ i}, device_id_type=pl.DeviceIdType.MESH
        )
    xg[0] = x_ref[...]
    pl.semaphore_wait(barrier, 10)

    def feature_copy(k, src, dst, to, part=None):
        src_ref = xg.at[src] if part is None else xg.at[src, part]
        dst_ref = xg.at[dst] if part is None else xg.at[dst, part]
        return remote(src_ref, dst_ref, gather_send.at[k], gather_recv.at[k], tp=tp ^ to)

    along_x = [feature_copy(0, 0, 2, 2, 0), feature_copy(1, 0, 2, 2, 1)]
    along_y = [feature_copy(2, 0, 4, 4, 1), feature_copy(3, 0, 4, 4, 0)]
    to_sibling = [feature_copy(6, 0, 1, 1)]
    along_x[0].start()
    along_y[0].start()
    along_x[1].start()
    along_y[1].start()
    to_sibling[0].start()

    for load in cache_loads:
        load.wait()
    load_weights(1, 2, 4)
    move_bits = [(1, 2) if j < moves // 2 else (2, 1) for j in range(moves)]
    first_moves = []
    for j in range(moves):
        leave[j] = cache[slot_ref[inst, j]]
        move = remote(
            leave.at[j], mid_in.at[j], move_send.at[j], move_recv.at[j], inst=inst ^ move_bits[j][0]
        )
        move.start()
        first_moves.append(move)

    @pl.loop(0, rows)
    def _(r):
        level = jnp.full((1, 2 * hd), len_ref[inst * rows + r], jnp.int32)
        place[pl.ds(r, 1), :] = level[:, :hd]

    row_ids = lax.broadcasted_iota(jnp.int32, (rows, hd), 0)
    own_place = place[...]
    next_place = own_place
    for j in range(moves):
        partner = inst ^ mask_ref[j]
        length = len_ref[partner * rows + slot_ref[partner, j]]
        next_place = jnp.where(row_ids == slot_ref[inst, j], length, next_place)
    positions = jnp.concatenate([own_place, next_place + 1], 0).astype(jnp.float32)
    lane = lax.broadcasted_iota(jnp.int32, (1, hd), 1)
    pair_id = jnp.where(lane < hd // 2, lane, lane - hd // 2).astype(jnp.float32)
    frequency = jnp.exp(pair_id * (-2.0 * math.log(rope_base) / hd))
    angles = positions * frequency
    cosine = jnp.cos(angles)
    sine = jnp.sin(angles)
    sine = jnp.where(lane < hd // 2, -sine, sine)

    acc[...] = jnp.zeros_like(acc)
    square[...] = jnp.zeros_like(square)
    q_width = wq.shape[2]

    def project(i):
        for load in weight_loads[i]:
            load.wait()
        wide = xg[i].reshape(2 * rows, width).astype(jnp.float32)
        square[...] += jnp.sum(wide * wide, -1, keepdims=True)
        start = pl.multiple_of((tp ^ i) * width, width)
        gain = gain_ref[pl.ds(start, width)]
        scaled = (wide * gain[None, :]).astype(jnp.bfloat16)

        for c in range(0, q_width, 512):
            cols = slice(c, c + 512)
            acc[:, cols] += jnp.dot(scaled, wq[i, :, cols], preferred_element_type=jnp.float32)

        acc[:, q_width:] += jnp.dot(scaled, wkv[i], preferred_element_type=jnp.float32)

    along_x[0].wait_recv()
    along_y[0].wait_recv()
    across = [feature_copy(4, 2, 6, 4, 0), feature_copy(5, 4, 6, 2, 1)]
    across[0].start()
    across[1].start()
    project(0)
    load_weights(3, 5)
    to_sibling[0].wait_recv()
    project(1)
    load_weights(6, 7)
    along_x[1].wait_recv()
    to_sibling.append(feature_copy(7, 2, 3, 1))
    to_sibling[1].start()
    along_y[1].wait_recv()
    to_sibling.append(feature_copy(8, 4, 5, 1))
    to_sibling[2].start()
    project(2)
    project(4)
    for i in (7, 3, 6, 5):
        out_loads[i].start()
    to_sibling[1].wait_recv()
    project(3)
    to_sibling[2].wait_recv()
    project(5)
    for i in (2, 1, 4, 0):
        out_loads[i].start()
    across[0].wait_recv()
    across[1].wait_recv()
    to_sibling.append(feature_copy(9, 6, 7, 1))
    to_sibling[3].start()
    project(6)
    to_sibling[3].wait_recv()
    project(7)

    factor = lax.rsqrt(square[...] * (1.0 / (8 * width)) + eps_norm)

    def turned(part):
        part = part * factor
        return (part * cosine + pltpu.roll(part, hd // 2, 1) * sine).astype(jnp.bfloat16)

    for h in range(heads):
        rotated = turned(acc[:, h * hd : (h + 1) * hd]).astype(jnp.float32)
        qs[:, h, :] = rotated[:rows]
        qs[:, heads + h, :] = rotated[rows:]
    fresh[:, :hd] = turned(acc[:, q_width : q_width + hd]).astype(jnp.float32)
    fresh[:, hd:] = (acc[:, q_width + hd :] * factor).astype(jnp.bfloat16).astype(jnp.float32)

    slots = [slot_ref[inst, j] for j in range(moves)]
    ask_query[...] = jnp.concatenate([qs[slot, heads:, :] for slot in slots], 0).astype(
        jnp.bfloat16
    )
    for j in range(moves):
        ask_fresh[pl.ds(j, 1), :] = fresh[pl.ds(rows + slots[j], 1), :]
    asks = []
    for i in range(3):
        pair = (
            remote(
                ask_query, asked_query.at[i], ask_send.at[i], ask_recv.at[i], inst=inst ^ (i + 1)
            ),
            remote(
                ask_fresh,
                asked_fresh.at[i],
                ask_send.at[3 + i],
                ask_recv.at[3 + i],
                inst=inst ^ (i + 1),
            ),
        )
        for copy in pair:
            copy.start()
            asks.append(copy)

    def matched(mask, parts):
        return jnp.where(mask == 1, parts[0], jnp.where(mask == 2, parts[1], parts[2]))

    def attend(requests):
        scores = [
            scale
            * lax.dot_general(
                queries.astype(jnp.bfloat16),
                keys,
                (((1,), (1,)), ((), ())),
                preferred_element_type=jnp.float32,
            )
            for queries, keys, values, length, news in requests
        ]
        spots = lax.broadcasted_iota(jnp.int32, scores[0].shape, 1)
        scores = [
            jnp.where(spots < request[3], score, floor_score)
            for score, request in zip(scores, requests)
        ]
        tops = [jnp.max(score, -1, keepdims=True) for score in scores]
        marks = []
        for queries, keys, values, length, news in requests:
            row_marks = []
            for row, allowed in news:
                mark = scale * jnp.sum(queries * row[:, :hd], -1, keepdims=True)
                if allowed is not None:
                    mark = jnp.where(allowed, mark, floor_score)
                row_marks.append(mark)
            marks.append(row_marks)
        weights = [
            jnp.where(spots < request[3], jnp.exp(score - top), 0.0).astype(jnp.bfloat16)
            for score, top, request in zip(scores, tops, requests)
        ]
        mixes = [
            jnp.dot(weight, request[2], preferred_element_type=jnp.float32)
            for weight, request in zip(weights, requests)
        ]
        totals = [jnp.sum(weight.astype(jnp.float32), -1, keepdims=True) for weight in weights]
        answers = []
        for request, top, row_marks, mix, total in zip(requests, tops, marks, mixes, totals):
            overall = reduce(jnp.maximum, row_marks, top)
            share = jnp.exp(top - overall)
            numerator = share * mix
            denominator = share * total
            for (row, allowed), mark in zip(request[4], row_marks):
                share = jnp.exp(mark - overall)
                if allowed is not None:
                    share = jnp.where(allowed, share, 0.0)
                numerator = numerator + share * row[:, hd:]
                denominator = denominator + share
            answers.append(numerator / denominator)
        return answers

    later = lax.broadcasted_iota(jnp.int32, (2 * heads, 1), 0) >= heads
    batch = 16

    def attend_slots(first, last):
        @pl.loop(first, last)
        def _(group):
            ids = [group * batch + u for u in range(batch)]
            answers = attend(
                [
                    (
                        qs[r],
                        cache[r, :, :hd],
                        cache[r, :, hd:],
                        len_ref[inst * rows + r],
                        [(fresh[pl.ds(r, 1), :], None), (fresh[pl.ds(rows + r, 1), :], later)],
                    )
                    for r in ids
                ]
            )
            for r, answer in zip(ids, answers):
                mixed[r] = answer

    groups = rows // batch
    attend_slots(0, groups // 4)

    attend_slots(groups // 4, groups // 2)

    for copy in asks:
        copy.wait_recv()
    requests = []
    for j in range(moves):
        slot = slots[j]
        mask = mask_ref[j]
        part = slice(j * heads, (j + 1) * heads)
        queries = matched(mask, [asked_query[i].astype(jnp.float32)[part] for i in range(3)])
        news = matched(mask, [asked_fresh[i, pl.ds(j, 1), :] for i in range(3)])
        requests.append(
            (
                queries,
                cache[slot, :, :hd],
                cache[slot, :, hd:],
                len_ref[inst * rows + slot],
                [(fresh[pl.ds(slot, 1), :], None), (news, None)],
            )
        )
    reply[...] = jnp.concatenate(attend(requests), 0).astype(jnp.bfloat16)
    replies = []
    for i in range(3):
        copy = remote(
            reply, replied.at[i], reply_send.at[i], reply_recv.at[i], inst=inst ^ (i + 1)
        )
        copy.start()
        replies.append(copy)

    second_moves = []
    for j in range(moves):
        first_moves[j].wait_recv()
        taken = (mask_ref[j] & move_bits[j][0]) != 0
        mid[j] = jnp.where(taken, mid_in[j], leave[j])
        move = remote(
            mid.at[j],
            last_in.at[j],
            move_send.at[moves + j],
            move_recv.at[moves + j],
            inst=inst ^ move_bits[j][1],
        )
        move.start()
        second_moves.append(move)

    attend_slots(groups // 2, groups)

    for copy in replies:
        copy.wait_recv()
    came = [
        matched(
            mask_ref[j],
            [replied[i].astype(jnp.float32)[j * heads : (j + 1) * heads] for i in range(3)],
        )
        for j in range(moves)
    ]
    for h in range(heads):
        cols = slice(h * hd, (h + 1) * hd)
        attended[:rows, cols] = mixed[:, h, :].astype(jnp.bfloat16)
        second = mixed[:, heads + h, :]
        for j in range(moves):
            second = jnp.where(row_ids == slots[j], came[j][h : h + 1], second)
        attended[rows:, cols] = second.astype(jnp.bfloat16)

    tile = 512

    def column_loop(body):
        for c in range(0, width, tile):
            body(slice(c, c + tile))

    def term(i, cols):
        return jnp.dot(attended[...], wo[i, :, cols], preferred_element_type=jnp.float32)

    first_sums = [[None, None], [None, None]]

    def send_first(s, n):
        k = 4 + 2 * s + n
        copy = remote(
            first_send.at[s, n],
            first_recv.at[s, n],
            sum_send.at[k],
            sum_recv.at[k],
            tp=tp ^ (2, 4)[s],
        )
        copy.start()
        first_sums[s][n] = copy

    sibling_sums = {}
    for i in (7, 3, 6, 5, 2, 1, 4, 0):
        k = i // 2
        out_loads[i].wait()
        if i % 2 == 0:
            sibling_sums[k].wait_recv()

        def body(cols):
            chip = term(i, cols)
            if i % 2:
                sib_send[k, :, cols] = chip.astype(jnp.bfloat16)
                return
            chip = chip + sib_recv[k, :, cols].astype(jnp.float32)
            if i == 6:
                first_send[0, 1, :, cols] = chip[:rows].astype(jnp.bfloat16)
                first_send[1, 1, :, cols] = chip[rows:].astype(jnp.bfloat16)
            elif i == 2:
                first_send[0, 0, :, cols] = chip[:rows].astype(jnp.bfloat16)
                own[1, :rows, cols] = chip[rows:]
            elif i == 4:
                own[1, rows:, cols] = chip[:rows]
                first_send[1, 0, :, cols] = chip[rows:].astype(jnp.bfloat16)
            else:
                own[0, :, cols] = chip

        column_loop(body)
        if i % 2:
            copy = remote(
                sib_send.at[k], sib_recv.at[k], sum_send.at[k], sum_recv.at[k], tp=tp ^ 1
            )
            copy.start()
            sibling_sums[k] = copy
        elif i == 6:
            send_first(0, 1)
            send_first(1, 1)
        elif i == 2:
            send_first(0, 0)
        elif i == 4:
            send_first(1, 0)

    second_sums = []
    for s in range(2):
        first_sums[s][1].wait_recv()
        base = own[1, rows:, :] if s == 0 else own[1, :rows, :]
        second_send[s] = (base + first_recv[s, 1].astype(jnp.float32)).astype(jnp.bfloat16)
        copy = remote(
            second_send.at[s],
            second_recv.at[s],
            sum_send.at[8 + s],
            sum_recv.at[8 + s],
            tp=tp ^ (4, 2)[s],
        )
        copy.start()
        second_sums.append(copy)

    for j in range(moves):
        second_moves[j].wait_recv()
        taken = (mask_ref[j] & move_bits[j][1]) != 0
        arrived_ref[j, 0] = jnp.where(taken, last_in[j], mid[j])

    for s in range(2):
        first_sums[s][0].wait_recv()
        second_sums[s].wait_recv()
        part = own[0, s * rows : (s + 1) * rows, :]
        part = part + first_recv[s, 0].astype(jnp.float32)
        out_ref[s] = (part + second_recv[s].astype(jnp.float32)).astype(jnp.bfloat16)

    for copy in (
        along_x
        + along_y
        + across
        + to_sibling
        + first_moves
        + second_moves
        + asks
        + replies
        + list(sibling_sums.values())
        + first_sums[0]
        + first_sums[1]
        + second_sums
    ):
        copy.wait_send()


def fused(
    x_steps, norm_gain, w_query, w_keyval, w_out, key_cache, lengths, moved_slots, partner_mask
):
    steps, rows, width = x_steps.shape
    moves = moved_slots.shape[1]
    block_len, pair_dim = key_cache.shape[2:]
    hd = pair_dim // 2
    q_width = w_query.shape[1]
    heads = q_width // hd
    both = steps * rows
    bf16, f32 = jnp.bfloat16, jnp.float32
    smem = pl.BlockSpec(memory_space=pltpu.SMEM)
    vmem = pl.BlockSpec(memory_space=pltpu.VMEM)
    anywhere = pl.BlockSpec(memory_space=pl.ANY)
    dma = pltpu.SemaphoreType.DMA
    results = pl.pallas_call(
        fused_kernel,
        out_shape=(
            jax.ShapeDtypeStruct((steps, rows, width), bf16),
            jax.ShapeDtypeStruct((moves,) + key_cache.shape[1:], bf16),
        ),
        in_specs=[smem, smem, smem, vmem, vmem, anywhere, anywhere, anywhere, anywhere],
        out_specs=(vmem, vmem),
        scratch_shapes=[
            pltpu.VMEM((8, width, q_width), bf16),
            pltpu.VMEM((8, width, pair_dim), bf16),
            pltpu.VMEM((8, q_width, width), bf16),
            pltpu.VMEM((rows, block_len, pair_dim), bf16),
            pltpu.VMEM((8, steps, rows, width), bf16),
            pltpu.VMEM((both, q_width + pair_dim), f32),
            pltpu.VMEM((both, 1), f32),
            pltpu.VMEM((rows, hd), jnp.int32),
            pltpu.VMEM((rows, 2 * heads, hd), f32),
            pltpu.VMEM((both, pair_dim), f32),
            pltpu.VMEM((rows, 2 * heads, hd), f32),
            pltpu.VMEM((both, q_width), bf16),
            pltpu.VMEM((moves, block_len, pair_dim), bf16),
            pltpu.VMEM((moves, block_len, pair_dim), bf16),
            pltpu.VMEM((moves, block_len, pair_dim), bf16),
            pltpu.VMEM((moves, block_len, pair_dim), bf16),
            pltpu.VMEM((moves * heads, hd), bf16),
            pltpu.VMEM((moves, pair_dim), f32),
            pltpu.VMEM((3, moves * heads, hd), bf16),
            pltpu.VMEM((3, moves, pair_dim), f32),
            pltpu.VMEM((moves * heads, hd), bf16),
            pltpu.VMEM((3, moves * heads, hd), bf16),
            pltpu.VMEM((4, both, width), bf16),
            pltpu.VMEM((4, both, width), bf16),
            pltpu.VMEM((2, both, width), f32),
            pltpu.VMEM((2, 2, rows, width), bf16),
            pltpu.VMEM((2, 2, rows, width), bf16),
            pltpu.VMEM((2, rows, width), bf16),
            pltpu.VMEM((2, rows, width), bf16),
            dma((28,)),
            dma((10,)),
            dma((10,)),
            dma((2 * moves,)),
            dma((2 * moves,)),
            dma((6,)),
            dma((6,)),
            dma((3,)),
            dma((3,)),
            dma((10,)),
            dma((10,)),
        ],
        compiler_params=pltpu.CompilerParams(
            collective_id=0, has_side_effects=True, vmem_limit_bytes=60 * 2**20
        ),
        cost_estimate=pl.CostEstimate(
            flops=2 * both * w_query.shape[0] * (2 * q_width + pair_dim),
            bytes_accessed=2 * (w_query.size + w_keyval.size + w_out.size + key_cache.size),
            transcendentals=0,
        ),
    )(
        lengths,
        moved_slots,
        partner_mask,
        x_steps,
        norm_gain,
        w_query,
        w_keyval,
        w_out,
        key_cache.reshape(rows, block_len, pair_dim),
    )
    return pl.pallas_call(
        hand_on,
        out_shape=tuple(jax.ShapeDtypeStruct(part.shape, part.dtype) for part in results),
        in_specs=[vmem, vmem],
        out_specs=(vmem, vmem),
    )(*results)


def solution(mesh):
    placed = (
        P(None, "inst", "tp"),
        P(),
        P(None, "tp"),
        P(None, "tp"),
        P("tp", None),
        P("inst", "tp", None, None),
        P(),
        P(),
        P(),
    )
    body = fused if mesh.shape["tp"] == KVH and mesh.shape["inst"] == 4 else shards
    return jax.shard_map(
        body,
        mesh=mesh,
        in_specs=placed,
        out_specs=(P(None, "inst", "tp"), P("inst", "tp", None, None)),
        check_vma=False,
    )
```

```python
from functools import reduce
import math

import jax
import jax.numpy as jnp
from jax import lax
from jax.experimental import pallas as pl
from jax.experimental.pallas import tpu as pltpu
from jax.sharding import PartitionSpec as P

KVH = 8


eps_norm = 1e-05
rope_base = 500000.0
floor_score = -1e30


def from_partner(block, axis, bit):
    count = lax.axis_size(axis)
    route = []
    for low in range(count):
        high = low | 1 << bit
        if high != low and high < count:
            route += [(low, high), (high, low)]
    return lax.ppermute(block, axis, route)


def as_sent(value):

    def short(part):
        return part.astype(jnp.bfloat16) if part.dtype == jnp.float32 else part

    return jax.tree.map(short, value)


def rotary(vectors, positions):
    half_dim = vectors.shape[-1] // 2
    frequency = rope_base ** (-(jnp.arange(half_dim, dtype=jnp.float32) * 2.0) / vectors.shape[-1])
    angles = positions.astype(jnp.float32)[..., None] * frequency
    cosine = jnp.cos(angles)[..., None, :]
    sine_part = jnp.sin(angles)[..., None, :]
    first_half = vectors[..., :half_dim]
    second_half = vectors[..., half_dim:]
    return jnp.concatenate(
        [
            first_half * cosine - second_half * sine_part,
            second_half * cosine + first_half * sine_part,
        ],
        -1,
    )


def block_terms(queries, block, start, length_rows):
    head_dim = queries.shape[-1]
    block_len = block.shape[1]
    scores = jnp.einsum(
        "rhd,rtd->rht", queries, block[..., :head_dim], preferred_element_type=jnp.float32
    ) / math.sqrt(head_dim)
    places = start + jnp.arange(block_len, dtype=jnp.int32)
    visible = (places[None, :] < length_rows[:, None])[:, None, :]
    scores = jnp.where(visible, scores, floor_score)
    block_max = jnp.max(scores, -1)
    weights = jnp.where(visible, jnp.exp(scores - block_max[..., None]), 0.0).astype(jnp.bfloat16)
    block_sum = jnp.sum(weights.astype(jnp.float32), -1)
    block_mix = jnp.einsum(
        "rht,rtd->rhd", weights, block[..., head_dim:], preferred_element_type=jnp.float32
    )
    return (block_max, block_sum, block_mix)


def fresh_terms(queries, fresh_kv):
    head_dim = queries.shape[-1]
    score = jnp.einsum(
        "rhd,rd->rh", queries, fresh_kv[:, :head_dim], preferred_element_type=jnp.float32
    ) / math.sqrt(head_dim)
    block_mix = jnp.broadcast_to(fresh_kv[:, None, head_dim:].astype(jnp.float32), queries.shape)
    return (score, jnp.ones_like(score), block_mix)


def combine(pieces):
    overall_max = reduce(jnp.maximum, [piece[0] for piece in pieces])
    numerator = reduce(
        jnp.add, [jnp.exp(piece[0] - overall_max)[..., None] * piece[2] for piece in pieces]
    )
    denominator = reduce(jnp.add, [jnp.exp(piece[0] - overall_max) * piece[1] for piece in pieces])
    return numerator / denominator[..., None]


def shards(
    x_steps, norm_gain, w_query, w_keyval, w_out, key_cache, lengths, moved_slots, partner_mask
):
    row_count = x_steps.shape[1]
    head_dim = key_cache.shape[-1] // 2
    block_len = key_cache.shape[2]
    group_size = lax.axis_size("tp") // KVH
    group_bits = group_size.bit_length() - 1
    member = lax.axis_index("tp") % group_size
    instance = lax.axis_index("inst")
    own_heads = w_query.shape[1] // head_dim
    own_lengths = lax.dynamic_slice_in_dim(lengths, instance * row_count, row_count)

    def collect(value, swapper):
        stacked = jax.tree.map(lambda leaf: leaf[None], value)
        for bit_index in range(group_bits):
            received = swapper(stacked, bit_index)
            low_side = member >> bit_index & 1 == 0
            stacked = jax.tree.map(
                lambda mine_part, their_part: jnp.where(
                    low_side,
                    jnp.concatenate([mine_part, their_part], 0),
                    jnp.concatenate([their_part, mine_part], 0),
                ),
                stacked,
                received,
            )
        return stacked

    def decode(step_index, positions, cache_rows, length_rows, earlier):
        gathered = lax.all_gather(x_steps[step_index], "tp", axis=1, tiled=True)
        widened = gathered.astype(jnp.float32)
        normed = (
            widened
            * lax.rsqrt(jnp.mean(widened * widened, -1, keepdims=True) + eps_norm)
            * norm_gain
        ).astype(jnp.bfloat16)
        query_raw = jnp.dot(normed, w_query, preferred_element_type=jnp.float32)
        keyval_raw = jnp.dot(normed, w_keyval, preferred_element_type=jnp.float32)
        joined = collect(
            jnp.concatenate([query_raw, keyval_raw], 1),
            lambda value, bit_index: from_partner(value, "tp", bit_index),
        )
        query_width = own_heads * head_dim
        query_all = jnp.moveaxis(joined[:, :, :query_width], 0, 1).reshape(
            row_count, group_size * own_heads, head_dim
        )
        keyval = jnp.moveaxis(joined[:, :, query_width:], 0, 1).reshape(row_count, 2 * head_dim)
        queries = rotary(query_all, positions).astype(jnp.bfloat16)
        partial_value = block_terms(queries, cache_rows[:, 0], member * block_len, length_rows)
        shared = collect(
            partial_value, lambda value, bit_index: from_partner(value, "tp", bit_index)
        )
        own_queries = lax.dynamic_slice_in_dim(queries, member * own_heads, own_heads, 1)
        pieces = [
            tuple(
                (
                    lax.dynamic_slice_in_dim(
                        member_part[block_index], member * own_heads, own_heads, 1
                    )
                    for member_part in shared
                )
            )
            for block_index in range(group_size)
        ]
        fresh_kv = jnp.concatenate(
            [rotary(keyval[:, None, :head_dim], positions)[:, 0], keyval[:, head_dim:]], -1
        ).astype(jnp.bfloat16)
        for fresh_item in earlier + [fresh_kv]:
            pieces.append(fresh_terms(own_queries, fresh_item))
        attended = combine(pieces).reshape(row_count, own_heads * head_dim).astype(jnp.bfloat16)
        head_terms = jnp.dot(attended, w_out, preferred_element_type=jnp.float32)
        return (
            lax.psum_scatter(head_terms, "tp", scatter_dimension=1, tiled=True).astype(
                jnp.bfloat16
            ),
            fresh_kv,
        )

    first_out, first_fresh = decode(0, own_lengths, key_cache, own_lengths, [])
    move_count = moved_slots.shape[1]
    move_ids = jnp.arange(move_count, dtype=jnp.int32)
    partner = jnp.bitwise_xor(instance, partner_mask)
    slots_self = moved_slots[instance]
    slots_partner = moved_slots[partner, move_ids]
    payload = (key_cache[slots_self], first_fresh[slots_self])
    moving = payload
    for bit_index in range(lax.axis_size("inst").bit_length() - 1):
        received = jax.tree.map(
            lambda part, own: part.astype(own.dtype),
            from_partner(as_sent(moving), "inst", bit_index),
            moving,
        )
        use_swap = partner_mask >> bit_index & 1 == 1
        moving = jax.tree.map(
            lambda their_part, mine_part: jnp.where(
                use_swap.reshape((move_count,) + (1,) * (mine_part.ndim - 1)), their_part, mine_part
            ),
            received,
            moving,
        )
    arrived_rows, arrived_fresh = moving
    cache_next = key_cache.at[slots_self].set(arrived_rows)
    fresh_next = first_fresh.at[slots_self].set(arrived_fresh)
    length_next = own_lengths.at[slots_self].set(lengths[partner * row_count + slots_partner])
    second_out, unused = decode(1, length_next + 1, cache_next, length_next, [fresh_next])
    return (jnp.stack([first_out, second_out]), arrived_rows)


def hand_on(out_ref, arrived_ref, out_final, arrived_final):
    out_final[...] = out_ref[...]
    arrived_final[...] = arrived_ref[...]


def fused_kernel(
    len_ref,
    slot_ref,
    mask_ref,
    x_ref,
    gain_ref,
    wq_hbm,
    wkv_hbm,
    wo_hbm,
    cache_hbm,
    out_ref,
    arrived_ref,
    wq,
    wkv,
    wo,
    cache,
    xg,
    acc,
    square,
    place,
    qs,
    fresh,
    mixed,
    attended,
    leave,
    mid_in,
    mid,
    last_in,
    ask_query,
    ask_fresh,
    asked_query,
    asked_fresh,
    reply,
    replied,
    sib_send,
    sib_recv,
    own,
    first_send,
    first_recv,
    second_send,
    second_recv,
    load_sem,
    gather_send,
    gather_recv,
    move_send,
    move_recv,
    ask_send,
    ask_recv,
    reply_send,
    reply_recv,
    sum_send,
    sum_recv,
):
    tp = lax.axis_index("tp")
    inst = lax.axis_index("inst")
    rows = x_ref.shape[1]
    width = x_ref.shape[2]
    moves = slot_ref.shape[1]
    hd = cache.shape[-1] // 2
    heads = qs.shape[2]
    half = rows // 2
    scale = 1.0 / math.sqrt(hd)

    def remote(src, dst, send, recv, **where):
        return pltpu.make_async_remote_copy(
            src_ref=src,
            dst_ref=dst,
            send_sem=send,
            recv_sem=recv,
            device_id=where,
            device_id_type=pl.DeviceIdType.MESH,
        )

    quarter = rows // 4
    cache_loads = [
        pltpu.make_async_copy(
            cache_hbm.at[pl.ds(n * quarter, quarter)],
            cache.at[pl.ds(n * quarter, quarter)],
            load_sem.at[24 + n],
        )
        for n in range(4)
    ]
    for load in cache_loads:
        load.start()
    weight_loads = []
    out_loads = []
    for i in range(8):
        start = pl.multiple_of((tp ^ i) * width, width)
        weight_loads.append(
            (
                pltpu.make_async_copy(wq_hbm.at[pl.ds(start, width), :], wq.at[i], load_sem.at[i]),
                pltpu.make_async_copy(
                    wkv_hbm.at[pl.ds(start, width), :], wkv.at[i], load_sem.at[8 + i]
                ),
            )
        )
        out_loads.append(
            pltpu.make_async_copy(
                wo_hbm.at[:, pl.ds(start, width)], wo.at[i], load_sem.at[16 + i]
            )
        )

    def load_weights(*order):
        for i in order:
            for load in weight_loads[i]:
                load.start()

    load_weights(0)

    barrier = pltpu.get_barrier_semaphore()
    for i in range(1, 8):
        pl.semaphore_signal(
            barrier, inc=1, device_id={"tp": tp ^ i}, device_id_type=pl.DeviceIdType.MESH
        )
    for i in range(1, 4):
        pl.semaphore_signal(
            barrier, inc=1, device_id={"inst": inst ^ i}, device_id_type=pl.DeviceIdType.MESH
        )
    xg[0] = x_ref[...]
    pl.semaphore_wait(barrier, 10)

    def feature_copy(k, s, src, dst, to, part=slice(None)):
        start, size = part.indices(rows)[0], len(range(*part.indices(rows)))
        return remote(
            xg.at[src, s, pl.ds(start, size)],
            xg.at[dst, s, pl.ds(start, size)],
            gather_send.at[8 * s + k],
            gather_recv.at[8 * s + k],
            tp=tp ^ to,
        )

    gathers = [
        {
            "x": feature_copy(0, s, 0, 2, 2),
            "y": feature_copy(1, s, 0, 4, 4),
            "xy": feature_copy(2, s, 2, 6, 4, slice(0, half)),
            "yx": feature_copy(3, s, 4, 6, 2, slice(half, rows)),
            1: feature_copy(4, s, 0, 1, 1),
            3: feature_copy(5, s, 2, 3, 1),
            5: feature_copy(6, s, 4, 5, 1),
            7: feature_copy(7, s, 6, 7, 1),
        }
        for s in range(2)
    ]

    def start_gather(s):
        for name in ("x", "y", 1):
            gathers[s][name].start()

    def forward_gather(s):
        gathers[s]["x"].wait_recv()
        gathers[s]["xy"].start()
        gathers[s]["y"].wait_recv()
        gathers[s]["yx"].start()

    def share_gather(s):
        gathers[s][3].start()
        gathers[s][5].start()

    start_gather(0)

    for load in cache_loads:
        load.wait()
    load_weights(1, 2, 4, 3)
    move_bits = [(1, 2) if j < moves // 2 else (2, 1) for j in range(moves)]
    first_moves = []
    for j in range(moves):
        leave[j] = cache[slot_ref[inst, j]]
        move = remote(
            leave.at[j], mid_in.at[j], move_send.at[j], move_recv.at[j], inst=inst ^ move_bits[j][0]
        )
        move.start()
        first_moves.append(move)

    @pl.loop(0, rows)
    def _(r):
        level = jnp.full((1, 2 * hd), len_ref[inst * rows + r], jnp.int32)
        place[pl.ds(r, 1), :] = level[:, :hd]

    row_ids = lax.broadcasted_iota(jnp.int32, (rows, hd), 0)
    own_place = place[...]
    next_place = own_place
    for j in range(moves):
        partner = inst ^ mask_ref[j]
        length = len_ref[partner * rows + slot_ref[partner, j]]
        next_place = jnp.where(row_ids == slot_ref[inst, j], length, next_place)
    positions = jnp.concatenate([own_place, next_place + 1], 0).astype(jnp.float32)
    lane = lax.broadcasted_iota(jnp.int32, (1, hd), 1)
    pair_id = jnp.where(lane < hd // 2, lane, lane - hd // 2).astype(jnp.float32)
    frequency = jnp.exp(pair_id * (-2.0 * math.log(rope_base) / hd))
    angles = positions * frequency
    cosine = jnp.cos(angles)
    sine = jnp.sin(angles)
    sine = jnp.where(lane < hd // 2, -sine, sine)

    acc[...] = jnp.zeros_like(acc)
    square[...] = jnp.zeros_like(square)
    q_width = wq.shape[2]

    def project(i, s):
        if s == 0:
            for load in weight_loads[i]:
                load.wait()
        part = slice(s * rows, (s + 1) * rows)
        wide = xg[i, s].astype(jnp.float32)
        square[part] += jnp.sum(wide * wide, -1, keepdims=True)
        start = pl.multiple_of((tp ^ i) * width, width)
        gain = gain_ref[pl.ds(start, width)]
        scaled = (wide * gain[None, :]).astype(jnp.bfloat16)

        for c in range(0, q_width, 512):
            cols = slice(c, c + 512)
            acc[part, cols] += jnp.dot(scaled, wq[i, :, cols], preferred_element_type=jnp.float32)

        acc[part, q_width:] += jnp.dot(scaled, wkv[i], preferred_element_type=jnp.float32)

    def rotate(s):
        part = slice(s * rows, (s + 1) * rows)
        factor = lax.rsqrt(square[part] * (1.0 / (8 * width)) + eps_norm)

        def turned(block):
            block = block * factor
            block = block * cosine[part] + pltpu.roll(block, hd // 2, 1) * sine[part]
            return block.astype(jnp.bfloat16).astype(jnp.float32)

        for h in range(heads):
            qs[s, :, h, :] = turned(acc[part, h * hd : (h + 1) * hd])
        fresh[part, :hd] = turned(acc[part, q_width : q_width + hd])
        value = acc[part, q_width + hd :] * factor
        fresh[part, hd:] = value.astype(jnp.bfloat16).astype(jnp.float32)

    forward_gather(0)
    start_gather(1)
    share_gather(0)
    project(0, 0)
    load_weights(5, 6, 7)
    gathers[0][1].wait_recv()
    project(1, 0)
    project(2, 0)
    project(4, 0)
    for i in (7, 3, 6, 5):
        out_loads[i].start()
    gathers[0][3].wait_recv()
    project(3, 0)
    gathers[0]["xy"].wait_recv()
    gathers[0]["yx"].wait_recv()
    gathers[0][7].start()
    gathers[0][5].wait_recv()
    project(5, 0)
    for i in (2, 1, 4, 0):
        out_loads[i].start()
    project(6, 0)
    gathers[0][7].wait_recv()
    project(7, 0)
    rotate(0)
    forward_gather(1)
    share_gather(1)

    def matched(mask, parts):
        return jnp.where(mask == 1, parts[0], jnp.where(mask == 2, parts[1], parts[2]))

    def attend(requests):
        scores = [
            scale
            * lax.dot_general(
                queries.astype(jnp.bfloat16),
                keys,
                (((1,), (1,)), ((), ())),
                preferred_element_type=jnp.float32,
            )
            for queries, keys, values, length, news in requests
        ]
        spots = lax.broadcasted_iota(jnp.int32, scores[0].shape, 1)
        scores = [
            jnp.where(spots < request[3], score, floor_score)
            for score, request in zip(scores, requests)
        ]
        tops = [jnp.max(score, -1, keepdims=True) for score in scores]
        marks = []
        for queries, keys, values, length, news in requests:
            row_marks = []
            for row, allowed in news:
                mark = scale * jnp.sum(queries * row[:, :hd], -1, keepdims=True)
                if allowed is not None:
                    mark = jnp.where(allowed, mark, floor_score)
                row_marks.append(mark)
            marks.append(row_marks)
        weights = [
            jnp.where(spots < request[3], jnp.exp(score - top), 0.0).astype(jnp.bfloat16)
            for score, top, request in zip(scores, tops, requests)
        ]
        mixes = [
            jnp.dot(weight, request[2], preferred_element_type=jnp.float32)
            for weight, request in zip(weights, requests)
        ]
        totals = [jnp.sum(weight.astype(jnp.float32), -1, keepdims=True) for weight in weights]
        answers = []
        for request, top, row_marks, mix, total in zip(requests, tops, marks, mixes, totals):
            overall = reduce(jnp.maximum, row_marks, top)
            share = jnp.exp(top - overall)
            numerator = share * mix
            denominator = share * total
            for (row, allowed), mark in zip(request[4], row_marks):
                share = jnp.exp(mark - overall)
                if allowed is not None:
                    share = jnp.where(allowed, share, 0.0)
                numerator = numerator + share * row[:, hd:]
                denominator = denominator + share
            answers.append(numerator / denominator)
        return answers

    batch = 16

    def attend_slots(s, first, last):
        @pl.loop(first, last)
        def _(group):
            ids = [group * batch + u for u in range(batch)]
            answers = attend(
                [
                    (
                        qs[s, r],
                        cache[r, :, :hd],
                        cache[r, :, hd:],
                        len_ref[inst * rows + r],
                        [(fresh[pl.ds(n * rows + r, 1), :], None) for n in range(s + 1)],
                    )
                    for r in ids
                ]
            )
            for r, answer in zip(ids, answers):
                mixed[r] = answer

    groups = rows // batch

    tile = 512
    sibling_sums = [{}, {}]
    first_sums = [{}, {}]
    second_sums = [[], []]

    def send_first(s, n, m):
        k = 10 * s + 4 + 2 * n + m
        copy = remote(
            first_send.at[s, n, m],
            first_recv.at[s, n, m],
            sum_send.at[k],
            sum_recv.at[k],
            tp=tp ^ (2, 4)[n],
        )
        copy.start()
        first_sums[s][n, m] = copy

    def output_block(i, s):
        k = i // 2
        if s == 0:
            out_loads[i].wait()
        if i % 2 == 0:
            sibling_sums[s][k].wait_recv()
        for c in range(0, width, tile):
            cols = slice(c, c + tile)
            chip = jnp.dot(attended[s], wo[i, :, cols], preferred_element_type=jnp.float32)
            if i % 2:
                sib_send[s, k, :, cols] = chip.astype(jnp.bfloat16)
                continue
            chip = chip + sib_recv[s, k, :, cols].astype(jnp.float32)
            if i in (2, 6):
                first_send[s, 0, i // 4, :, cols] = chip[:half].astype(jnp.bfloat16)
            if i in (4, 6):
                first_send[s, 1, int(i == 6), :, cols] = chip[half:].astype(jnp.bfloat16)
            if i == 2:
                own[s, 1, half:, cols] = chip[half:]
            elif i == 4:
                own[s, 1, :half, cols] = chip[:half]
            elif i == 0:
                own[s, 0, :, cols] = chip
        if i % 2:
            k_sem = 10 * s + k
            copy = remote(
                sib_send.at[s, k],
                sib_recv.at[s, k],
                sum_send.at[k_sem],
                sum_recv.at[k_sem],
                tp=tp ^ 1,
            )
            copy.start()
            sibling_sums[s][k] = copy
        if i in (2, 6):
            send_first(s, 0, i // 4)
        if i in (4, 6):
            send_first(s, 1, int(i == 6))

    def output(s):
        for i in (7, 3, 6, 5, 2, 1, 4, 0):
            output_block(i, s)

    def send_second(s):
        for n in range(2):
            first_sums[s][n, 1].wait_recv()
            base = own[s, 1, n * half : (n + 1) * half, :]
            total = base + first_recv[s, n, 1].astype(jnp.float32)
            second_send[s, n] = total.astype(jnp.bfloat16)
            k = 10 * s + 8 + n
            copy = remote(
                second_send.at[s, n],
                second_recv.at[s, n],
                sum_send.at[k],
                sum_recv.at[k],
                tp=tp ^ (4, 2)[n],
            )
            copy.start()
            second_sums[s].append(copy)

    def finish(s):
        for n in range(2):
            first_sums[s][n, 0].wait_recv()
            second_sums[s][n].wait_recv()
            part = slice(n * half, (n + 1) * half)
            total = own[s, 0, part, :] + first_recv[s, n, 0].astype(jnp.float32)
            total = total + second_recv[s, n].astype(jnp.float32)
            out_ref[s, part, :] = total.astype(jnp.bfloat16)

    attend_slots(0, 0, groups)
    for h in range(heads):
        attended[0, :, h * hd : (h + 1) * hd] = mixed[:, h, :].astype(jnp.bfloat16)
    output(0)

    for name in (1, 3, 5, "xy", "yx"):
        gathers[1][name].wait_recv()
    gathers[1][7].start()
    for i in range(7):
        project(i, 1)
    gathers[1][7].wait_recv()
    project(7, 1)
    rotate(1)

    slots = [slot_ref[inst, j] for j in range(moves)]
    ask_query[...] = jnp.concatenate([qs[1, slot] for slot in slots], 0).astype(
        jnp.bfloat16
    )
    for j in range(moves):
        ask_fresh[pl.ds(j, 1), :] = fresh[pl.ds(rows + slots[j], 1), :]
    asks = []
    for i in range(3):
        pair = (
            remote(
                ask_query, asked_query.at[i], ask_send.at[i], ask_recv.at[i], inst=inst ^ (i + 1)
            ),
            remote(
                ask_fresh,
                asked_fresh.at[i],
                ask_send.at[3 + i],
                ask_recv.at[3 + i],
                inst=inst ^ (i + 1),
            ),
        )
        for copy in pair:
            copy.start()
            asks.append(copy)

    send_second(0)
    attend_slots(1, 0, groups // 2)

    for copy in asks:
        copy.wait_recv()
    requests = []
    for j in range(moves):
        slot = slots[j]
        mask = mask_ref[j]
        part = slice(j * heads, (j + 1) * heads)
        queries = matched(mask, [asked_query[i].astype(jnp.float32)[part] for i in range(3)])
        news = matched(mask, [asked_fresh[i, pl.ds(j, 1), :] for i in range(3)])
        requests.append(
            (
                queries,
                cache[slot, :, :hd],
                cache[slot, :, hd:],
                len_ref[inst * rows + slot],
                [(fresh[pl.ds(slot, 1), :], None), (news, None)],
            )
        )
    reply[...] = jnp.concatenate(attend(requests), 0).astype(jnp.bfloat16)
    replies = []
    for i in range(3):
        copy = remote(
            reply, replied.at[i], reply_send.at[i], reply_recv.at[i], inst=inst ^ (i + 1)
        )
        copy.start()
        replies.append(copy)

    second_moves = []
    for j in range(moves):
        first_moves[j].wait_recv()
        taken = (mask_ref[j] & move_bits[j][0]) != 0
        mid[j] = jnp.where(taken, mid_in[j], leave[j])
        move = remote(
            mid.at[j],
            last_in.at[j],
            move_send.at[moves + j],
            move_recv.at[moves + j],
            inst=inst ^ move_bits[j][1],
        )
        move.start()
        second_moves.append(move)

    attend_slots(1, groups // 2, groups)

    for copy in replies:
        copy.wait_recv()
    came = [
        matched(
            mask_ref[j],
            [replied[i].astype(jnp.float32)[j * heads : (j + 1) * heads] for i in range(3)],
        )
        for j in range(moves)
    ]
    for h in range(heads):
        second = mixed[:, h, :]
        for j in range(moves):
            second = jnp.where(row_ids == slots[j], came[j][h : h + 1], second)
        attended[1, :, h * hd : (h + 1) * hd] = second.astype(jnp.bfloat16)
    output(1)
    finish(0)
    send_second(1)

    for j in range(moves):
        second_moves[j].wait_recv()
        taken = (mask_ref[j] & move_bits[j][1]) != 0
        arrived_ref[j, 0] = jnp.where(taken, last_in[j], mid[j])

    finish(1)

    for copy in (
        first_moves
        + second_moves
        + asks
        + replies
        + [copy for group in gathers for copy in group.values()]
        + [copy for group in sibling_sums for copy in group.values()]
        + [copy for group in first_sums for copy in group.values()]
        + second_sums[0]
        + second_sums[1]
    ):
        copy.wait_send()


def fused(
    x_steps, norm_gain, w_query, w_keyval, w_out, key_cache, lengths, moved_slots, partner_mask
):
    steps, rows, width = x_steps.shape
    moves = moved_slots.shape[1]
    block_len, pair_dim = key_cache.shape[2:]
    hd = pair_dim // 2
    q_width = w_query.shape[1]
    heads = q_width // hd
    both = steps * rows
    bf16, f32 = jnp.bfloat16, jnp.float32
    smem = pl.BlockSpec(memory_space=pltpu.SMEM)
    vmem = pl.BlockSpec(memory_space=pltpu.VMEM)
    anywhere = pl.BlockSpec(memory_space=pl.ANY)
    dma = pltpu.SemaphoreType.DMA
    results = pl.pallas_call(
        fused_kernel,
        out_shape=(
            jax.ShapeDtypeStruct((steps, rows, width), bf16),
            jax.ShapeDtypeStruct((moves,) + key_cache.shape[1:], bf16),
        ),
        in_specs=[smem, smem, smem, vmem, vmem, anywhere, anywhere, anywhere, anywhere],
        out_specs=(vmem, vmem),
        scratch_shapes=[
            pltpu.VMEM((8, width, q_width), bf16),
            pltpu.VMEM((8, width, pair_dim), bf16),
            pltpu.VMEM((8, q_width, width), bf16),
            pltpu.VMEM((rows, block_len, pair_dim), bf16),
            pltpu.VMEM((8, steps, rows, width), bf16),
            pltpu.VMEM((both, q_width + pair_dim), f32),
            pltpu.VMEM((both, 1), f32),
            pltpu.VMEM((rows, hd), jnp.int32),
            pltpu.VMEM((steps, rows, heads, hd), f32),
            pltpu.VMEM((both, pair_dim), f32),
            pltpu.VMEM((rows, heads, hd), f32),
            pltpu.VMEM((steps, rows, q_width), bf16),
            pltpu.VMEM((moves, block_len, pair_dim), bf16),
            pltpu.VMEM((moves, block_len, pair_dim), bf16),
            pltpu.VMEM((moves, block_len, pair_dim), bf16),
            pltpu.VMEM((moves, block_len, pair_dim), bf16),
            pltpu.VMEM((moves * heads, hd), bf16),
            pltpu.VMEM((moves, pair_dim), f32),
            pltpu.VMEM((3, moves * heads, hd), bf16),
            pltpu.VMEM((3, moves, pair_dim), f32),
            pltpu.VMEM((moves * heads, hd), bf16),
            pltpu.VMEM((3, moves * heads, hd), bf16),
            pltpu.VMEM((steps, 4, rows, width), bf16),
            pltpu.VMEM((steps, 4, rows, width), bf16),
            pltpu.VMEM((steps, 2, rows, width), f32),
            pltpu.VMEM((steps, 2, 2, rows // 2, width), bf16),
            pltpu.VMEM((steps, 2, 2, rows // 2, width), bf16),
            pltpu.VMEM((steps, 2, rows // 2, width), bf16),
            pltpu.VMEM((steps, 2, rows // 2, width), bf16),
            dma((28,)),
            dma((16,)),
            dma((16,)),
            dma((2 * moves,)),
            dma((2 * moves,)),
            dma((6,)),
            dma((6,)),
            dma((3,)),
            dma((3,)),
            dma((20,)),
            dma((20,)),
        ],
        compiler_params=pltpu.CompilerParams(
            collective_id=0, has_side_effects=True, vmem_limit_bytes=60 * 2**20
        ),
        cost_estimate=pl.CostEstimate(
            flops=2 * both * w_query.shape[0] * (2 * q_width + pair_dim),
            bytes_accessed=2 * (w_query.size + w_keyval.size + w_out.size + key_cache.size),
            transcendentals=0,
        ),
    )(
        lengths,
        moved_slots,
        partner_mask,
        x_steps,
        norm_gain,
        w_query,
        w_keyval,
        w_out,
        key_cache.reshape(rows, block_len, pair_dim),
    )
    return pl.pallas_call(
        hand_on,
        out_shape=tuple(jax.ShapeDtypeStruct(part.shape, part.dtype) for part in results),
        in_specs=[vmem, vmem],
        out_specs=(vmem, vmem),
    )(*results)


def solution(mesh):
    placed = (
        P(None, "inst", "tp"),
        P(),
        P(None, "tp"),
        P(None, "tp"),
        P("tp", None),
        P("inst", "tp", None, None),
        P(),
        P(),
        P(),
    )
    body = fused if mesh.shape["tp"] == KVH and mesh.shape["inst"] == 4 else shards
    return jax.shard_map(
        body,
        mesh=mesh,
        in_specs=placed,
        out_specs=(P(None, "inst", "tp"), P("inst", "tp", None, None)),
        check_vma=False,
    )
```

```python
from functools import reduce
import math

import jax
import jax.numpy as jnp
from jax import lax
from jax.experimental import pallas as pl
from jax.experimental.pallas import tpu as pltpu
from jax.sharding import PartitionSpec as P

KVH = 8


eps_norm = 1e-05
rope_base = 500000.0
floor_score = -1e30


def from_partner(block, axis, bit):
    count = lax.axis_size(axis)
    route = []
    for low in range(count):
        high = low | 1 << bit
        if high != low and high < count:
            route += [(low, high), (high, low)]
    return lax.ppermute(block, axis, route)


def as_sent(value):

    def short(part):
        return part.astype(jnp.bfloat16) if part.dtype == jnp.float32 else part

    return jax.tree.map(short, value)


def rotary(vectors, positions):
    half_dim = vectors.shape[-1] // 2
    frequency = rope_base ** (-(jnp.arange(half_dim, dtype=jnp.float32) * 2.0) / vectors.shape[-1])
    angles = positions.astype(jnp.float32)[..., None] * frequency
    cosine = jnp.cos(angles)[..., None, :]
    sine_part = jnp.sin(angles)[..., None, :]
    first_half = vectors[..., :half_dim]
    second_half = vectors[..., half_dim:]
    return jnp.concatenate(
        [
            first_half * cosine - second_half * sine_part,
            second_half * cosine + first_half * sine_part,
        ],
        -1,
    )


def block_terms(queries, block, start, length_rows):
    head_dim = queries.shape[-1]
    block_len = block.shape[1]
    scores = jnp.einsum(
        "rhd,rtd->rht", queries, block[..., :head_dim], preferred_element_type=jnp.float32
    ) / math.sqrt(head_dim)
    places = start + jnp.arange(block_len, dtype=jnp.int32)
    visible = (places[None, :] < length_rows[:, None])[:, None, :]
    scores = jnp.where(visible, scores, floor_score)
    block_max = jnp.max(scores, -1)
    weights = jnp.where(visible, jnp.exp(scores - block_max[..., None]), 0.0).astype(jnp.bfloat16)
    block_sum = jnp.sum(weights.astype(jnp.float32), -1)
    block_mix = jnp.einsum(
        "rht,rtd->rhd", weights, block[..., head_dim:], preferred_element_type=jnp.float32
    )
    return (block_max, block_sum, block_mix)


def fresh_terms(queries, fresh_kv):
    head_dim = queries.shape[-1]
    score = jnp.einsum(
        "rhd,rd->rh", queries, fresh_kv[:, :head_dim], preferred_element_type=jnp.float32
    ) / math.sqrt(head_dim)
    block_mix = jnp.broadcast_to(fresh_kv[:, None, head_dim:].astype(jnp.float32), queries.shape)
    return (score, jnp.ones_like(score), block_mix)


def combine(pieces):
    overall_max = reduce(jnp.maximum, [piece[0] for piece in pieces])
    numerator = reduce(
        jnp.add, [jnp.exp(piece[0] - overall_max)[..., None] * piece[2] for piece in pieces]
    )
    denominator = reduce(jnp.add, [jnp.exp(piece[0] - overall_max) * piece[1] for piece in pieces])
    return numerator / denominator[..., None]


def shards(
    x_steps, norm_gain, w_query, w_keyval, w_out, key_cache, lengths, moved_slots, partner_mask
):
    row_count = x_steps.shape[1]
    head_dim = key_cache.shape[-1] // 2
    block_len = key_cache.shape[2]
    group_size = lax.axis_size("tp") // KVH
    group_bits = group_size.bit_length() - 1
    member = lax.axis_index("tp") % group_size
    instance = lax.axis_index("inst")
    own_heads = w_query.shape[1] // head_dim
    own_lengths = lax.dynamic_slice_in_dim(lengths, instance * row_count, row_count)

    def collect(value, swapper):
        stacked = jax.tree.map(lambda leaf: leaf[None], value)
        for bit_index in range(group_bits):
            received = swapper(stacked, bit_index)
            low_side = member >> bit_index & 1 == 0
            stacked = jax.tree.map(
                lambda mine_part, their_part: jnp.where(
                    low_side,
                    jnp.concatenate([mine_part, their_part], 0),
                    jnp.concatenate([their_part, mine_part], 0),
                ),
                stacked,
                received,
            )
        return stacked

    def decode(step_index, positions, cache_rows, length_rows, earlier):
        gathered = lax.all_gather(x_steps[step_index], "tp", axis=1, tiled=True)
        widened = gathered.astype(jnp.float32)
        normed = (
            widened
            * lax.rsqrt(jnp.mean(widened * widened, -1, keepdims=True) + eps_norm)
            * norm_gain
        ).astype(jnp.bfloat16)
        query_raw = jnp.dot(normed, w_query, preferred_element_type=jnp.float32)
        keyval_raw = jnp.dot(normed, w_keyval, preferred_element_type=jnp.float32)
        joined = collect(
            jnp.concatenate([query_raw, keyval_raw], 1),
            lambda value, bit_index: from_partner(value, "tp", bit_index),
        )
        query_width = own_heads * head_dim
        query_all = jnp.moveaxis(joined[:, :, :query_width], 0, 1).reshape(
            row_count, group_size * own_heads, head_dim
        )
        keyval = jnp.moveaxis(joined[:, :, query_width:], 0, 1).reshape(row_count, 2 * head_dim)
        queries = rotary(query_all, positions).astype(jnp.bfloat16)
        partial_value = block_terms(queries, cache_rows[:, 0], member * block_len, length_rows)
        shared = collect(
            partial_value, lambda value, bit_index: from_partner(value, "tp", bit_index)
        )
        own_queries = lax.dynamic_slice_in_dim(queries, member * own_heads, own_heads, 1)
        pieces = [
            tuple(
                (
                    lax.dynamic_slice_in_dim(
                        member_part[block_index], member * own_heads, own_heads, 1
                    )
                    for member_part in shared
                )
            )
            for block_index in range(group_size)
        ]
        fresh_kv = jnp.concatenate(
            [rotary(keyval[:, None, :head_dim], positions)[:, 0], keyval[:, head_dim:]], -1
        ).astype(jnp.bfloat16)
        for fresh_item in earlier + [fresh_kv]:
            pieces.append(fresh_terms(own_queries, fresh_item))
        attended = combine(pieces).reshape(row_count, own_heads * head_dim).astype(jnp.bfloat16)
        head_terms = jnp.dot(attended, w_out, preferred_element_type=jnp.float32)
        return (
            lax.psum_scatter(head_terms, "tp", scatter_dimension=1, tiled=True).astype(
                jnp.bfloat16
            ),
            fresh_kv,
        )

    first_out, first_fresh = decode(0, own_lengths, key_cache, own_lengths, [])
    move_count = moved_slots.shape[1]
    move_ids = jnp.arange(move_count, dtype=jnp.int32)
    partner = jnp.bitwise_xor(instance, partner_mask)
    slots_self = moved_slots[instance]
    slots_partner = moved_slots[partner, move_ids]
    payload = (key_cache[slots_self], first_fresh[slots_self])
    moving = payload
    for bit_index in range(lax.axis_size("inst").bit_length() - 1):
        received = jax.tree.map(
            lambda part, own: part.astype(own.dtype),
            from_partner(as_sent(moving), "inst", bit_index),
            moving,
        )
        use_swap = partner_mask >> bit_index & 1 == 1
        moving = jax.tree.map(
            lambda their_part, mine_part: jnp.where(
                use_swap.reshape((move_count,) + (1,) * (mine_part.ndim - 1)), their_part, mine_part
            ),
            received,
            moving,
        )
    arrived_rows, arrived_fresh = moving
    cache_next = key_cache.at[slots_self].set(arrived_rows)
    fresh_next = first_fresh.at[slots_self].set(arrived_fresh)
    length_next = own_lengths.at[slots_self].set(lengths[partner * row_count + slots_partner])
    second_out, unused = decode(1, length_next + 1, cache_next, length_next, [fresh_next])
    return (jnp.stack([first_out, second_out]), arrived_rows)


def hand_on(out_ref, arrived_ref, out_final, arrived_final):
    out_final[...] = out_ref[...]
    arrived_final[...] = arrived_ref[...]


def fused_kernel(
    len_ref,
    slot_ref,
    mask_ref,
    x_ref,
    gain_ref,
    wq_hbm,
    wkv_hbm,
    wo_hbm,
    cache_hbm,
    out_ref,
    arrived_ref,
    wq,
    wkv,
    wo,
    cache,
    xg,
    acc,
    square,
    place,
    qs,
    fresh,
    mixed,
    attended,
    leave,
    mid_in,
    mid,
    last_in,
    ask_query,
    ask_fresh,
    asked_query,
    asked_fresh,
    reply,
    replied,
    sib_send,
    sib_recv,
    own,
    first_send,
    first_recv,
    second_send,
    second_recv,
    load_sem,
    gather_send,
    gather_recv,
    move_send,
    move_recv,
    ask_send,
    ask_recv,
    reply_send,
    reply_recv,
    sum_send,
    sum_recv,
):
    tp = lax.axis_index("tp")
    inst = lax.axis_index("inst")
    rows = x_ref.shape[1]
    width = x_ref.shape[2]
    moves = slot_ref.shape[1]
    hd = cache.shape[-1] // 2
    heads = qs.shape[1] // 2
    scale = 1.0 / math.sqrt(hd)

    def remote(src, dst, send, recv, **where):
        return pltpu.make_async_remote_copy(
            src_ref=src,
            dst_ref=dst,
            send_sem=send,
            recv_sem=recv,
            device_id=where,
            device_id_type=pl.DeviceIdType.MESH,
        )

    quarter = rows // 4
    cache_loads = [
        pltpu.make_async_copy(
            cache_hbm.at[pl.ds(n * quarter, quarter)],
            cache.at[pl.ds(n * quarter, quarter)],
            load_sem.at[24 + n],
        )
        for n in range(4)
    ]
    for load in cache_loads:
        load.start()
    weight_loads = []
    out_loads = []
    for i in range(8):
        start = pl.multiple_of((tp ^ i) * width, width)
        weight_loads.append(
            (
                pltpu.make_async_copy(wq_hbm.at[pl.ds(start, width), :], wq.at[i], load_sem.at[i]),
                pltpu.make_async_copy(
                    wkv_hbm.at[pl.ds(start, width), :], wkv.at[i], load_sem.at[8 + i]
                ),
            )
        )
        out_loads.append(
            pltpu.make_async_copy(
                wo_hbm.at[:, pl.ds(start, width)], wo.at[i], load_sem.at[16 + i]
            )
        )

    def load_weights(*order):
        for i in order:
            for load in weight_loads[i]:
                load.start()

    load_weights(0)

    barrier = pltpu.get_barrier_semaphore()
    for i in range(1, 8):
        pl.semaphore_signal(
            barrier, inc=1, device_id={"tp": tp ^ i}, device_id_type=pl.DeviceIdType.MESH
        )
    for i in range(1, 4):
        pl.semaphore_signal(
            barrier, inc=1, device_id={"inst": inst ^ i}, device_id_type=pl.DeviceIdType.MESH
        )
    xg[0] = x_ref[...]
    pl.semaphore_wait(barrier, 10)

    def feature_copy(k, src, dst, to, part=None):
        src_ref = xg.at[src] if part is None else xg.at[src, part]
        dst_ref = xg.at[dst] if part is None else xg.at[dst, part]
        return remote(src_ref, dst_ref, gather_send.at[k], gather_recv.at[k], tp=tp ^ to)

    along_x = [feature_copy(0, 0, 2, 2, 0), feature_copy(1, 0, 2, 2, 1)]
    along_y = [feature_copy(2, 0, 4, 4, 1), feature_copy(3, 0, 4, 4, 0)]
    to_sibling = [feature_copy(6, 0, 1, 1)]
    along_x[0].start()
    along_y[0].start()
    along_x[1].start()
    along_y[1].start()
    to_sibling[0].start()

    for load in cache_loads:
        load.wait()
    load_weights(1, 2, 4)
    move_bits = [(1, 2) if j < moves // 2 else (2, 1) for j in range(moves)]
    first_moves = {}
    trip_order = [n + m * (moves // 2) for n in range(moves // 2) for m in range(2)]
    for j in trip_order:
        leave[j] = cache[slot_ref[inst, j]]
        move = remote(
            leave.at[j], mid_in.at[j], move_send.at[j], move_recv.at[j], inst=inst ^ move_bits[j][0]
        )
        move.start()
        first_moves[j] = move

    @pl.loop(0, rows)
    def _(r):
        level = jnp.full((1, 2 * hd), len_ref[inst * rows + r], jnp.int32)
        place[pl.ds(r, 1), :] = level[:, :hd]

    row_ids = lax.broadcasted_iota(jnp.int32, (rows, hd), 0)
    own_place = place[...]
    next_place = own_place
    for j in range(moves):
        partner = inst ^ mask_ref[j]
        length = len_ref[partner * rows + slot_ref[partner, j]]
        next_place = jnp.where(row_ids == slot_ref[inst, j], length, next_place)
    positions = jnp.concatenate([own_place, next_place + 1], 0).astype(jnp.float32)
    lane = lax.broadcasted_iota(jnp.int32, (1, hd), 1)
    pair_id = jnp.where(lane < hd // 2, lane, lane - hd // 2).astype(jnp.float32)
    frequency = jnp.exp(pair_id * (-2.0 * math.log(rope_base) / hd))
    angles = positions * frequency
    cosine = jnp.cos(angles)
    sine = jnp.sin(angles)
    sine = jnp.where(lane < hd // 2, -sine, sine)

    acc[...] = jnp.zeros_like(acc)
    square[...] = jnp.zeros_like(square)
    q_width = wq.shape[2]

    def project(i):
        for load in weight_loads[i]:
            load.wait()
        wide = xg[i].reshape(2 * rows, width).astype(jnp.float32)
        square[...] += jnp.sum(wide * wide, -1, keepdims=True)
        start = pl.multiple_of((tp ^ i) * width, width)
        gain = gain_ref[pl.ds(start, width)]
        scaled = (wide * gain[None, :]).astype(jnp.bfloat16)

        for c in range(0, q_width, 512):
            cols = slice(c, c + 512)
            acc[:, cols] += jnp.dot(scaled, wq[i, :, cols], preferred_element_type=jnp.float32)

        acc[:, q_width:] += jnp.dot(scaled, wkv[i], preferred_element_type=jnp.float32)

    along_x[0].wait_recv()
    along_y[0].wait_recv()
    across = [feature_copy(4, 2, 6, 4, 0), feature_copy(5, 4, 6, 2, 1)]
    across[0].start()
    across[1].start()
    project(0)
    load_weights(3, 5)
    to_sibling[0].wait_recv()
    project(1)
    load_weights(6, 7)
    along_x[1].wait_recv()
    to_sibling.append(feature_copy(7, 2, 3, 1))
    to_sibling[1].start()
    along_y[1].wait_recv()
    to_sibling.append(feature_copy(8, 4, 5, 1))
    to_sibling[2].start()
    project(2)
    project(4)
    for i in (7, 3, 6, 5):
        out_loads[i].start()
    to_sibling[1].wait_recv()
    project(3)
    to_sibling[2].wait_recv()
    project(5)
    for i in (2, 1, 4, 0):
        out_loads[i].start()
    across[0].wait_recv()
    across[1].wait_recv()
    to_sibling.append(feature_copy(9, 6, 7, 1))
    to_sibling[3].start()
    project(6)
    to_sibling[3].wait_recv()
    project(7)

    factor = lax.rsqrt(square[...] * (1.0 / (8 * width)) + eps_norm)

    def turned(part):
        part = part * factor
        return (part * cosine + pltpu.roll(part, hd // 2, 1) * sine).astype(jnp.bfloat16)

    for h in range(heads):
        rotated = turned(acc[:, h * hd : (h + 1) * hd]).astype(jnp.float32)
        qs[:, h, :] = rotated[:rows]
        qs[:, heads + h, :] = rotated[rows:]
    fresh[:, :hd] = turned(acc[:, q_width : q_width + hd]).astype(jnp.float32)
    fresh[:, hd:] = (acc[:, q_width + hd :] * factor).astype(jnp.bfloat16).astype(jnp.float32)

    slots = [slot_ref[inst, j] for j in range(moves)]
    ask_query[...] = jnp.concatenate([qs[slot, heads:, :] for slot in slots], 0).astype(
        jnp.bfloat16
    )
    for j in range(moves):
        ask_fresh[pl.ds(j, 1), :] = fresh[pl.ds(rows + slots[j], 1), :]
    asks = []
    for i in range(3):
        pair = (
            remote(
                ask_query, asked_query.at[i], ask_send.at[i], ask_recv.at[i], inst=inst ^ (i + 1)
            ),
            remote(
                ask_fresh,
                asked_fresh.at[i],
                ask_send.at[3 + i],
                ask_recv.at[3 + i],
                inst=inst ^ (i + 1),
            ),
        )
        for copy in pair:
            copy.start()
            asks.append(copy)

    second_moves = {}

    def second_trip(ids):
        for j in ids:
            first_moves[j].wait_recv()
            taken = (mask_ref[j] & move_bits[j][0]) != 0
            mid[j] = jnp.where(taken, mid_in[j], leave[j])
            move = remote(
                mid.at[j],
                last_in.at[j],
                move_send.at[moves + j],
                move_recv.at[moves + j],
                inst=inst ^ move_bits[j][1],
            )
            move.start()
            second_moves[j] = move

    def matched(mask, parts):
        return jnp.where(mask == 1, parts[0], jnp.where(mask == 2, parts[1], parts[2]))

    def attend(requests):
        scores = [
            scale
            * lax.dot_general(
                queries.astype(jnp.bfloat16),
                keys,
                (((1,), (1,)), ((), ())),
                preferred_element_type=jnp.float32,
            )
            for queries, keys, values, length, news in requests
        ]
        spots = lax.broadcasted_iota(jnp.int32, scores[0].shape, 1)
        scores = [
            jnp.where(spots < request[3], score, floor_score)
            for score, request in zip(scores, requests)
        ]
        tops = [jnp.max(score, -1, keepdims=True) for score in scores]
        marks = []
        for queries, keys, values, length, news in requests:
            row_marks = []
            for row, allowed in news:
                mark = scale * jnp.sum(queries * row[:, :hd], -1, keepdims=True)
                if allowed is not None:
                    mark = jnp.where(allowed, mark, floor_score)
                row_marks.append(mark)
            marks.append(row_marks)
        weights = [
            jnp.where(spots < request[3], jnp.exp(score - top), 0.0).astype(jnp.bfloat16)
            for score, top, request in zip(scores, tops, requests)
        ]
        mixes = [
            jnp.dot(weight, request[2], preferred_element_type=jnp.float32)
            for weight, request in zip(weights, requests)
        ]
        totals = [jnp.sum(weight.astype(jnp.float32), -1, keepdims=True) for weight in weights]
        answers = []
        for request, top, row_marks, mix, total in zip(requests, tops, marks, mixes, totals):
            overall = reduce(jnp.maximum, row_marks, top)
            share = jnp.exp(top - overall)
            numerator = share * mix
            denominator = share * total
            for (row, allowed), mark in zip(request[4], row_marks):
                share = jnp.exp(mark - overall)
                if allowed is not None:
                    share = jnp.where(allowed, share, 0.0)
                numerator = numerator + share * row[:, hd:]
                denominator = denominator + share
            answers.append(numerator / denominator)
        return answers

    later = lax.broadcasted_iota(jnp.int32, (2 * heads, 1), 0) >= heads
    batch = 16

    def attend_slots(first, last):
        @pl.loop(first, last)
        def _(group):
            ids = [group * batch + u for u in range(batch)]
            answers = attend(
                [
                    (
                        qs[r],
                        cache[r, :, :hd],
                        cache[r, :, hd:],
                        len_ref[inst * rows + r],
                        [(fresh[pl.ds(r, 1), :], None), (fresh[pl.ds(rows + r, 1), :], later)],
                    )
                    for r in ids
                ]
            )
            for r, answer in zip(ids, answers):
                mixed[r] = answer

    groups = rows // batch
    attend_slots(0, groups // 4)
    second_trip(trip_order[:2])
    attend_slots(groups // 4, groups // 2)
    second_trip(trip_order[2:4])

    for copy in asks:
        copy.wait_recv()
    requests = []
    for j in range(moves):
        slot = slots[j]
        mask = mask_ref[j]
        part = slice(j * heads, (j + 1) * heads)
        queries = matched(mask, [asked_query[i].astype(jnp.float32)[part] for i in range(3)])
        news = matched(mask, [asked_fresh[i, pl.ds(j, 1), :] for i in range(3)])
        requests.append(
            (
                queries,
                cache[slot, :, :hd],
                cache[slot, :, hd:],
                len_ref[inst * rows + slot],
                [(fresh[pl.ds(slot, 1), :], None), (news, None)],
            )
        )
    reply[...] = jnp.concatenate(attend(requests), 0).astype(jnp.bfloat16)
    replies = []
    for i in range(3):
        copy = remote(
            reply, replied.at[i], reply_send.at[i], reply_recv.at[i], inst=inst ^ (i + 1)
        )
        copy.start()
        replies.append(copy)

    second_trip(trip_order[4:])

    attend_slots(groups // 2, groups)

    for copy in replies:
        copy.wait_recv()
    came = [
        matched(
            mask_ref[j],
            [replied[i].astype(jnp.float32)[j * heads : (j + 1) * heads] for i in range(3)],
        )
        for j in range(moves)
    ]
    for h in range(heads):
        cols = slice(h * hd, (h + 1) * hd)
        attended[:rows, cols] = mixed[:, h, :].astype(jnp.bfloat16)
        second = mixed[:, heads + h, :]
        for j in range(moves):
            second = jnp.where(row_ids == slots[j], came[j][h : h + 1], second)
        attended[rows:, cols] = second.astype(jnp.bfloat16)

    tile = 512

    def column_loop(body):
        for c in range(0, width, tile):
            body(slice(c, c + tile))

    def term(i, cols):
        return jnp.dot(attended[...], wo[i, :, cols], preferred_element_type=jnp.float32)

    first_sums = [[None, None], [None, None]]

    def send_first(s, n):
        k = 4 + 2 * s + n
        copy = remote(
            first_send.at[s, n],
            first_recv.at[s, n],
            sum_send.at[k],
            sum_recv.at[k],
            tp=tp ^ (2, 4)[s],
        )
        copy.start()
        first_sums[s][n] = copy

    sibling_sums = {}
    for i in (7, 3, 6, 5, 2, 1, 4, 0):
        k = i // 2
        out_loads[i].wait()
        if i % 2 == 0:
            sibling_sums[k].wait_recv()

        def body(cols):
            chip = term(i, cols)
            if i % 2:
                sib_send[k, :, cols] = chip.astype(jnp.bfloat16)
                return
            chip = chip + sib_recv[k, :, cols].astype(jnp.float32)
            if i == 6:
                first_send[0, 1, :, cols] = chip[:rows].astype(jnp.bfloat16)
                first_send[1, 1, :, cols] = chip[rows:].astype(jnp.bfloat16)
            elif i == 2:
                first_send[0, 0, :, cols] = chip[:rows].astype(jnp.bfloat16)
                own[1, :rows, cols] = chip[rows:]
            elif i == 4:
                own[1, rows:, cols] = chip[:rows]
                first_send[1, 0, :, cols] = chip[rows:].astype(jnp.bfloat16)
            else:
                own[0, :, cols] = chip

        column_loop(body)
        if i % 2:
            copy = remote(
                sib_send.at[k], sib_recv.at[k], sum_send.at[k], sum_recv.at[k], tp=tp ^ 1
            )
            copy.start()
            sibling_sums[k] = copy
        elif i == 6:
            send_first(0, 1)
            send_first(1, 1)
        elif i == 2:
            send_first(0, 0)
        elif i == 4:
            send_first(1, 0)

    second_sums = []
    for s in range(2):
        first_sums[s][1].wait_recv()
        base = own[1, rows:, :] if s == 0 else own[1, :rows, :]
        second_send[s] = (base + first_recv[s, 1].astype(jnp.float32)).astype(jnp.bfloat16)
        copy = remote(
            second_send.at[s],
            second_recv.at[s],
            sum_send.at[8 + s],
            sum_recv.at[8 + s],
            tp=tp ^ (4, 2)[s],
        )
        copy.start()
        second_sums.append(copy)

    for j in range(moves):
        second_moves[j].wait_recv()
        taken = (mask_ref[j] & move_bits[j][1]) != 0
        arrived_ref[j, 0] = jnp.where(taken, last_in[j], mid[j])

    for s in range(2):
        first_sums[s][0].wait_recv()
        second_sums[s].wait_recv()
        part = own[0, s * rows : (s + 1) * rows, :]
        part = part + first_recv[s, 0].astype(jnp.float32)
        out_ref[s] = (part + second_recv[s].astype(jnp.float32)).astype(jnp.bfloat16)

    for copy in (
        along_x
        + along_y
        + across
        + to_sibling
        + list(first_moves.values())
        + list(second_moves.values())
        + asks
        + replies
        + list(sibling_sums.values())
        + first_sums[0]
        + first_sums[1]
        + second_sums
    ):
        copy.wait_send()


def fused(
    x_steps, norm_gain, w_query, w_keyval, w_out, key_cache, lengths, moved_slots, partner_mask
):
    steps, rows, width = x_steps.shape
    moves = moved_slots.shape[1]
    block_len, pair_dim = key_cache.shape[2:]
    hd = pair_dim // 2
    q_width = w_query.shape[1]
    heads = q_width // hd
    both = steps * rows
    bf16, f32 = jnp.bfloat16, jnp.float32
    smem = pl.BlockSpec(memory_space=pltpu.SMEM)
    vmem = pl.BlockSpec(memory_space=pltpu.VMEM)
    anywhere = pl.BlockSpec(memory_space=pl.ANY)
    dma = pltpu.SemaphoreType.DMA
    results = pl.pallas_call(
        fused_kernel,
        out_shape=(
            jax.ShapeDtypeStruct((steps, rows, width), bf16),
            jax.ShapeDtypeStruct((moves,) + key_cache.shape[1:], bf16),
        ),
        in_specs=[smem, smem, smem, vmem, vmem, anywhere, anywhere, anywhere, anywhere],
        out_specs=(vmem, vmem),
        scratch_shapes=[
            pltpu.VMEM((8, width, q_width), bf16),
            pltpu.VMEM((8, width, pair_dim), bf16),
            pltpu.VMEM((8, q_width, width), bf16),
            pltpu.VMEM((rows, block_len, pair_dim), bf16),
            pltpu.VMEM((8, steps, rows, width), bf16),
            pltpu.VMEM((both, q_width + pair_dim), f32),
            pltpu.VMEM((both, 1), f32),
            pltpu.VMEM((rows, hd), jnp.int32),
            pltpu.VMEM((rows, 2 * heads, hd), f32),
            pltpu.VMEM((both, pair_dim), f32),
            pltpu.VMEM((rows, 2 * heads, hd), f32),
            pltpu.VMEM((both, q_width), bf16),
            pltpu.VMEM((moves, block_len, pair_dim), bf16),
            pltpu.VMEM((moves, block_len, pair_dim), bf16),
            pltpu.VMEM((moves, block_len, pair_dim), bf16),
            pltpu.VMEM((moves, block_len, pair_dim), bf16),
            pltpu.VMEM((moves * heads, hd), bf16),
            pltpu.VMEM((moves, pair_dim), f32),
            pltpu.VMEM((3, moves * heads, hd), bf16),
            pltpu.VMEM((3, moves, pair_dim), f32),
            pltpu.VMEM((moves * heads, hd), bf16),
            pltpu.VMEM((3, moves * heads, hd), bf16),
            pltpu.VMEM((4, both, width), bf16),
            pltpu.VMEM((4, both, width), bf16),
            pltpu.VMEM((2, both, width), f32),
            pltpu.VMEM((2, 2, rows, width), bf16),
            pltpu.VMEM((2, 2, rows, width), bf16),
            pltpu.VMEM((2, rows, width), bf16),
            pltpu.VMEM((2, rows, width), bf16),
            dma((28,)),
            dma((10,)),
            dma((10,)),
            dma((2 * moves,)),
            dma((2 * moves,)),
            dma((6,)),
            dma((6,)),
            dma((3,)),
            dma((3,)),
            dma((10,)),
            dma((10,)),
        ],
        compiler_params=pltpu.CompilerParams(
            collective_id=0, has_side_effects=True, vmem_limit_bytes=60 * 2**20
        ),
        cost_estimate=pl.CostEstimate(
            flops=2 * both * w_query.shape[0] * (2 * q_width + pair_dim),
            bytes_accessed=2 * (w_query.size + w_keyval.size + w_out.size + key_cache.size),
            transcendentals=0,
        ),
    )(
        lengths,
        moved_slots,
        partner_mask,
        x_steps,
        norm_gain,
        w_query,
        w_keyval,
        w_out,
        key_cache.reshape(rows, block_len, pair_dim),
    )
    return pl.pallas_call(
        hand_on,
        out_shape=tuple(jax.ShapeDtypeStruct(part.shape, part.dtype) for part in results),
        in_specs=[vmem, vmem],
        out_specs=(vmem, vmem),
    )(*results)


def solution(mesh):
    placed = (
        P(None, "inst", "tp"),
        P(),
        P(None, "tp"),
        P(None, "tp"),
        P("tp", None),
        P("inst", "tp", None, None),
        P(),
        P(),
        P(),
    )
    body = fused if mesh.shape["tp"] == KVH and mesh.shape["inst"] == 4 else shards
    return jax.shard_map(
        body,
        mesh=mesh,
        in_specs=placed,
        out_specs=(P(None, "inst", "tp"), P("inst", "tp", None, None)),
        check_vma=False,
    )
```

```python
from functools import reduce
import math

import jax
import jax.numpy as jnp
from jax import lax
from jax.experimental import pallas as pl
from jax.experimental.pallas import tpu as pltpu
from jax.sharding import PartitionSpec as P

KVH = 8


eps_norm = 1e-05
rope_base = 500000.0
floor_score = -1e30


def from_partner(block, axis, bit):
    count = lax.axis_size(axis)
    route = []
    for low in range(count):
        high = low | 1 << bit
        if high != low and high < count:
            route += [(low, high), (high, low)]
    return lax.ppermute(block, axis, route)


def as_sent(value):

    def short(part):
        return part.astype(jnp.bfloat16) if part.dtype == jnp.float32 else part

    return jax.tree.map(short, value)


def rotary(vectors, positions):
    half_dim = vectors.shape[-1] // 2
    frequency = rope_base ** (-(jnp.arange(half_dim, dtype=jnp.float32) * 2.0) / vectors.shape[-1])
    angles = positions.astype(jnp.float32)[..., None] * frequency
    cosine = jnp.cos(angles)[..., None, :]
    sine_part = jnp.sin(angles)[..., None, :]
    first_half = vectors[..., :half_dim]
    second_half = vectors[..., half_dim:]
    return jnp.concatenate(
        [
            first_half * cosine - second_half * sine_part,
            second_half * cosine + first_half * sine_part,
        ],
        -1,
    )


def block_terms(queries, block, start, length_rows):
    head_dim = queries.shape[-1]
    block_len = block.shape[1]
    scores = jnp.einsum(
        "rhd,rtd->rht", queries, block[..., :head_dim], preferred_element_type=jnp.float32
    ) / math.sqrt(head_dim)
    places = start + jnp.arange(block_len, dtype=jnp.int32)
    visible = (places[None, :] < length_rows[:, None])[:, None, :]
    scores = jnp.where(visible, scores, floor_score)
    block_max = jnp.max(scores, -1)
    weights = jnp.where(visible, jnp.exp(scores - block_max[..., None]), 0.0).astype(jnp.bfloat16)
    block_sum = jnp.sum(weights.astype(jnp.float32), -1)
    block_mix = jnp.einsum(
        "rht,rtd->rhd", weights, block[..., head_dim:], preferred_element_type=jnp.float32
    )
    return (block_max, block_sum, block_mix)


def fresh_terms(queries, fresh_kv):
    head_dim = queries.shape[-1]
    score = jnp.einsum(
        "rhd,rd->rh", queries, fresh_kv[:, :head_dim], preferred_element_type=jnp.float32
    ) / math.sqrt(head_dim)
    block_mix = jnp.broadcast_to(fresh_kv[:, None, head_dim:].astype(jnp.float32), queries.shape)
    return (score, jnp.ones_like(score), block_mix)


def combine(pieces):
    overall_max = reduce(jnp.maximum, [piece[0] for piece in pieces])
    numerator = reduce(
        jnp.add, [jnp.exp(piece[0] - overall_max)[..., None] * piece[2] for piece in pieces]
    )
    denominator = reduce(jnp.add, [jnp.exp(piece[0] - overall_max) * piece[1] for piece in pieces])
    return numerator / denominator[..., None]


def shards(
    x_steps, norm_gain, w_query, w_keyval, w_out, key_cache, lengths, moved_slots, partner_mask
):
    row_count = x_steps.shape[1]
    head_dim = key_cache.shape[-1] // 2
    block_len = key_cache.shape[2]
    group_size = lax.axis_size("tp") // KVH
    group_bits = group_size.bit_length() - 1
    member = lax.axis_index("tp") % group_size
    instance = lax.axis_index("inst")
    own_heads = w_query.shape[1] // head_dim
    own_lengths = lax.dynamic_slice_in_dim(lengths, instance * row_count, row_count)

    def collect(value, swapper):
        stacked = jax.tree.map(lambda leaf: leaf[None], value)
        for bit_index in range(group_bits):
            received = swapper(stacked, bit_index)
            low_side = member >> bit_index & 1 == 0
            stacked = jax.tree.map(
                lambda mine_part, their_part: jnp.where(
                    low_side,
                    jnp.concatenate([mine_part, their_part], 0),
                    jnp.concatenate([their_part, mine_part], 0),
                ),
                stacked,
                received,
            )
        return stacked

    def decode(step_index, positions, cache_rows, length_rows, earlier):
        gathered = lax.all_gather(x_steps[step_index], "tp", axis=1, tiled=True)
        widened = gathered.astype(jnp.float32)
        normed = (
            widened
            * lax.rsqrt(jnp.mean(widened * widened, -1, keepdims=True) + eps_norm)
            * norm_gain
        ).astype(jnp.bfloat16)
        query_raw = jnp.dot(normed, w_query, preferred_element_type=jnp.float32)
        keyval_raw = jnp.dot(normed, w_keyval, preferred_element_type=jnp.float32)
        joined = collect(
            jnp.concatenate([query_raw, keyval_raw], 1),
            lambda value, bit_index: from_partner(value, "tp", bit_index),
        )
        query_width = own_heads * head_dim
        query_all = jnp.moveaxis(joined[:, :, :query_width], 0, 1).reshape(
            row_count, group_size * own_heads, head_dim
        )
        keyval = jnp.moveaxis(joined[:, :, query_width:], 0, 1).reshape(row_count, 2 * head_dim)
        queries = rotary(query_all, positions).astype(jnp.bfloat16)
        partial_value = block_terms(queries, cache_rows[:, 0], member * block_len, length_rows)
        shared = collect(
            partial_value, lambda value, bit_index: from_partner(value, "tp", bit_index)
        )
        own_queries = lax.dynamic_slice_in_dim(queries, member * own_heads, own_heads, 1)
        pieces = [
            tuple(
                (
                    lax.dynamic_slice_in_dim(
                        member_part[block_index], member * own_heads, own_heads, 1
                    )
                    for member_part in shared
                )
            )
            for block_index in range(group_size)
        ]
        fresh_kv = jnp.concatenate(
            [rotary(keyval[:, None, :head_dim], positions)[:, 0], keyval[:, head_dim:]], -1
        ).astype(jnp.bfloat16)
        for fresh_item in earlier + [fresh_kv]:
            pieces.append(fresh_terms(own_queries, fresh_item))
        attended = combine(pieces).reshape(row_count, own_heads * head_dim).astype(jnp.bfloat16)
        head_terms = jnp.dot(attended, w_out, preferred_element_type=jnp.float32)
        return (
            lax.psum_scatter(head_terms, "tp", scatter_dimension=1, tiled=True).astype(
                jnp.bfloat16
            ),
            fresh_kv,
        )

    first_out, first_fresh = decode(0, own_lengths, key_cache, own_lengths, [])
    move_count = moved_slots.shape[1]
    move_ids = jnp.arange(move_count, dtype=jnp.int32)
    partner = jnp.bitwise_xor(instance, partner_mask)
    slots_self = moved_slots[instance]
    slots_partner = moved_slots[partner, move_ids]
    payload = (key_cache[slots_self], first_fresh[slots_self])
    moving = payload
    for bit_index in range(lax.axis_size("inst").bit_length() - 1):
        received = jax.tree.map(
            lambda part, own: part.astype(own.dtype),
            from_partner(as_sent(moving), "inst", bit_index),
            moving,
        )
        use_swap = partner_mask >> bit_index & 1 == 1
        moving = jax.tree.map(
            lambda their_part, mine_part: jnp.where(
                use_swap.reshape((move_count,) + (1,) * (mine_part.ndim - 1)), their_part, mine_part
            ),
            received,
            moving,
        )
    arrived_rows, arrived_fresh = moving
    cache_next = key_cache.at[slots_self].set(arrived_rows)
    fresh_next = first_fresh.at[slots_self].set(arrived_fresh)
    length_next = own_lengths.at[slots_self].set(lengths[partner * row_count + slots_partner])
    second_out, unused = decode(1, length_next + 1, cache_next, length_next, [fresh_next])
    return (jnp.stack([first_out, second_out]), arrived_rows)


def hand_on(out_ref, arrived_ref, out_final, arrived_final):
    out_final[...] = out_ref[...]
    arrived_final[...] = arrived_ref[...]


def fused_kernel(
    len_ref,
    slot_ref,
    mask_ref,
    x_ref,
    gain_ref,
    wq_hbm,
    wkv_hbm,
    wo_hbm,
    cache_hbm,
    out_ref,
    arrived_ref,
    wq,
    wkv,
    wo,
    cache,
    xg,
    acc,
    square,
    place,
    qs,
    fresh,
    mixed,
    attended,
    leave,
    mid_in,
    mid,
    last_in,
    ask_query,
    ask_fresh,
    asked_query,
    asked_fresh,
    reply,
    replied,
    sib_send,
    sib_recv,
    own,
    first_send,
    first_recv,
    second_send,
    second_recv,
    load_sem,
    gather_send,
    gather_recv,
    move_send,
    move_recv,
    ask_send,
    ask_recv,
    reply_send,
    reply_recv,
    sum_send,
    sum_recv,
):
    tp = lax.axis_index("tp")
    inst = lax.axis_index("inst")
    rows = x_ref.shape[1]
    width = x_ref.shape[2]
    moves = slot_ref.shape[1]
    hd = cache.shape[-1] // 2
    heads = qs.shape[1] // 2
    scale = 1.0 / math.sqrt(hd)

    def remote(src, dst, send, recv, **where):
        return pltpu.make_async_remote_copy(
            src_ref=src,
            dst_ref=dst,
            send_sem=send,
            recv_sem=recv,
            device_id=where,
            device_id_type=pl.DeviceIdType.MESH,
        )

    quarter = rows // 4
    cache_loads = [
        pltpu.make_async_copy(
            cache_hbm.at[pl.ds(n * quarter, quarter)],
            cache.at[pl.ds(n * quarter, quarter)],
            load_sem.at[24 + n],
        )
        for n in range(4)
    ]
    for load in cache_loads:
        load.start()
    weight_loads = []
    out_loads = []
    for i in range(8):
        start = pl.multiple_of((tp ^ i) * width, width)
        weight_loads.append(
            (
                pltpu.make_async_copy(wq_hbm.at[pl.ds(start, width), :], wq.at[i], load_sem.at[i]),
                pltpu.make_async_copy(
                    wkv_hbm.at[pl.ds(start, width), :], wkv.at[i], load_sem.at[8 + i]
                ),
            )
        )
        out_loads.append(
            pltpu.make_async_copy(
                wo_hbm.at[:, pl.ds(start, width)], wo.at[i], load_sem.at[16 + i]
            )
        )

    def load_weights(*order):
        for i in order:
            for load in weight_loads[i]:
                load.start()

    load_weights(0)

    barrier = pltpu.get_barrier_semaphore()
    for i in range(1, 8):
        pl.semaphore_signal(
            barrier, inc=1, device_id={"tp": tp ^ i}, device_id_type=pl.DeviceIdType.MESH
        )
    for i in range(1, 4):
        pl.semaphore_signal(
            barrier, inc=1, device_id={"inst": inst ^ i}, device_id_type=pl.DeviceIdType.MESH
        )
    xg[0] = x_ref[...]
    pl.semaphore_wait(barrier, 10)

    def feature_copy(k, src, dst, to, part=None):
        src_ref = xg.at[src] if part is None else xg.at[src, part]
        dst_ref = xg.at[dst] if part is None else xg.at[dst, part]
        return remote(src_ref, dst_ref, gather_send.at[k], gather_recv.at[k], tp=tp ^ to)

    along_x = [feature_copy(0, 0, 2, 2, 0), feature_copy(1, 0, 2, 2, 1)]
    along_y = [feature_copy(2, 0, 4, 4, 1), feature_copy(3, 0, 4, 4, 0)]
    to_sibling = [feature_copy(6, 0, 1, 1)]
    along_x[0].start()
    along_y[0].start()
    along_x[1].start()
    along_y[1].start()
    to_sibling[0].start()

    for load in cache_loads:
        load.wait()
    load_weights(1, 2, 4)
    move_bits = [(1, 2) if j < moves // 2 else (2, 1) for j in range(moves)]
    first_moves = {}
    trip_order = [n + m * (moves // 2) for n in range(moves // 2) for m in range(2)]
    for j in trip_order:
        leave[j] = cache[slot_ref[inst, j]]
        move = remote(
            leave.at[j], mid_in.at[j], move_send.at[j], move_recv.at[j], inst=inst ^ move_bits[j][0]
        )
        move.start()
        first_moves[j] = move

    @pl.loop(0, rows)
    def _(r):
        level = jnp.full((1, 2 * hd), len_ref[inst * rows + r], jnp.int32)
        place[pl.ds(r, 1), :] = level[:, :hd]

    row_ids = lax.broadcasted_iota(jnp.int32, (rows, hd), 0)
    own_place = place[...]
    next_place = own_place
    for j in range(moves):
        partner = inst ^ mask_ref[j]
        length = len_ref[partner * rows + slot_ref[partner, j]]
        next_place = jnp.where(row_ids == slot_ref[inst, j], length, next_place)
    positions = jnp.concatenate([own_place, next_place + 1], 0).astype(jnp.float32)
    lane = lax.broadcasted_iota(jnp.int32, (1, hd), 1)
    pair_id = jnp.where(lane < hd // 2, lane, lane - hd // 2).astype(jnp.float32)
    frequency = jnp.exp(pair_id * (-2.0 * math.log(rope_base) / hd))
    angles = positions * frequency
    cosine = jnp.cos(angles)
    sine = jnp.sin(angles)
    sine = jnp.where(lane < hd // 2, -sine, sine)

    acc[...] = jnp.zeros_like(acc)
    square[...] = jnp.zeros_like(square)
    q_width = wq.shape[2]

    def project(i):
        for load in weight_loads[i]:
            load.wait()
        wide = xg[i].reshape(2 * rows, width).astype(jnp.float32)
        square[...] += jnp.sum(wide * wide, -1, keepdims=True)
        start = pl.multiple_of((tp ^ i) * width, width)
        gain = gain_ref[pl.ds(start, width)]
        scaled = (wide * gain[None, :]).astype(jnp.bfloat16)

        for c in range(0, q_width, 512):
            cols = slice(c, c + 512)
            acc[:, cols] += jnp.dot(scaled, wq[i, :, cols], preferred_element_type=jnp.float32)

        acc[:, q_width:] += jnp.dot(scaled, wkv[i], preferred_element_type=jnp.float32)

    along_x[0].wait_recv()
    along_y[0].wait_recv()
    across = [feature_copy(4, 2, 6, 4, 0), feature_copy(5, 4, 6, 2, 1)]
    across[0].start()
    across[1].start()
    project(0)
    load_weights(3, 5)
    to_sibling[0].wait_recv()
    project(1)
    load_weights(6, 7)
    along_x[1].wait_recv()
    to_sibling.append(feature_copy(7, 2, 3, 1))
    to_sibling[1].start()
    along_y[1].wait_recv()
    to_sibling.append(feature_copy(8, 4, 5, 1))
    to_sibling[2].start()
    project(2)
    project(4)
    for i in (7, 3, 6, 5):
        out_loads[i].start()
    to_sibling[1].wait_recv()
    project(3)
    to_sibling[2].wait_recv()
    project(5)
    for i in (2, 1, 4, 0):
        out_loads[i].start()
    across[0].wait_recv()
    across[1].wait_recv()
    to_sibling.append(feature_copy(9, 6, 7, 1))
    to_sibling[3].start()
    project(6)
    to_sibling[3].wait_recv()
    project(7)

    factor = lax.rsqrt(square[...] * (1.0 / (8 * width)) + eps_norm)

    def turned(part):
        part = part * factor
        return (part * cosine + pltpu.roll(part, hd // 2, 1) * sine).astype(jnp.bfloat16)

    for h in range(heads):
        rotated = turned(acc[:, h * hd : (h + 1) * hd]).astype(jnp.float32)
        qs[:, h, :] = rotated[:rows]
        qs[:, heads + h, :] = rotated[rows:]
    fresh[:, :hd] = turned(acc[:, q_width : q_width + hd]).astype(jnp.float32)
    fresh[:, hd:] = (acc[:, q_width + hd :] * factor).astype(jnp.bfloat16).astype(jnp.float32)

    slots = [slot_ref[inst, j] for j in range(moves)]
    ask_query[...] = jnp.concatenate([qs[slot, heads:, :] for slot in slots], 0).astype(
        jnp.bfloat16
    )
    for j in range(moves):
        ask_fresh[pl.ds(j, 1), :] = fresh[pl.ds(rows + slots[j], 1), :]
    asks = []
    for i in range(3):
        pair = (
            remote(
                ask_query, asked_query.at[i], ask_send.at[i], ask_recv.at[i], inst=inst ^ (i + 1)
            ),
            remote(
                ask_fresh,
                asked_fresh.at[i],
                ask_send.at[3 + i],
                ask_recv.at[3 + i],
                inst=inst ^ (i + 1),
            ),
        )
        for copy in pair:
            copy.start()
            asks.append(copy)

    second_moves = {}

    def second_trip(ids):
        for j in ids:
            first_moves[j].wait_recv()
            taken = (mask_ref[j] & move_bits[j][0]) != 0
            mid[j] = jnp.where(taken, mid_in[j], leave[j])
            move = remote(
                mid.at[j],
                last_in.at[j],
                move_send.at[moves + j],
                move_recv.at[moves + j],
                inst=inst ^ move_bits[j][1],
            )
            move.start()
            second_moves[j] = move

    def matched(mask, parts):
        return jnp.where(mask == 1, parts[0], jnp.where(mask == 2, parts[1], parts[2]))

    def attend(requests):
        scores = [
            scale
            * lax.dot_general(
                queries.astype(jnp.bfloat16),
                keys,
                (((1,), (1,)), ((), ())),
                preferred_element_type=jnp.float32,
            )
            for queries, keys, values, length, news in requests
        ]
        spots = lax.broadcasted_iota(jnp.int32, scores[0].shape, 1)
        scores = [
            jnp.where(spots < request[3], score, floor_score)
            for score, request in zip(scores, requests)
        ]
        tops = [jnp.max(score, -1, keepdims=True) for score in scores]
        marks = []
        for queries, keys, values, length, news in requests:
            row_marks = []
            for row, allowed in news:
                mark = scale * jnp.sum(queries * row[:, :hd], -1, keepdims=True)
                if allowed is not None:
                    mark = jnp.where(allowed, mark, floor_score)
                row_marks.append(mark)
            marks.append(row_marks)
        weights = [
            jnp.where(spots < request[3], jnp.exp(score - top), 0.0).astype(jnp.bfloat16)
            for score, top, request in zip(scores, tops, requests)
        ]
        mixes = [
            jnp.dot(weight, request[2], preferred_element_type=jnp.float32)
            for weight, request in zip(weights, requests)
        ]
        totals = [jnp.sum(weight.astype(jnp.float32), -1, keepdims=True) for weight in weights]
        answers = []
        for request, top, row_marks, mix, total in zip(requests, tops, marks, mixes, totals):
            overall = reduce(jnp.maximum, row_marks, top)
            share = jnp.exp(top - overall)
            numerator = share * mix
            denominator = share * total
            for (row, allowed), mark in zip(request[4], row_marks):
                share = jnp.exp(mark - overall)
                if allowed is not None:
                    share = jnp.where(allowed, share, 0.0)
                numerator = numerator + share * row[:, hd:]
                denominator = denominator + share
            answers.append(numerator / denominator)
        return answers

    later = lax.broadcasted_iota(jnp.int32, (2 * heads, 1), 0) >= heads
    batch = 32

    def attend_slots(first, last):
        @pl.loop(first, last)
        def _(group):
            ids = [group * batch + u for u in range(batch)]
            answers = attend(
                [
                    (
                        qs[r],
                        cache[r, :, :hd],
                        cache[r, :, hd:],
                        len_ref[inst * rows + r],
                        [(fresh[pl.ds(r, 1), :], None), (fresh[pl.ds(rows + r, 1), :], later)],
                    )
                    for r in ids
                ]
            )
            for r, answer in zip(ids, answers):
                mixed[r] = answer

    groups = rows // batch
    attend_slots(0, groups // 4)
    second_trip(trip_order[:2])
    attend_slots(groups // 4, groups // 2)
    second_trip(trip_order[2:4])

    for copy in asks:
        copy.wait_recv()
    requests = []
    for j in range(moves):
        slot = slots[j]
        mask = mask_ref[j]
        part = slice(j * heads, (j + 1) * heads)
        queries = matched(mask, [asked_query[i].astype(jnp.float32)[part] for i in range(3)])
        news = matched(mask, [asked_fresh[i, pl.ds(j, 1), :] for i in range(3)])
        requests.append(
            (
                queries,
                cache[slot, :, :hd],
                cache[slot, :, hd:],
                len_ref[inst * rows + slot],
                [(fresh[pl.ds(slot, 1), :], None), (news, None)],
            )
        )
    reply[...] = jnp.concatenate(attend(requests), 0).astype(jnp.bfloat16)
    replies = []
    for i in range(3):
        copy = remote(
            reply, replied.at[i], reply_send.at[i], reply_recv.at[i], inst=inst ^ (i + 1)
        )
        copy.start()
        replies.append(copy)

    second_trip(trip_order[4:])

    attend_slots(groups // 2, groups)

    for copy in replies:
        copy.wait_recv()
    came = [
        matched(
            mask_ref[j],
            [replied[i].astype(jnp.float32)[j * heads : (j + 1) * heads] for i in range(3)],
        )
        for j in range(moves)
    ]
    for h in range(heads):
        cols = slice(h * hd, (h + 1) * hd)
        attended[:rows, cols] = mixed[:, h, :].astype(jnp.bfloat16)
        second = mixed[:, heads + h, :]
        for j in range(moves):
            second = jnp.where(row_ids == slots[j], came[j][h : h + 1], second)
        attended[rows:, cols] = second.astype(jnp.bfloat16)

    tile = 512

    def column_loop(body):
        for c in range(0, width, tile):
            body(slice(c, c + tile))

    def term(i, cols):
        return jnp.dot(attended[...], wo[i, :, cols], preferred_element_type=jnp.float32)

    first_sums = [[None, None], [None, None]]

    def send_first(s, n):
        k = 4 + 2 * s + n
        copy = remote(
            first_send.at[s, n],
            first_recv.at[s, n],
            sum_send.at[k],
            sum_recv.at[k],
            tp=tp ^ (2, 4)[s],
        )
        copy.start()
        first_sums[s][n] = copy

    sibling_sums = {}
    for i in (7, 3, 6, 5, 2, 1, 4, 0):
        k = i // 2
        out_loads[i].wait()
        if i % 2 == 0:
            sibling_sums[k].wait_recv()

        def body(cols):
            chip = term(i, cols)
            if i % 2:
                sib_send[k, :, cols] = chip.astype(jnp.bfloat16)
                return
            chip = chip + sib_recv[k, :, cols].astype(jnp.float32)
            if i == 6:
                first_send[0, 1, :, cols] = chip[:rows].astype(jnp.bfloat16)
                first_send[1, 1, :, cols] = chip[rows:].astype(jnp.bfloat16)
            elif i == 2:
                first_send[0, 0, :, cols] = chip[:rows].astype(jnp.bfloat16)
                own[1, :rows, cols] = chip[rows:]
            elif i == 4:
                own[1, rows:, cols] = chip[:rows]
                first_send[1, 0, :, cols] = chip[rows:].astype(jnp.bfloat16)
            else:
                own[0, :, cols] = chip

        column_loop(body)
        if i % 2:
            copy = remote(
                sib_send.at[k], sib_recv.at[k], sum_send.at[k], sum_recv.at[k], tp=tp ^ 1
            )
            copy.start()
            sibling_sums[k] = copy
        elif i == 6:
            send_first(0, 1)
            send_first(1, 1)
        elif i == 2:
            send_first(0, 0)
        elif i == 4:
            send_first(1, 0)

    second_sums = []
    for s in range(2):
        first_sums[s][1].wait_recv()
        base = own[1, rows:, :] if s == 0 else own[1, :rows, :]
        second_send[s] = (base + first_recv[s, 1].astype(jnp.float32)).astype(jnp.bfloat16)
        copy = remote(
            second_send.at[s],
            second_recv.at[s],
            sum_send.at[8 + s],
            sum_recv.at[8 + s],
            tp=tp ^ (4, 2)[s],
        )
        copy.start()
        second_sums.append(copy)

    for j in range(moves):
        second_moves[j].wait_recv()
        taken = (mask_ref[j] & move_bits[j][1]) != 0
        arrived_ref[j, 0] = jnp.where(taken, last_in[j], mid[j])

    for s in range(2):
        first_sums[s][0].wait_recv()
        second_sums[s].wait_recv()
        part = own[0, s * rows : (s + 1) * rows, :]
        part = part + first_recv[s, 0].astype(jnp.float32)
        out_ref[s] = (part + second_recv[s].astype(jnp.float32)).astype(jnp.bfloat16)

    for copy in (
        along_x
        + along_y
        + across
        + to_sibling
        + list(first_moves.values())
        + list(second_moves.values())
        + asks
        + replies
        + list(sibling_sums.values())
        + first_sums[0]
        + first_sums[1]
        + second_sums
    ):
        copy.wait_send()


def fused(
    x_steps, norm_gain, w_query, w_keyval, w_out, key_cache, lengths, moved_slots, partner_mask
):
    steps, rows, width = x_steps.shape
    moves = moved_slots.shape[1]
    block_len, pair_dim = key_cache.shape[2:]
    hd = pair_dim // 2
    q_width = w_query.shape[1]
    heads = q_width // hd
    both = steps * rows
    bf16, f32 = jnp.bfloat16, jnp.float32
    smem = pl.BlockSpec(memory_space=pltpu.SMEM)
    vmem = pl.BlockSpec(memory_space=pltpu.VMEM)
    anywhere = pl.BlockSpec(memory_space=pl.ANY)
    dma = pltpu.SemaphoreType.DMA
    results = pl.pallas_call(
        fused_kernel,
        out_shape=(
            jax.ShapeDtypeStruct((steps, rows, width), bf16),
            jax.ShapeDtypeStruct((moves,) + key_cache.shape[1:], bf16),
        ),
        in_specs=[smem, smem, smem, vmem, vmem, anywhere, anywhere, anywhere, anywhere],
        out_specs=(vmem, vmem),
        scratch_shapes=[
            pltpu.VMEM((8, width, q_width), bf16),
            pltpu.VMEM((8, width, pair_dim), bf16),
            pltpu.VMEM((8, q_width, width), bf16),
            pltpu.VMEM((rows, block_len, pair_dim), bf16),
            pltpu.VMEM((8, steps, rows, width), bf16),
            pltpu.VMEM((both, q_width + pair_dim), f32),
            pltpu.VMEM((both, 1), f32),
            pltpu.VMEM((rows, hd), jnp.int32),
            pltpu.VMEM((rows, 2 * heads, hd), f32),
            pltpu.VMEM((both, pair_dim), f32),
            pltpu.VMEM((rows, 2 * heads, hd), f32),
            pltpu.VMEM((both, q_width), bf16),
            pltpu.VMEM((moves, block_len, pair_dim), bf16),
            pltpu.VMEM((moves, block_len, pair_dim), bf16),
            pltpu.VMEM((moves, block_len, pair_dim), bf16),
            pltpu.VMEM((moves, block_len, pair_dim), bf16),
            pltpu.VMEM((moves * heads, hd), bf16),
            pltpu.VMEM((moves, pair_dim), f32),
            pltpu.VMEM((3, moves * heads, hd), bf16),
            pltpu.VMEM((3, moves, pair_dim), f32),
            pltpu.VMEM((moves * heads, hd), bf16),
            pltpu.VMEM((3, moves * heads, hd), bf16),
            pltpu.VMEM((4, both, width), bf16),
            pltpu.VMEM((4, both, width), bf16),
            pltpu.VMEM((2, both, width), f32),
            pltpu.VMEM((2, 2, rows, width), bf16),
            pltpu.VMEM((2, 2, rows, width), bf16),
            pltpu.VMEM((2, rows, width), bf16),
            pltpu.VMEM((2, rows, width), bf16),
            dma((28,)),
            dma((10,)),
            dma((10,)),
            dma((2 * moves,)),
            dma((2 * moves,)),
            dma((6,)),
            dma((6,)),
            dma((3,)),
            dma((3,)),
            dma((10,)),
            dma((10,)),
        ],
        compiler_params=pltpu.CompilerParams(
            collective_id=0, has_side_effects=True, vmem_limit_bytes=60 * 2**20
        ),
        cost_estimate=pl.CostEstimate(
            flops=2 * both * w_query.shape[0] * (2 * q_width + pair_dim),
            bytes_accessed=2 * (w_query.size + w_keyval.size + w_out.size + key_cache.size),
            transcendentals=0,
        ),
    )(
        lengths,
        moved_slots,
        partner_mask,
        x_steps,
        norm_gain,
        w_query,
        w_keyval,
        w_out,
        key_cache.reshape(rows, block_len, pair_dim),
    )
    return pl.pallas_call(
        hand_on,
        out_shape=tuple(jax.ShapeDtypeStruct(part.shape, part.dtype) for part in results),
        in_specs=[vmem, vmem],
        out_specs=(vmem, vmem),
    )(*results)


def solution(mesh):
    placed = (
        P(None, "inst", "tp"),
        P(),
        P(None, "tp"),
        P(None, "tp"),
        P("tp", None),
        P("inst", "tp", None, None),
        P(),
        P(),
        P(),
    )
    body = fused if mesh.shape["tp"] == KVH and mesh.shape["inst"] == 4 else shards
    return jax.shard_map(
        body,
        mesh=mesh,
        in_specs=placed,
        out_specs=(P(None, "inst", "tp"), P("inst", "tp", None, None)),
        check_vma=False,
    )
```
